128 devices in a mesh: gz: 8 (over y, core), xy: 16 (over z, x).
Axes of the slice: x: 4, y: 4, z: 4, core: 2. Of those that a mesh axis runs over, the one named last changes fastest.
Arguments:
- velocity: float32 [128, 512, 1024], P('gz', 'xy'), may hold values from -6 to 6
- yield_stress: float32 [128, 512, 1024], P('gz', 'xy'), may hold values from 0.2 to 2
- stress_step: float32 [128, 512, 1024], P('gz', 'xy'), may hold values from -6 to 6
- block_weights: bfloat16 [8192, 32, 128], P(('gz', 'xy')), may hold values from -0.5 to 0.5
- block_cells: int32 [8192, 128], P(('gz', 'xy')), may hold values from 0 to 524287
- block_plane: int32 [8192], P(('gz', 'xy')), may hold values from 0 to 40
Outputs:
- stress_product: float32 [128, 512, 1024], P('gz', 'xy')
- plane_obs: float32 [40, 32], replicated
The draws below stay inside these ranges and needn't reach their ends.
Inputs may be any that keep to these rules, and one draw needn't show every extreme that they name: `block_plane`: value 40 marks an empty slot. `block_cells`: flat index into the brick of the device that holds the block; cells may repeat.
All inputs are finite; a program needn't handle non-finite values.
Results may differ from the reference program's by a relative error of at most 0.0003.
Values sent between devices are 32-bit elements; how exact they have to be, the bound alone decides.
A program may use at most 192 MiB of HBM per device.

```python
import math
import jax
import jax.numpy as jnp
from jax import lax

CZ = 16
CY = 32
NX = 1024
BLK_DEV = 64
SAMPLES = 32
KCELLS = 128
PLANES = 40
ITERS = 4
NZ = 128
NY = 512
NB = 8192
N_XY = 16


def set_ends(values, key, low, high):
    dims = values.shape
    spot = [jax.random.randint(jax.random.fold_in(key, axis), (), 0, dims[axis]) for axis in range(len(dims))]
    values = values.at[tuple(spot)].set(low)
    longest = dims.index(max(dims))
    spot[longest] = (spot[longest] + 1) % dims[longest]
    return values.at[tuple(spot)].set(high)


def levels(key, shape, pieces, low, high):
    factor_of, own = 1.0, jax.random.fold_in(key, 6)
    for axis_at, blocks in pieces:
        heights = jnp.exp(jax.random.uniform(jax.random.fold_in(own, axis_at), (blocks,), jnp.float32, low / len(pieces), high / len(pieces)))
        factor_of = factor_of * jnp.repeat(heights, shape[axis_at] // blocks).reshape([-1 if axis == axis_at else 1 for axis in range(len(shape))])
    return factor_of


def noise(stream_key, extent, deviation, reach, pieces=(), held_as=jnp.bfloat16):
    result = deviation * jax.random.normal(stream_key, extent, jnp.float32)
    if pieces:
        result = result * levels(stream_key, extent, pieces, -0.22, 0.18)
    return jnp.clip(result, -reach, reach).astype(held_as)


def setup_inputs(seed: int = 0) -> dict:
    key_of = jax.random.split(jax.random.key(seed), 7)
    return {
        "velocity": noise(key_of[0], (NZ, NY, NX), 1.0, 6.0, ((0, 8), (1, 16)), jnp.float32),
        "yield_stress": jnp.clip(jnp.exp(math.log(2.0) - 2.3025851 * jax.random.uniform(key_of[1], (NZ, NY, NX), jnp.float32) ** levels(key_of[1], (NZ, NY, NX), ((0, 8), (1, 16)), -0.2, 0.2)), 0.2, 2.0),
        "stress_step": noise(key_of[2], (NZ, NY, NX), 1.0, 6.0, ((0, 8), (1, 16)), jnp.float32),
        "block_weights": noise(key_of[3], (NB, SAMPLES, KCELLS), KCELLS ** -0.5, 0.5, ((0, 128),)),
        "block_cells": set_ends(jax.random.randint(key_of[4], (NB, KCELLS), 0, CZ * CY * NX), jax.random.fold_in(key_of[4], 1), 0, (CZ * CY * NX) - 1).astype(jnp.int32),
        "block_plane": set_ends(jax.random.randint(key_of[5], (NB,), 0, PLANES + 1), jax.random.fold_in(key_of[5], 1), 0, PLANES).astype(jnp.int32),
    }


mass_matrix_term = 1.0
viscosity_base = 1.0
damping_factor = 0.8
regular_sq = 0.01

def padded_field(field):
    return jnp.pad(field, ((1, 1), (1, 1), (0, 0)))

def neighbours(arr):
    centre = arr[1:-1, 1:-1]
    zero = jnp.zeros_like(centre[:, :, :1])
    return (centre, [arr[2:, 1:-1], arr[:-2, 1:-1], arr[1:-1, 2:], arr[1:-1, :-2], jnp.concatenate([centre[:, :, 1:], zero], axis=2), jnp.concatenate([zero, centre[:, :, :-1]], axis=2)])

def face_flux_sum(coef, field):
    cm, nms = neighbours(coef)
    cv, nvs = neighbours(field)
    total = jnp.zeros_like(cv)
    for nm, nv in zip(nms, nvs):
        total = total + (cm + nm) * 0.5 * (cv - nv)
    return total

def neighbour_weight_sum(coef):
    cm, nms = neighbours(coef)
    total = jnp.full(cm.shape, mass_matrix_term, jnp.float32)
    for nm in nms:
        total = total + (cm + nm) * 0.5
    return total

def cross_sum(first, second):
    cu, nus = neighbours(first)
    cl, nls = neighbours(second)
    total = jnp.zeros_like(cu)
    for nu, nl in zip(nus, nls):
        total = total + (cu - nu) * (cl - nl) * 0.5
    return total

def shear_rate(upad):
    centre = upad[1:-1, 1:-1]
    zero = jnp.zeros_like(centre[:, :, :1])
    dz = upad[2:, 1:-1] - centre
    dy = upad[1:-1, 2:] - centre
    dx = jnp.concatenate([centre[:, :, 1:], zero], axis=2) - centre
    return dz * dz + dy * dy + dx * dx

def reference(velocity, yield_stress, stress_step, block_weights, block_cells, block_plane):
    upad = padded_field(velocity)
    regul = 1.0 / jnp.sqrt(shear_rate(upad) + regular_sq)
    effective_viscosity = viscosity_base + yield_stress * regul
    dvisc = stress_step * regul
    padded_velocity = padded_field(effective_viscosity)
    source = -face_flux_sum(padded_field(dvisc), upad)
    diagonal_entries = neighbour_weight_sum(padded_velocity)

    def solve(right_hand_side):
        forward_state = jnp.zeros_like(right_hand_side)
        for sweep in range(ITERS):
            forward_state = forward_state + damping_factor * (right_hand_side - (mass_matrix_term * forward_state + face_flux_sum(padded_velocity, padded_field(forward_state)))) / diagonal_entries
        return forward_state
    tangent = solve(source)
    owner = (jnp.arange(NB, dtype=jnp.int32) // BLK_DEV).astype(jnp.int32)
    slab = owner // N_XY
    tile = owner % N_XY
    lz = block_cells // (CY * NX)
    ly = block_cells // NX % CY
    lx = block_cells % NX
    gidx = ((slab[:, None] * CZ + lz) * NY + tile[:, None] * CY + ly) * NX + lx
    gidx = gidx.astype(jnp.int32)
    cells = tangent.reshape(-1)[gidx]
    wts = block_weights.astype(jnp.float32)
    part = jnp.einsum('bsk,bk->bs', wts, cells, precision=lax.Precision.HIGHEST)
    onehot = (block_plane[:, None] == jnp.arange(PLANES, dtype=jnp.int32)[None, :]).astype(jnp.float32)
    plane_obs = jnp.dot(onehot.T, part, precision=lax.Precision.HIGHEST)
    per_block = jnp.dot(onehot, plane_obs, precision=lax.Precision.HIGHEST)
    back = jnp.einsum('bsk,bs->bk', wts, per_block, precision=lax.Precision.HIGHEST)
    adj_src = jnp.zeros((NZ * NY * NX,), jnp.float32).at[gidx.reshape(-1)].add(back.reshape(-1))
    adjoint = solve(adj_src.reshape(NZ, NY, NX))
    product = -regul * cross_sum(upad, padded_field(adjoint))
    return (product, plane_obs)
```

```python
import functools
import jax
import jax.numpy as jnp
from jax import lax
from jax.experimental import pallas as pl
from jax.experimental.pallas import tpu as pltpu
from jax.sharding import PartitionSpec as P

PLANES = 40
KEEP = 0.2
DAMP = 0.8
MESH = pl.DeviceIdType.MESH
F32 = jnp.float32
BF16 = jnp.bfloat16
VMEM = pl.BlockSpec(memory_space=pltpu.VMEM)
SMEM = pl.BlockSpec(memory_space=pltpu.SMEM)
ANY = pl.BlockSpec(memory_space=pl.ANY)
LIMIT = 56 * 1024 * 1024


def ids(shape):
    rank = len(shape)
    return (
        lax.broadcasted_iota(jnp.int32, shape, rank - 2),
        lax.broadcasted_iota(jnp.int32, shape, rank - 1),
    )


def x_next(a, wrap=True):
    sub, lane = ids(a.shape)
    r = pltpu.roll(a, 127, a.ndim - 1)
    r = jnp.where(lane == 127, pltpu.roll(r, 7, a.ndim - 2), r)
    return r if wrap else jnp.where((lane == 127) & (sub == 7), 0.0, r)


def x_prev(a, wrap=True):
    sub, lane = ids(a.shape)
    r = pltpu.roll(a, 1, a.ndim - 1)
    r = jnp.where(lane == 0, pltpu.roll(r, 1, a.ndim - 2), r)
    return r if wrap else jnp.where((lane == 0) & (sub == 0), 0.0, r)


def divisor(n, most):
    return max(d for d in range(1, most + 1) if n % d == 0)


class Faces:
    def __init__(self, CZ, CY, send, recv):
        self.CZ, self.CY, self.send, self.recv = CZ, CY, send, recv
        G, X = lax.axis_size("gz"), lax.axis_size("xy")
        g, x = lax.axis_index("gz"), lax.axis_index("xy")
        self.has = (g > 0, g < G - 1, x > 0, x < X - 1)
        lower, upper = jnp.maximum(g - 1, 0), jnp.minimum(g + 1, G - 1)
        left, right = jnp.maximum(x - 1, 0), jnp.minimum(x + 1, X - 1)
        self.to = ((lower, x), (upper, x), (g, left), (g, right))

    def barrier(self):
        sem = pltpu.get_barrier_semaphore()
        count = jnp.int32(0)
        for has, to in zip(self.has, self.to):
            count = count + has.astype(jnp.int32)

            @pl.when(has)
            def _():
                pl.semaphore_signal(sem, inc=1, device_id=to, device_id_type=MESH)

        pl.semaphore_wait(sem, count)

    def copy(self, buf, e, d):
        CZ, CY = self.CZ, self.CY
        zs, ys = pl.ds(1, CZ), pl.ds(1, CY)
        src = (buf.at[1, ys], buf.at[CZ, ys], buf.at[zs, 1], buf.at[zs, CY])[d]
        dst = (buf.at[CZ + 1, ys], buf.at[0, ys], buf.at[zs, CY + 1], buf.at[zs, 0])[d]
        return pltpu.make_async_remote_copy(
            src_ref=src,
            dst_ref=dst,
            send_sem=self.send.at[e, d],
            recv_sem=self.recv.at[e, d],
            device_id=self.to[d],
            device_id_type=MESH,
        )

    def start(self, buf, e):
        for d in range(4):

            @pl.when(self.has[d])
            def _():
                self.copy(buf, e, d).start()

    def arrive(self, buf, e):
        for d in range(4):

            @pl.when(self.has[d ^ 1])
            def _():
                self.copy(buf, e, d).wait_recv()

    def finish(self, buf, e):
        for d in range(4):

            @pl.when(self.has[d])
            def _():
                self.copy(buf, e, d).wait_send()


def clear_faces(bufs, CZ, CY):
    plane = jnp.zeros((CY + 2, 8, 128), F32)
    row = jnp.zeros((CZ, 8, 128), F32)
    for buf in bufs:
        buf[0] = plane
        buf[CZ + 1] = plane
        buf[pl.ds(1, CZ), 0] = row
        buf[pl.ds(1, CZ), CY + 1] = row


def interior(CZ, CY, f):
    yn = divisor(CY - 2, 10)
    per = (CY - 2) // yn

    @pl.loop(0, (CZ - 2) * per)
    def _(i):
        f(1 + i // per, 1 + (i % per) * yn, 1, yn)


def boundary(CZ, CY, f):
    yn = divisor(CY, 8)
    per = CY // yn
    zn = divisor(CZ - 2, 8)
    parts = (CZ - 2) // zn

    @pl.loop(0, 2 * per)
    def _(i):
        f((i // per) * (CZ - 1), (i % per) * yn, 1, yn)

    @pl.loop(0, 2 * parts)
    def _(i):
        f(1 + (i % parts) * zn, (i // parts) * (CY - 1), zn, 1)


def around(ref, z, y, zn, yn):
    zs, ys = pl.ds(z + 1, zn), pl.ds(y + 1, yn)
    if zn == 1:
        wide = ref[zs, pl.ds(y, yn + 2)]
        return (
            wide[:, 1 : yn + 1],
            wide[:, :yn],
            wide[:, 2:],
            ref[pl.ds(z, 1), ys],
            ref[pl.ds(z + 2, 1), ys],
        )
    wide = ref[pl.ds(z, zn + 2), ys]
    return (
        wide[1 : zn + 1],
        ref[zs, pl.ds(y, yn)],
        ref[zs, pl.ds(y + 2, yn)],
        wide[:zn],
        wide[2:],
    )


def coefficients(MU, z, y, zn, yn):
    m, ym, yp, zm, zp = around(MU, z, y, zn, yn)
    xm, xp = x_prev(m, False), x_next(m, False)
    total = ((xm + xp) + (ym + yp)) + (zm + zp)
    dinv = DAMP / (1.0 + (3.0 * m + 0.5 * total))
    half = 0.5 * dinv
    sub, lane = ids(m.shape)
    first, last = (sub == 0) & (lane == 0), (sub == 7) & (lane == 127)
    faces = (
        jnp.where(first, 0.0, half * (m + xm)),
        jnp.where(last, 0.0, half * (m + xp)),
        half * (m + ym),
        half * (m + yp),
        half * (m + zm),
        half * (m + zp),
    )
    return faces, dinv


def sweep(A, R, src, dst, pad, z, y, zn, yn):
    w, ym, yp, zm, zp = around(src, z, y, zn, yn)
    zs, ys = pl.ds(z, zn), pl.ds(y, yn)
    total = KEEP * w + R[zs, ys]
    for at, value in enumerate((x_prev(w), x_next(w), ym, yp, zm, zp)):
        total = total + A[at, zs, ys] * value
    dst[pl.ds(z + pad, zn), pl.ds(y + pad, yn)] = total


def tangent_kernel(
    CZ, CY, v_in, y_in, s_in, tan_out, mu_out, v_out, reg_out,
    vin, yin, sin, V, MU, DMU, REG, A, R, W1, W2, W3, T, load, store, send, recv,
):
    tiles = CY // 8
    loads = [
        pltpu.make_async_copy(src, dst, load.at[i])
        for i, (src, dst) in enumerate(((v_in, vin), (y_in, yin), (s_in, sin)))
    ]
    for c in loads:
        c.start()
    faces = Faces(CZ, CY, send, recv)
    clear_faces((V, MU, DMU, W1, W2, W3), CZ, CY)
    faces.barrier()
    loads[0].wait()

    @pl.loop(0, CZ * tiles)
    def _(i):
        z, y = i // tiles, (i % tiles) * 8
        for s in range(8):
            V[z + 1, y + 1 + s] = vin[i, pl.ds(s, 8, stride=8), :]

    faces.start(V, 0)
    loads[1].wait()
    loads[2].wait()

    def viscosity(z, t):
        i, y = z * tiles + t, t * 8
        here = pl.ds(y + 1, 8)
        c = V[z + 1, here]
        dz = V[z + 2, here] - c
        dy = V[z + 1, pl.ds(y + 2, 8)] - c
        dx = x_next(c, False) - c
        reg = lax.rsqrt((dz * dz + dy * dy + dx * dx) + 0.01)
        REG[z, pl.ds(y, 8)] = reg
        for s in range(8):
            MU[z + 1, y + 1 + s] = 1.0 + yin[i, pl.ds(s, 8, stride=8), :] * reg[s]
            DMU[z + 1, y + 1 + s] = sin[i, pl.ds(s, 8, stride=8), :] * reg[s]

    @pl.loop(0, (CZ - 1) * (tiles - 1))
    def _(i):
        viscosity(i // (tiles - 1), i % (tiles - 1))

    faces.arrive(V, 0)

    @pl.loop(0, CZ)
    def _(i):
        viscosity(i, tiles - 1)

    @pl.loop(0, tiles - 1)
    def _(i):
        viscosity(CZ - 1, i)

    faces.start(MU, 1)
    faces.start(DMU, 2)

    def source(z, y, zn, yn):
        zs, ys = pl.ds(z, zn), pl.ds(y, yn)
        face, dinv = coefficients(MU, z, y, zn, yn)
        for at in range(6):
            A[at, zs, ys] = face[at]
        d, *ds = around(DMU, z, y, zn, yn)
        v, *vs = around(V, z, y, zn, yn)
        ds += [x_prev(d, False), x_next(d, False)]
        vs += [x_prev(v, False), x_next(v, False)]
        total = (d + ds[0]) * (vs[0] - v)
        for dn, vn in zip(ds[1:], vs[1:]):
            total = total + (d + dn) * (vn - v)
        first = (0.5 * dinv) * total
        R[zs, ys] = first
        W1[pl.ds(z + 1, zn), pl.ds(y + 1, yn)] = first

    interior(CZ, CY, source)
    faces.arrive(MU, 1)
    faces.arrive(DMU, 2)
    stores = [
        pltpu.make_async_copy(src, dst, store.at[i])
        for i, (src, dst) in enumerate(((MU, mu_out), (V, v_out), (REG, reg_out)))
    ]
    for c in stores:
        c.start()
    boundary(CZ, CY, source)
    for step, (src, dst, pad) in enumerate(((W1, W2, 1), (W2, W3, 1), (W3, T, 0))):
        faces.start(src, 3 + step)
        go = functools.partial(sweep, A, R, src, dst, pad)
        interior(CZ, CY, go)
        faces.arrive(src, 3 + step)
        boundary(CZ, CY, go)
    last = pltpu.make_async_copy(T, tan_out, store.at[3])
    last.start()
    for e, buf in enumerate((V, MU, DMU, W1, W2, W3)):
        faces.finish(buf, e)
    for c in stores + [last]:
        c.wait()


def adjoint_kernel(
    CZ, CY, q_in, mu_in, v_in, reg_in, out,
    Q, MU, V, REG, A, R, W1, W2, W3, W4, T, load, store, send, recv,
):
    loads = [
        pltpu.make_async_copy(src, dst, load.at[i])
        for i, (src, dst) in enumerate(((mu_in, MU), (q_in, Q), (v_in, V), (reg_in, REG)))
    ]
    for c in loads:
        c.start()
    faces = Faces(CZ, CY, send, recv)
    clear_faces((W1, W2, W3, W4), CZ, CY)
    faces.barrier()
    loads[0].wait()
    loads[1].wait()

    def begin(z, y, zn, yn):
        zs, ys = pl.ds(z, zn), pl.ds(y, yn)
        face, dinv = coefficients(MU, z, y, zn, yn)
        for at in range(6):
            A[at, zs, ys] = face[at]
        first = dinv * Q[zs, ys]
        R[zs, ys] = first
        W1[pl.ds(z + 1, zn), pl.ds(y + 1, yn)] = first

    def product(z, y, zn, yn):
        zs, ys = pl.ds(z, zn), pl.ds(y, yn)
        v, *vs = around(V, z, y, zn, yn)
        a, *many = around(W4, z, y, zn, yn)
        vs += [x_prev(v, False), x_next(v, False)]
        many += [x_prev(a, False), x_next(a, False)]
        total = (v - vs[0]) * (a - many[0])
        for vn, an in zip(vs[1:], many[1:]):
            total = total + (v - vn) * (a - an)
        T[zs, ys] = (-0.5 * REG[zs, ys]) * total

    boundary(CZ, CY, begin)
    faces.start(W1, 0)
    interior(CZ, CY, begin)
    for step, (src, dst) in enumerate(((W1, W2), (W2, W3), (W3, W4))):
        if step:
            faces.start(src, step)
        go = functools.partial(sweep, A, R, src, dst, 1)
        interior(CZ, CY, go)
        faces.arrive(src, step)
        boundary(CZ, CY, go)
    faces.start(W4, 3)
    loads[2].wait()
    loads[3].wait()
    interior(CZ, CY, product)
    faces.arrive(W4, 3)
    boundary(CZ, CY, product)
    last = pltpu.make_async_copy(T, out, store)
    last.start()
    for e, buf in enumerate((W1, W2, W3, W4)):
        faces.finish(buf, e)
    last.wait()


def gather_kernel(B, K, cells_s, plane_s, cells_v, weights, field, out, rows):
    @pl.loop(0, B)
    def _(b):
        for k in range(K):
            r = cells_s[b, k] >> 7
            rows[b, pl.ds(k, 1), :] = field[pl.ds(r, 1), :]

    step = divisor(B, 8)
    sub, _ = ids((128, K))
    _, lane = ids((8, 128))

    def group(g, acc):
        low, high = acc
        inner = cells_v[g] & 127
        for j in range(step):
            b = g * step + j
            hot = jnp.where(sub == inner[j : j + 1, :], 1.0, 0.0).T
            picked = rows[b] * hot
            main = picked.astype(BF16)
            rest = (picked - main.astype(F32)).astype(BF16)
            w = weights[b]
            part = jnp.dot(w, main, preferred_element_type=F32) + jnp.dot(
                w, rest, preferred_element_type=F32
            )
            total = jnp.sum(part, axis=1, keepdims=True)
            p = plane_s[b]
            p = jnp.where(p < PLANES, p, -1000)
            for n in range(3):
                low = low + jnp.where(lane == p + PLANES * n, total[8 * n : 8 * n + 8], 0.0)
            high = high + jnp.where(lane == p, total[24:32], 0.0)
        return low, high

    zero = jnp.zeros((8, 128), F32)
    low, high = lax.fori_loop(0, B // step, group, (zero, zero))
    out[0:8, :] = low
    out[8:16, :] = high


def sum_kernel(G, X, part, out, one, two, mid, s1, r1, s2, r2):
    g, x = lax.axis_index("gz"), lax.axis_index("xy")
    sem = pltpu.get_barrier_semaphore()
    for d in range(1, G):
        pl.semaphore_signal(sem, inc=1, device_id=(lax.rem(g + d, G), x), device_id_type=MESH)
    for d in range(1, X):
        pl.semaphore_signal(sem, inc=1, device_id=(g, lax.rem(x + d, X)), device_id_type=MESH)
    pl.semaphore_wait(sem, G + X - 2)

    def stage(src, buf, me, n, target, send, recv):
        copies = []
        for d in range(1, n):
            c = pltpu.make_async_remote_copy(
                src_ref=src,
                dst_ref=buf.at[me],
                send_sem=send.at[d],
                recv_sem=recv.at[d],
                device_id=target(lax.rem(me + d, n)),
                device_id_type=MESH,
            )
            c.start()
            copies.append(c)
        buf[me] = src[...]
        for c in copies:
            c.wait_recv()
        total = buf[0]
        for i in range(1, n):
            total = total + buf[i]
        return total, copies

    total, first = stage(part, one, g, G, lambda t: (t, x), s1, r1)
    mid[...] = total
    total, second = stage(mid, two, x, X, lambda t: (g, t), s2, r2)
    out[...] = total
    for c in first + second:
        c.wait_send()


def scatter_kernel(B, K, copies, cells_s, plane_s, cells_v, weights, table, out, obs, values, *accs):
    rows = out.shape[0]

    @pl.loop(0, rows // 64)
    def _(i):
        for acc in accs:
            acc[pl.ds(i * 64, 64), :] = jnp.zeros((64, 128), F32)

    step = divisor(B, 8)
    sub, _ = ids((128, K))
    _, lane = ids((32, 128))
    packed = table[...]
    low = packed[0:8]
    po = jnp.concatenate(
        [low, pltpu.roll(low, 128 - PLANES, 1), pltpu.roll(low, 128 - 2 * PLANES, 1), packed[8:16]],
        axis=0,
    )
    po = jnp.where(lane < PLANES, po, 0.0)
    obs[...] = po[:, :PLANES]

    @pl.loop(0, B // step)
    def _(g):
        inner = cells_v[g] & 127
        for j in range(step):
            b = g * step + j
            mine = jnp.sum(jnp.where(lane == plane_s[b], po, 0.0), axis=1, keepdims=True)
            back = jnp.sum(weights[b].astype(F32) * mine, axis=0, keepdims=True)
            values[b] = jnp.where(sub == inner[j : j + 1, :], back, 0.0).T

    @pl.loop(0, B)
    def _(b):
        for k in range(0, K, copies):
            at = [pl.ds(cells_s[b, k + j] >> 7, 1) for j in range(copies)]
            new = [accs[j][at[j], :] + values[b, pl.ds(k + j, 1), :] for j in range(copies)]
            for j in range(copies):
                accs[j][at[j], :] = new[j]

    @pl.loop(0, rows // 64)
    def _(i):
        here = pl.ds(i * 64, 64)
        total = accs[0][here, :]
        for acc in accs[1:]:
            total = total + acc[here, :]
        out[here, :] = total


def shards(velocity, yield_stress, stress_step, block_weights, block_cells, block_plane):
    CZ, CY, NX = velocity.shape
    B, S, K = block_weights.shape
    G, X = lax.axis_size("gz"), lax.axis_size("xy")
    core, padded = (CZ, CY, 8, 128), (CZ + 2, CY + 2, 8, 128)
    tiles = (CZ * CY // 8, 64, 128)

    def tiled(field):
        return field.reshape(CZ, CY // 8, 8, 8, 128).transpose(0, 1, 3, 2, 4).reshape(tiles)

    def sds(shape):
        return jax.ShapeDtypeStruct(shape, F32)

    def vm(shape):
        return pltpu.VMEM(shape, F32)

    def params(n=None):
        if n is None:
            return pltpu.CompilerParams(vmem_limit_bytes=LIMIT)
        return pltpu.CompilerParams(vmem_limit_bytes=LIMIT, collective_id=n, has_side_effects=True)

    DMA = pltpu.SemaphoreType.DMA
    tangent, mu, vel, reg = pl.pallas_call(
        functools.partial(tangent_kernel, CZ, CY),
        out_shape=(sds(core), sds(padded), sds(padded), sds(core)),
        in_specs=[ANY] * 3,
        out_specs=(ANY,) * 4,
        scratch_shapes=[vm(tiles)] * 3 + [vm(padded)] * 3 + [vm(core), vm((6,) + core), vm(core)]
        + [vm(padded)] * 3 + [vm(core), DMA((3,)), DMA((4,)), DMA((6, 4)), DMA((6, 4))],
        compiler_params=params(0),
        name="tangent",
    )(tiled(velocity), tiled(yield_stress), tiled(stress_step))

    groups = divisor(B, 8)
    cells_v = block_cells.reshape(B // groups, groups, K)
    part = pl.pallas_call(
        functools.partial(gather_kernel, B, K),
        out_shape=sds((16, 128)),
        in_specs=[SMEM, SMEM, VMEM, VMEM, VMEM],
        out_specs=VMEM,
        scratch_shapes=[vm((B, K, 128))],
        compiler_params=params(),
        name="gather",
    )(block_cells, block_plane, cells_v, block_weights, tangent.reshape(CZ * CY * 8, 128))

    table = pl.pallas_call(
        functools.partial(sum_kernel, G, X),
        out_shape=sds((16, 128)),
        in_specs=[VMEM],
        out_specs=VMEM,
        scratch_shapes=[vm((G, 16, 128)), vm((X, 16, 128)), vm((16, 128)), DMA((G,)), DMA((G,)), DMA((X,)), DMA((X,))],
        compiler_params=params(1),
        name="sum",
    )(part)

    copies = 8
    adj, obs = pl.pallas_call(
        functools.partial(scatter_kernel, B, K, copies),
        out_shape=(sds((CZ * CY * 8, 128)), sds((S, PLANES))),
        in_specs=[SMEM, SMEM, VMEM, VMEM, VMEM],
        out_specs=(VMEM, VMEM),
        scratch_shapes=[vm((B, K, 128))] + [vm((CZ * CY * 8, 128))] * copies,
        compiler_params=params(),
        name="scatter",
    )(block_cells, block_plane, cells_v, block_weights, table)

    product = pl.pallas_call(
        functools.partial(adjoint_kernel, CZ, CY),
        out_shape=sds(core),
        in_specs=[ANY] * 4,
        out_specs=ANY,
        scratch_shapes=[vm(core), vm(padded), vm(padded), vm(core), vm((6,) + core), vm(core)]
        + [vm(padded)] * 4 + [vm(core), DMA((4,)), DMA, DMA((4, 4)), DMA((4, 4))],
        compiler_params=params(2),
        name="adjoint",
    )(adj.reshape(core), mu, vel, reg)
    return product.reshape(CZ, CY, NX), obs.T


def solution(mesh):
    placed = (
        P("gz", "xy", None),
        P("gz", "xy", None),
        P("gz", "xy", None),
        P(("gz", "xy"), None, None),
        P(("gz", "xy"), None),
        P(("gz", "xy")),
    )
    return jax.shard_map(
        shards, mesh=mesh, in_specs=placed, out_specs=(P("gz", "xy", None), P()), check_vma=False
    )
```

```python
import functools
import jax
import jax.numpy as jnp
from jax import lax
from jax.experimental import pallas as pl
from jax.experimental.pallas import tpu as pltpu
from jax.sharding import PartitionSpec as P

PLANES = 40
KEEP = 0.2
DAMP = 0.8
MESH = pl.DeviceIdType.MESH
F32 = jnp.float32
BF16 = jnp.bfloat16
VMEM = pl.BlockSpec(memory_space=pltpu.VMEM)
SMEM = pl.BlockSpec(memory_space=pltpu.SMEM)
ANY = pl.BlockSpec(memory_space=pl.ANY)
LIMIT = 56 * 1024 * 1024


def ids(shape):
    rank = len(shape)
    return (
        lax.broadcasted_iota(jnp.int32, shape, rank - 2),
        lax.broadcasted_iota(jnp.int32, shape, rank - 1),
    )


def x_next(a, wrap=True):
    sub, lane = ids(a.shape)
    r = pltpu.roll(a, 127, a.ndim - 1)
    r = jnp.where(lane == 127, pltpu.roll(r, 7, a.ndim - 2), r)
    return r if wrap else jnp.where((lane == 127) & (sub == 7), 0.0, r)


def x_prev(a, wrap=True):
    sub, lane = ids(a.shape)
    r = pltpu.roll(a, 1, a.ndim - 1)
    r = jnp.where(lane == 0, pltpu.roll(r, 1, a.ndim - 2), r)
    return r if wrap else jnp.where((lane == 0) & (sub == 0), 0.0, r)


def divisor(n, most):
    return max(d for d in range(1, most + 1) if n % d == 0)


class Faces:
    def __init__(self, CZ, CY, send, recv):
        self.CZ, self.CY, self.send, self.recv = CZ, CY, send, recv
        G, X = lax.axis_size("gz"), lax.axis_size("xy")
        g, x = lax.axis_index("gz"), lax.axis_index("xy")
        self.has = (g > 0, g < G - 1, x > 0, x < X - 1)
        lower, upper = jnp.maximum(g - 1, 0), jnp.minimum(g + 1, G - 1)
        left, right = jnp.maximum(x - 1, 0), jnp.minimum(x + 1, X - 1)
        self.to = ((lower, x), (upper, x), (g, left), (g, right))

    def copy(self, buf, e, d):
        CZ, CY = self.CZ, self.CY
        zs, ys = pl.ds(1, CZ), pl.ds(1, CY)
        src = (buf.at[1, ys], buf.at[CZ, ys], buf.at[zs, 1], buf.at[zs, CY])[d]
        dst = (buf.at[CZ + 1, ys], buf.at[0, ys], buf.at[zs, CY + 1], buf.at[zs, 0])[d]
        return pltpu.make_async_remote_copy(
            src_ref=src,
            dst_ref=dst,
            send_sem=self.send.at[e, d],
            recv_sem=self.recv.at[e, d],
            device_id=self.to[d],
            device_id_type=MESH,
        )

    def start(self, buf, e, which=(0, 1, 2, 3)):
        for d in which:

            @pl.when(self.has[d])
            def _():
                self.copy(buf, e, d).start()

    def arrive(self, buf, e):
        for d in range(4):

            @pl.when(self.has[d ^ 1])
            def _():
                self.copy(buf, e, d).wait_recv()

    def finish(self, buf, e):
        for d in range(4):

            @pl.when(self.has[d])
            def _():
                self.copy(buf, e, d).wait_send()


def greet(all_lines):
    G, X = lax.axis_size("gz"), lax.axis_size("xy")
    g, x = lax.axis_index("gz"), lax.axis_index("xy")
    sem = pltpu.get_barrier_semaphore()
    if all_lines:
        for d in range(1, G):
            pl.semaphore_signal(sem, inc=1, device_id=(lax.rem(g + d, G), x), device_id_type=MESH)
        for d in range(1, X):
            pl.semaphore_signal(sem, inc=1, device_id=(g, lax.rem(x + d, X)), device_id_type=MESH)
        pl.semaphore_wait(sem, G + X - 2)
        return
    count = jnp.int32(0)
    for has, to in (
        (g > 0, (jnp.maximum(g - 1, 0), x)),
        (g < G - 1, (jnp.minimum(g + 1, G - 1), x)),
        (x > 0, (g, jnp.maximum(x - 1, 0))),
        (x < X - 1, (g, jnp.minimum(x + 1, X - 1))),
    ):
        count = count + has.astype(jnp.int32)

        @pl.when(has)
        def _():
            pl.semaphore_signal(sem, inc=1, device_id=to, device_id_type=MESH)

    pl.semaphore_wait(sem, count)


def clear_faces(bufs, CZ, CY):
    plane = jnp.zeros((CY + 2, 8, 128), F32)
    row = jnp.zeros((CZ, 8, 128), F32)
    for buf in bufs:
        buf[0] = plane
        buf[CZ + 1] = plane
        buf[pl.ds(1, CZ), 0] = row
        buf[pl.ds(1, CZ), CY + 1] = row


def interior(CZ, CY, f, planes):
    yn = divisor(CY - 2, 6)
    planes = divisor(CZ - 2, planes)

    @pl.loop(0, (CZ - 2) // planes)
    def _(i):
        for p in range(planes):
            for y in range(1, CY - 1, yn):
                f(1 + i * planes + p, y, 1, yn)


def boundary_z(CZ, CY, f):
    yn = divisor(CY, 8)

    @pl.loop(0, 2)
    def _(i):
        for y in range(0, CY, yn):
            f(i * (CZ - 1), y, 1, yn)


def boundary_y(CZ, CY, f):
    zn = divisor(CZ - 2, 8)

    @pl.loop(0, 2)
    def _(i):
        for z in range(1, CZ - 1, zn):
            f(z, i * (CY - 1), zn, 1)


def around(ref, z, y, zn, yn):
    zs, ys = pl.ds(z + 1, zn), pl.ds(y + 1, yn)
    if zn == 1:
        wide = ref[zs, pl.ds(y, yn + 2)]
        return (
            wide[:, 1 : yn + 1],
            wide[:, :yn],
            wide[:, 2:],
            ref[pl.ds(z, 1), ys],
            ref[pl.ds(z + 2, 1), ys],
        )
    wide = ref[pl.ds(z, zn + 2), ys]
    return (
        wide[1 : zn + 1],
        ref[zs, pl.ds(y, yn)],
        ref[zs, pl.ds(y + 2, yn)],
        wide[:zn],
        wide[2:],
    )


def coefficients(MU, z, y, zn, yn):
    m, ym, yp, zm, zp = around(MU, z, y, zn, yn)
    xm, xp = x_prev(m, False), x_next(m, False)
    total = ((xm + xp) + (ym + yp)) + (zm + zp)
    dinv = DAMP / (1.0 + (3.0 * m + 0.5 * total))
    half = 0.5 * dinv
    sub, lane = ids(m.shape)
    first, last = (sub == 0) & (lane == 0), (sub == 7) & (lane == 127)
    faces = (
        jnp.where(first, 0.0, half * (m + xm)),
        jnp.where(last, 0.0, half * (m + xp)),
        half * (m + ym),
        half * (m + yp),
        half * (m + zm),
        half * (m + zp),
    )
    return faces, dinv


def sweep(A, R, src, put, z, y, zn, yn):
    w, ym, yp, zm, zp = around(src, z, y, zn, yn)
    zs, ys = pl.ds(z, zn), pl.ds(y, yn)
    total = KEEP * w + R[zs, ys]
    for at, value in enumerate((x_prev(w), x_next(w), ym, yp, zm, zp)):
        total = total + A[at, zs, ys] * value
    put(total, z, y, zn, yn)


def put_padded(dst):
    def put(value, z, y, zn, yn):
        dst[pl.ds(z + 1, zn), pl.ds(y + 1, yn)] = value

    return put


def put_rows(dst, CY):
    def put(value, z, y, zn, yn):
        for i in range(zn):
            at = pl.multiple_of(((z + i) * CY + y) * 8, 8)
            dst[pl.ds(at, 8 * yn), :] = value[i].reshape(8 * yn, 128)

    return put


def tangent_kernel(
    CZ, CY, cells_s, plane_s, cells_v, v_in, y_in, s_in, w_in, mu_out, v_out, reg_out, table,
    vin, yin, sin, weights, V, MU, DMU, REG, A, R, W1, W2, W3, T, rows0, rows1, one, two, part,
    load, store, send, recv, s1, r1, s2, r2,
):
    tiles = CY // 8
    loads = [
        pltpu.make_async_copy(src, dst, load.at[i])
        for i, (src, dst) in enumerate(
            ((v_in, vin), (y_in, yin), (s_in, sin), (w_in, weights))
        )
    ]
    for c in loads:
        c.start()
    faces = Faces(CZ, CY, send, recv)
    clear_faces((V, MU, DMU, W1, W2, W3), CZ, CY)
    greet(True)
    loads[0].wait()

    @pl.loop(0, CZ * tiles // 2)
    def _(j):
        for i in (2 * j, 2 * j + 1):
            z, y = i // tiles, (i % tiles) * 8
            for s in range(8):
                V[z + 1, y + 1 + s] = vin[i, pl.ds(s, 8, stride=8), :]

    faces.start(V, 0)
    loads[1].wait()
    loads[2].wait()

    def viscosity(z, t):
        i, y = z * tiles + t, t * 8
        here = pl.ds(y + 1, 8)
        c = V[z + 1, here]
        dz = V[z + 2, here] - c
        dy = V[z + 1, pl.ds(y + 2, 8)] - c
        dx = x_next(c, False) - c
        reg = lax.rsqrt((dz * dz + dy * dy + dx * dx) + 0.01)
        REG[z, pl.ds(y, 8)] = reg
        for s in range(8):
            MU[z + 1, y + 1 + s] = 1.0 + yin[i, pl.ds(s, 8, stride=8), :] * reg[s]
            DMU[z + 1, y + 1 + s] = sin[i, pl.ds(s, 8, stride=8), :] * reg[s]

    @pl.loop(0, CZ - 1)
    def _(z):
        for t in range(tiles - 1):
            viscosity(z, t)

    faces.arrive(V, 0)
    for t in range(tiles):
        viscosity(CZ - 1, t)

    pair = divisor(CZ - 1, 3)

    @pl.loop(0, (CZ - 1) // pair)
    def _(i):
        for j in range(pair):
            viscosity(i * pair + j, tiles - 1)

    faces.start(MU, 1)
    faces.start(DMU, 2)

    def source(z, y, zn, yn):
        zs, ys = pl.ds(z, zn), pl.ds(y, yn)
        face, dinv = coefficients(MU, z, y, zn, yn)
        for at in range(6):
            A[at, zs, ys] = face[at]
        d, *ds = around(DMU, z, y, zn, yn)
        v, *vs = around(V, z, y, zn, yn)
        ds += [x_prev(d, False), x_next(d, False)]
        vs += [x_prev(v, False), x_next(v, False)]
        total = (d + ds[0]) * (vs[0] - v)
        for dn, vn in zip(ds[1:], vs[1:]):
            total = total + (d + dn) * (vn - v)
        first = (0.5 * dinv) * total
        R[zs, ys] = first
        W1[pl.ds(z + 1, zn), pl.ds(y + 1, yn)] = first

    interior(CZ, CY, source, 1)
    faces.arrive(MU, 1)
    faces.arrive(DMU, 2)
    stores = [
        pltpu.make_async_copy(src, dst, store.at[i])
        for i, (src, dst) in enumerate(((MU, mu_out), (V, v_out), (REG, reg_out)))
    ]
    for c in stores:
        c.start()
    boundary_z(CZ, CY, source)
    faces.start(W1, 3, (0, 1))
    boundary_y(CZ, CY, source)
    faces.start(W1, 3, (2, 3))
    for step, (src, dst) in enumerate(((W1, W2), (W2, W3), (W3, None))):
        put = put_rows(T, CY) if dst is None else put_padded(dst)
        go = functools.partial(sweep, A, R, src, put)
        interior(CZ, CY, go, 2)
        faces.arrive(src, 3 + step)
        boundary_z(CZ, CY, go)
        if dst is not None:
            faces.start(dst, 4 + step, (0, 1))
        boundary_y(CZ, CY, go)
        if dst is not None:
            faces.start(dst, 4 + step, (2, 3))

    loads[3].wait()
    observe(cells_s, plane_s, cells_v, weights, T, part, rows0, rows1)
    sum_all(part, table, one, two, s1, r1, s2, r2)
    for e, buf in enumerate((V, MU, DMU, W1, W2, W3)):
        faces.finish(buf, e)
    for c in stores:
        c.wait()


def adjoint_kernel(
    CZ, CY, q_in, mu_in, v_in, reg_in, out,
    Q, MU, V, REG, A, R, W1, W2, W3, W4, T, load, store, send, recv,
):
    loads = [
        pltpu.make_async_copy(src, dst, load.at[i])
        for i, (src, dst) in enumerate(((mu_in, MU), (q_in, Q), (v_in, V), (reg_in, REG)))
    ]
    for c in loads:
        c.start()
    faces = Faces(CZ, CY, send, recv)
    clear_faces((W1, W2, W3, W4), CZ, CY)
    greet(False)
    loads[0].wait()
    loads[1].wait()

    def begin(z, y, zn, yn):
        zs, ys = pl.ds(z, zn), pl.ds(y, yn)
        face, dinv = coefficients(MU, z, y, zn, yn)
        for at in range(6):
            A[at, zs, ys] = face[at]
        first = dinv * Q[zs, ys]
        R[zs, ys] = first
        W1[pl.ds(z + 1, zn), pl.ds(y + 1, yn)] = first

    def product(z, y, zn, yn):
        zs, ys = pl.ds(z, zn), pl.ds(y, yn)
        v, *vs = around(V, z, y, zn, yn)
        a, *many = around(W4, z, y, zn, yn)
        vs += [x_prev(v, False), x_next(v, False)]
        many += [x_prev(a, False), x_next(a, False)]
        total = (v - vs[0]) * (a - many[0])
        for vn, an in zip(vs[1:], many[1:]):
            total = total + (v - vn) * (a - an)
        T[zs, ys] = (-0.5 * REG[zs, ys]) * total

    boundary_z(CZ, CY, begin)
    faces.start(W1, 0, (0, 1))
    boundary_y(CZ, CY, begin)
    faces.start(W1, 0, (2, 3))
    interior(CZ, CY, begin, 1)
    for step, (src, dst) in enumerate(((W1, W2), (W2, W3), (W3, W4))):
        go = functools.partial(sweep, A, R, src, put_padded(dst))
        interior(CZ, CY, go, 2)
        faces.arrive(src, step)
        boundary_z(CZ, CY, go)
        faces.start(dst, step + 1, (0, 1))
        boundary_y(CZ, CY, go)
        faces.start(dst, step + 1, (2, 3))
    loads[2].wait()
    loads[3].wait()
    interior(CZ, CY, product, 1)
    faces.arrive(W4, 3)
    boundary_z(CZ, CY, product)
    boundary_y(CZ, CY, product)
    last = pltpu.make_async_copy(T, out, store)
    last.start()
    for e, buf in enumerate((W1, W2, W3, W4)):
        faces.finish(buf, e)
    last.wait()


def observe(cells_s, plane_s, cells_v, weights, field, part, rows0, rows1):
    B, K = cells_s.shape
    step = cells_v.shape[1]
    sub, _ = ids((128, K))
    _, lane = ids((8, 128))

    def fetch(b, rows):
        for k in range(K):
            r = cells_s[b, k] >> 7
            rows[pl.ds(k, 1), :] = field[pl.ds(r, 1), :]

    fetch(0, rows0)

    def group(g, acc):
        low, high = acc
        inner = cells_v[g] & 127
        for j in range(step):
            b = g * step + j
            rows, later = (rows0, rows1) if j % 2 == 0 else (rows1, rows0)
            fetch(jnp.minimum(b + 1, B - 1), later)
            hot = jnp.where(sub == inner[j : j + 1, :], 1.0, 0.0).T
            picked = rows[...] * hot
            main = picked.astype(BF16)
            rest = (picked - main.astype(F32)).astype(BF16)
            w = weights[b]
            both = jnp.dot(w, main, preferred_element_type=F32) + jnp.dot(
                w, rest, preferred_element_type=F32
            )
            total = jnp.sum(both, axis=1, keepdims=True)
            p = plane_s[b]
            p = jnp.where(p < PLANES, p, -1000)
            for n in range(3):
                low = low + jnp.where(lane == p + PLANES * n, total[8 * n : 8 * n + 8], 0.0)
            high = high + jnp.where(lane == p, total[24:32], 0.0)
        return low, high

    zero = jnp.zeros((8, 128), F32)
    low, high = lax.fori_loop(0, B // step, group, (zero, zero))
    part[0:8, :] = low
    part[8:16, :] = high


def sum_all(part, out, one, two, s1, r1, s2, r2):
    G, X = lax.axis_size("gz"), lax.axis_size("xy")
    g, x = lax.axis_index("gz"), lax.axis_index("xy")

    def stage(src, buf, me, n, target, send, recv):
        copies = []
        for d in range(1, n):
            c = pltpu.make_async_remote_copy(
                src_ref=src,
                dst_ref=buf.at[me],
                send_sem=send.at[d],
                recv_sem=recv.at[d],
                device_id=target(lax.rem(me + d, n)),
                device_id_type=MESH,
            )
            c.start()
            copies.append(c)
        buf[me] = src[...]
        for c in copies:
            c.wait_recv()
        total = buf[0]
        for i in range(1, n):
            total = total + buf[i]
        for c in copies:
            c.wait_send()
        return total

    total = stage(part, one, g, G, lambda t: (t, x), s1, r1)
    part[...] = total
    out[...] = stage(part, two, x, X, lambda t: (g, t), s2, r2)


def scatter_kernel(B, K, copies, cells_s, plane_s, cells_v, weights, table, out, obs, values0, values1, *accs):
    rows = out.shape[0]

    @pl.loop(0, rows // 64)
    def _(i):
        for acc in accs:
            acc[pl.ds(i * 64, 64), :] = jnp.zeros((64, 128), F32)

    step = divisor(B, 8)
    sub, _ = ids((128, K))
    _, lane = ids((32, 128))
    packed = table[...]
    low = packed[0:8]
    po = jnp.concatenate(
        [low, pltpu.roll(low, 128 - PLANES, 1), pltpu.roll(low, 128 - 2 * PLANES, 1), packed[8:16]],
        axis=0,
    )
    po = jnp.where(lane < PLANES, po, 0.0)
    obs[...] = po[:, :PLANES]

    def spread(b, values):
        inner = cells_v[b // step] & 127
        row = jnp.zeros((1, K), jnp.int32)
        for j in range(step):
            row = jnp.where(b % step == j, inner[j : j + 1, :], row)
        mine = jnp.sum(jnp.where(lane == plane_s[b], po, 0.0), axis=1, keepdims=True)
        back = jnp.sum(weights[b].astype(F32) * mine, axis=0, keepdims=True)
        values[...] = jnp.where(sub == row, back, 0.0).T

    def add(b, values):
        for k in range(0, K, copies):
            at = [pl.ds(cells_s[b, k + j] >> 7, 1) for j in range(copies)]
            new = [accs[j][at[j], :] + values[pl.ds(k + j, 1), :] for j in range(copies)]
            for j in range(copies):
                accs[j][at[j], :] = new[j]

    spread(0, values0)

    @pl.loop(0, B // 2)
    def _(i):
        spread(2 * i + 1, values1)
        add(2 * i, values0)
        spread(jnp.minimum(2 * i + 2, B - 1), values0)
        add(2 * i + 1, values1)

    @pl.loop(0, rows // 64)
    def _(i):
        here = pl.ds(i * 64, 64)
        total = accs[0][here, :]
        for acc in accs[1:]:
            total = total + acc[here, :]
        out[here, :] = total


def shards(velocity, yield_stress, stress_step, block_weights, block_cells, block_plane):
    CZ, CY, NX = velocity.shape
    B, S, K = block_weights.shape
    G, X = lax.axis_size("gz"), lax.axis_size("xy")
    core, padded = (CZ, CY, 8, 128), (CZ + 2, CY + 2, 8, 128)
    tiles = (CZ * CY // 8, 64, 128)

    def tiled(field):
        return field.reshape(CZ, CY // 8, 8, 8, 128).transpose(0, 1, 3, 2, 4).reshape(tiles)

    def sds(shape):
        return jax.ShapeDtypeStruct(shape, F32)

    def vm(shape):
        return pltpu.VMEM(shape, F32)

    def params(n=None):
        if n is None:
            return pltpu.CompilerParams(vmem_limit_bytes=LIMIT)
        return pltpu.CompilerParams(vmem_limit_bytes=LIMIT, collective_id=n, has_side_effects=True)

    DMA = pltpu.SemaphoreType.DMA
    groups = divisor(B, 8)
    cells_v = block_cells.reshape(B // groups, groups, K)
    mu, vel, reg, table = pl.pallas_call(
        functools.partial(tangent_kernel, CZ, CY),
        out_shape=(sds(padded), sds(padded), sds(core), sds((16, 128))),
        in_specs=[SMEM, SMEM, VMEM] + [ANY] * 4,
        out_specs=(ANY, ANY, ANY, VMEM),
        scratch_shapes=[vm(tiles)] * 3 + [pltpu.VMEM((B, S, K), BF16)]
        + [vm(padded)] * 3 + [vm(core), vm((6,) + core), vm(core)] + [vm(padded)] * 3
        + [vm((CZ * CY * 8, 128)), vm((K, 128)), vm((K, 128))]
        + [vm((G, 16, 128)), vm((X, 16, 128)), vm((16, 128))]
        + [DMA((4,)), DMA((3,)), DMA((6, 4)), DMA((6, 4)), DMA((G,)), DMA((G,)), DMA((X,)), DMA((X,))],
        compiler_params=params(0),
        name="tangent",
    )(
        block_cells, block_plane, cells_v,
        tiled(velocity), tiled(yield_stress), tiled(stress_step), block_weights,
    )

    copies = 8
    adj, obs = pl.pallas_call(
        functools.partial(scatter_kernel, B, K, copies),
        out_shape=(sds((CZ * CY * 8, 128)), sds((S, PLANES))),
        in_specs=[SMEM, SMEM, VMEM, VMEM, VMEM],
        out_specs=(VMEM, VMEM),
        scratch_shapes=[vm((K, 128))] * 2 + [vm((CZ * CY * 8, 128))] * copies,
        compiler_params=params(),
        name="scatter",
    )(block_cells, block_plane, cells_v, block_weights, table)

    product = pl.pallas_call(
        functools.partial(adjoint_kernel, CZ, CY),
        out_shape=sds(core),
        in_specs=[ANY] * 4,
        out_specs=ANY,
        scratch_shapes=[vm(core), vm(padded), vm(padded), vm(core), vm((6,) + core), vm(core)]
        + [vm(padded)] * 4 + [vm(core), DMA((4,)), DMA, DMA((4, 4)), DMA((4, 4))],
        compiler_params=params(1),
        name="adjoint",
    )(adj.reshape(core), mu, vel, reg)
    return product.reshape(CZ, CY, NX), obs.T


def solution(mesh):
    placed = (
        P("gz", "xy", None),
        P("gz", "xy", None),
        P("gz", "xy", None),
        P(("gz", "xy"), None, None),
        P(("gz", "xy"), None),
        P(("gz", "xy")),
    )
    return jax.shard_map(
        shards, mesh=mesh, in_specs=placed, out_specs=(P("gz", "xy", None), P()), check_vma=False
    )
```

```python
import functools
import jax
import jax.numpy as jnp
from jax import lax
from jax.experimental import pallas as pl
from jax.experimental.pallas import tpu as pltpu
from jax.sharding import PartitionSpec as P

PLANES = 40
KEEP = 0.2
DAMP = 0.8
MESH = pl.DeviceIdType.MESH
F32 = jnp.float32
BF16 = jnp.bfloat16
VMEM = pl.BlockSpec(memory_space=pltpu.VMEM)
SMEM = pl.BlockSpec(memory_space=pltpu.SMEM)
ANY = pl.BlockSpec(memory_space=pl.ANY)
LIMIT = 56 * 1024 * 1024


def ids(shape):
    rank = len(shape)
    return (
        lax.broadcasted_iota(jnp.int32, shape, rank - 2),
        lax.broadcasted_iota(jnp.int32, shape, rank - 1),
    )


def x_next(a, wrap=True):
    sub, lane = ids(a.shape)
    r = pltpu.roll(a, 127, a.ndim - 1)
    r = jnp.where(lane == 127, pltpu.roll(r, 7, a.ndim - 2), r)
    return r if wrap else jnp.where((lane == 127) & (sub == 7), 0.0, r)


def x_prev(a, wrap=True):
    sub, lane = ids(a.shape)
    r = pltpu.roll(a, 1, a.ndim - 1)
    r = jnp.where(lane == 0, pltpu.roll(r, 1, a.ndim - 2), r)
    return r if wrap else jnp.where((lane == 0) & (sub == 0), 0.0, r)


def divisor(n, most):
    return max(d for d in range(1, most + 1) if n % d == 0)


class Faces:
    def __init__(self, CZ, CY, send, recv):
        self.CZ, self.CY, self.send, self.recv = CZ, CY, send, recv
        G, X = lax.axis_size("gz"), lax.axis_size("xy")
        g, x = lax.axis_index("gz"), lax.axis_index("xy")
        self.has = (g > 0, g < G - 1, x > 0, x < X - 1)
        lower, upper = jnp.maximum(g - 1, 0), jnp.minimum(g + 1, G - 1)
        left, right = jnp.maximum(x - 1, 0), jnp.minimum(x + 1, X - 1)
        self.to = ((lower, x), (upper, x), (g, left), (g, right))

    def copy(self, buf, e, d):
        CZ, CY = self.CZ, self.CY
        zs, ys = pl.ds(1, CZ), pl.ds(1, CY)
        src = (buf.at[1, ys], buf.at[CZ, ys], buf.at[zs, 1], buf.at[zs, CY])[d]
        dst = (buf.at[CZ + 1, ys], buf.at[0, ys], buf.at[zs, CY + 1], buf.at[zs, 0])[d]
        return pltpu.make_async_remote_copy(
            src_ref=src,
            dst_ref=dst,
            send_sem=self.send.at[e, d],
            recv_sem=self.recv.at[e, d],
            device_id=self.to[d],
            device_id_type=MESH,
        )

    def start(self, buf, e, which=(0, 1, 2, 3)):
        for d in which:

            @pl.when(self.has[d])
            def _():
                self.copy(buf, e, d).start()

    def arrive(self, buf, e):
        for d in range(4):

            @pl.when(self.has[d ^ 1])
            def _():
                self.copy(buf, e, d).wait_recv()

    def finish(self, buf, e):
        for d in range(4):

            @pl.when(self.has[d])
            def _():
                self.copy(buf, e, d).wait_send()


def lines():
    G, X = lax.axis_size("gz"), lax.axis_size("xy")
    g, x = lax.axis_index("gz"), lax.axis_index("xy")
    across = min(X, 4)
    return (
        (2, g % 2, lambda t: ((g // 2) * 2 + t, x)),
        (G // 2, g // 2, lambda t: (t * 2 + g % 2, x)),
        (across, x % across, lambda t: (g, (x // across) * across + t)),
        (X // across, x // across, lambda t: (g, t * across + x % across)),
    )


def greet(all_lines):
    G, X = lax.axis_size("gz"), lax.axis_size("xy")
    g, x = lax.axis_index("gz"), lax.axis_index("xy")
    sem = pltpu.get_barrier_semaphore()
    count = jnp.int32(0)
    for has, to in (
        (g > 0, (jnp.maximum(g - 1, 0), x)),
        (g < G - 1, (jnp.minimum(g + 1, G - 1), x)),
        (x > 0, (g, jnp.maximum(x - 1, 0))),
        (x < X - 1, (g, jnp.minimum(x + 1, X - 1))),
    ):
        count = count + has.astype(jnp.int32)

        @pl.when(has)
        def _():
            pl.semaphore_signal(sem, inc=1, device_id=to, device_id_type=MESH)

    if all_lines:
        for n, me, target in lines():
            for d in range(1, n):
                to = target(lax.rem(me + d, n))
                pl.semaphore_signal(sem, inc=1, device_id=to, device_id_type=MESH)
            count = count + (n - 1)
    pl.semaphore_wait(sem, count)


def clear_faces(bufs, CZ, CY):
    plane = jnp.zeros((CY + 2, 8, 128), F32)
    row = jnp.zeros((CZ, 8, 128), F32)
    for buf in bufs:
        buf[0] = plane
        buf[CZ + 1] = plane
        buf[pl.ds(1, CZ), 0] = row
        buf[pl.ds(1, CZ), CY + 1] = row


def interior(CZ, CY, f, planes):
    yn = divisor(CY - 2, 6)
    planes = divisor(CZ - 2, planes)

    @pl.loop(0, (CZ - 2) // planes)
    def _(i):
        for p in range(planes):
            for y in range(1, CY - 1, yn):
                f(1 + i * planes + p, y, 1, yn)


def boundary_z(CZ, CY, f):
    yn = divisor(CY, 8)

    @pl.loop(0, 2)
    def _(i):
        for y in range(0, CY, yn):
            f(i * (CZ - 1), y, 1, yn)


def boundary_y(CZ, CY, f):
    zn = divisor(CZ - 2, 8)

    @pl.loop(0, 2)
    def _(i):
        for z in range(1, CZ - 1, zn):
            f(z, i * (CY - 1), zn, 1)


def around(ref, z, y, zn, yn):
    zs, ys = pl.ds(z + 1, zn), pl.ds(y + 1, yn)
    if zn == 1:
        wide = ref[zs, pl.ds(y, yn + 2)]
        return (
            wide[:, 1 : yn + 1],
            wide[:, :yn],
            wide[:, 2:],
            ref[pl.ds(z, 1), ys],
            ref[pl.ds(z + 2, 1), ys],
        )
    wide = ref[pl.ds(z, zn + 2), ys]
    return (
        wide[1 : zn + 1],
        ref[zs, pl.ds(y, yn)],
        ref[zs, pl.ds(y + 2, yn)],
        wide[:zn],
        wide[2:],
    )


def coefficients(MU, z, y, zn, yn):
    m, ym, yp, zm, zp = around(MU, z, y, zn, yn)
    xm, xp = x_prev(m, False), x_next(m, False)
    total = ((xm + xp) + (ym + yp)) + (zm + zp)
    dinv = DAMP / (1.0 + (3.0 * m + 0.5 * total))
    half = 0.5 * dinv
    sub, lane = ids(m.shape)
    first, last = (sub == 0) & (lane == 0), (sub == 7) & (lane == 127)
    faces = (
        jnp.where(first, 0.0, half * (m + xm)),
        jnp.where(last, 0.0, half * (m + xp)),
        half * (m + ym),
        half * (m + yp),
        half * (m + zm),
        half * (m + zp),
    )
    return faces, dinv


def sweep(A, R, src, put, z, y, zn, yn):
    w, ym, yp, zm, zp = around(src, z, y, zn, yn)
    zs, ys = pl.ds(z, zn), pl.ds(y, yn)
    total = KEEP * w + R[zs, ys]
    for at, value in enumerate((x_prev(w), x_next(w), ym, yp, zm, zp)):
        total = total + A[at, zs, ys] * value
    put(total, z, y, zn, yn)


def put_padded(dst):
    def put(value, z, y, zn, yn):
        dst[pl.ds(z + 1, zn), pl.ds(y + 1, yn)] = value

    return put


def put_rows(dst, CY):
    def put(value, z, y, zn, yn):
        for i in range(zn):
            at = pl.multiple_of(((z + i) * CY + y) * 1024, 1024)
            dst[:, pl.ds(at, 1024 * yn)] = value[i].reshape(1, 1024 * yn)

    return put


def row_of(cell):
    return pl.ds((cell >> 7) * 128, 128)


def tangent_kernel(
    CZ, CY, cells_s, plane_s, cells_v, v_in, y_in, s_in, w_in, mu_out, v_out, reg_out, table,
    vin, yin, sin, weights, V, MU, DMU, REG, A, R, W1, W2, W3, T, rows0, rows1, held, parts,
    load, store, send, recv, sum_send, sum_recv,
):
    tiles = CY // 8
    loads = [
        pltpu.make_async_copy(src, dst, load.at[i])
        for i, (src, dst) in enumerate(
            ((v_in, vin), (y_in, yin), (s_in, sin), (w_in, weights))
        )
    ]
    for c in loads:
        c.start()
    faces = Faces(CZ, CY, send, recv)
    clear_faces((V, MU, DMU, W1, W2, W3), CZ, CY)
    greet(True)
    loads[0].wait()

    @pl.loop(0, CZ * tiles // 2)
    def _(j):
        for i in (2 * j, 2 * j + 1):
            z, y = i // tiles, (i % tiles) * 8
            for s in range(8):
                V[z + 1, y + 1 + s] = vin[i, pl.ds(s, 8, stride=8), :]

    faces.start(V, 0)
    loads[1].wait()
    loads[2].wait()

    def viscosity(z, t):
        i, y = z * tiles + t, t * 8
        here = pl.ds(y + 1, 8)
        c = V[z + 1, here]
        dz = V[z + 2, here] - c
        dy = V[z + 1, pl.ds(y + 2, 8)] - c
        dx = x_next(c, False) - c
        reg = lax.rsqrt((dz * dz + dy * dy + dx * dx) + 0.01)
        REG[z, pl.ds(y, 8)] = reg
        for s in range(8):
            MU[z + 1, y + 1 + s] = 1.0 + yin[i, pl.ds(s, 8, stride=8), :] * reg[s]
            DMU[z + 1, y + 1 + s] = sin[i, pl.ds(s, 8, stride=8), :] * reg[s]

    @pl.loop(0, CZ - 1)
    def _(z):
        for t in range(tiles - 1):
            viscosity(z, t)

    faces.arrive(V, 0)
    for t in range(tiles):
        viscosity(CZ - 1, t)

    pair = divisor(CZ - 1, 3)

    @pl.loop(0, (CZ - 1) // pair)
    def _(i):
        for j in range(pair):
            viscosity(i * pair + j, tiles - 1)

    faces.start(MU, 1)
    faces.start(DMU, 2)

    def source(z, y, zn, yn):
        zs, ys = pl.ds(z, zn), pl.ds(y, yn)
        face, dinv = coefficients(MU, z, y, zn, yn)
        for at in range(6):
            A[at, zs, ys] = face[at]
        d, *ds = around(DMU, z, y, zn, yn)
        v, *vs = around(V, z, y, zn, yn)
        ds += [x_prev(d, False), x_next(d, False)]
        vs += [x_prev(v, False), x_next(v, False)]
        total = (d + ds[0]) * (vs[0] - v)
        for dn, vn in zip(ds[1:], vs[1:]):
            total = total + (d + dn) * (vn - v)
        first = (0.5 * dinv) * total
        R[zs, ys] = first
        W1[pl.ds(z + 1, zn), pl.ds(y + 1, yn)] = first

    interior(CZ, CY, source, 1)
    faces.arrive(MU, 1)
    faces.arrive(DMU, 2)
    stores = [
        pltpu.make_async_copy(src, dst, store.at[i])
        for i, (src, dst) in enumerate(((MU, mu_out), (V, v_out), (REG, reg_out)))
    ]
    for c in stores:
        c.start()
    boundary_z(CZ, CY, source)
    faces.start(W1, 3, (0, 1))
    boundary_y(CZ, CY, source)
    faces.start(W1, 3, (2, 3))
    for step, (src, dst) in enumerate(((W1, W2), (W2, W3), (W3, None))):
        put = put_rows(T, CY) if dst is None else put_padded(dst)
        go = functools.partial(sweep, A, R, src, put)
        interior(CZ, CY, go, 2)
        faces.arrive(src, 3 + step)
        boundary_z(CZ, CY, go)
        if dst is not None:
            faces.start(dst, 4 + step, (0, 1))
        boundary_y(CZ, CY, go)
        if dst is not None:
            faces.start(dst, 4 + step, (2, 3))

    loads[3].wait()
    observe(cells_s, plane_s, cells_v, weights, T, parts, rows0, rows1)
    sum_all(parts, table, held, sum_send, sum_recv)
    for e, buf in enumerate((V, MU, DMU, W1, W2, W3)):
        faces.finish(buf, e)
    for c in stores:
        c.wait()


def adjoint_kernel(
    CZ, CY, q_in, mu_in, v_in, reg_in, out,
    Q, MU, V, REG, A, R, W1, W2, W3, W4, T, load, store, send, recv,
):
    loads = [
        pltpu.make_async_copy(src, dst, load.at[i])
        for i, (src, dst) in enumerate(((mu_in, MU), (q_in, Q), (v_in, V), (reg_in, REG)))
    ]
    for c in loads:
        c.start()
    faces = Faces(CZ, CY, send, recv)
    clear_faces((W1, W2, W3, W4), CZ, CY)
    greet(False)
    loads[0].wait()
    loads[1].wait()

    def begin(z, y, zn, yn):
        zs, ys = pl.ds(z, zn), pl.ds(y, yn)
        face, dinv = coefficients(MU, z, y, zn, yn)
        for at in range(6):
            A[at, zs, ys] = face[at]
        first = dinv * Q[zs, ys]
        R[zs, ys] = first
        W1[pl.ds(z + 1, zn), pl.ds(y + 1, yn)] = first

    def product(z, y, zn, yn):
        zs, ys = pl.ds(z, zn), pl.ds(y, yn)
        v, *vs = around(V, z, y, zn, yn)
        a, *many = around(W4, z, y, zn, yn)
        vs += [x_prev(v, False), x_next(v, False)]
        many += [x_prev(a, False), x_next(a, False)]
        total = (v - vs[0]) * (a - many[0])
        for vn, an in zip(vs[1:], many[1:]):
            total = total + (v - vn) * (a - an)
        T[zs, ys] = (-0.5 * REG[zs, ys]) * total

    boundary_z(CZ, CY, begin)
    faces.start(W1, 0, (0, 1))
    boundary_y(CZ, CY, begin)
    faces.start(W1, 0, (2, 3))
    interior(CZ, CY, begin, 1)
    for step, (src, dst) in enumerate(((W1, W2), (W2, W3), (W3, W4))):
        go = functools.partial(sweep, A, R, src, put_padded(dst))
        interior(CZ, CY, go, 2)
        faces.arrive(src, step)
        boundary_z(CZ, CY, go)
        faces.start(dst, step + 1, (0, 1))
        boundary_y(CZ, CY, go)
        faces.start(dst, step + 1, (2, 3))
    loads[2].wait()
    loads[3].wait()
    interior(CZ, CY, product, 1)
    faces.arrive(W4, 3)
    boundary_z(CZ, CY, product)
    boundary_y(CZ, CY, product)
    last = pltpu.make_async_copy(T, out, store)
    last.start()
    for e, buf in enumerate((W1, W2, W3, W4)):
        faces.finish(buf, e)
    last.wait()


def observe(cells_s, plane_s, cells_v, weights, field, parts, rows0, rows1):
    B, K = cells_s.shape
    step = cells_v.shape[1]
    sub, _ = ids((128, K))
    _, lane = ids((8, 128))

    def fetch(b, rows):
        for k in range(K):
            rows[pl.ds(k, 1), :] = field[:, row_of(cells_s[b, k])]

    fetch(0, rows0)

    def group(g, acc):
        low, high = acc
        inner = cells_v[g] & 127
        for j in range(step):
            b = g * step + j
            rows, later = (rows0, rows1) if j % 2 == 0 else (rows1, rows0)
            fetch(jnp.minimum(b + 1, B - 1), later)
            hot = jnp.where(sub == inner[j : j + 1, :], 1.0, 0.0).T
            picked = rows[...] * hot
            main = picked.astype(BF16)
            rest = (picked - main.astype(F32)).astype(BF16)
            w = weights[b]
            both = jnp.dot(w, main, preferred_element_type=F32) + jnp.dot(
                w, rest, preferred_element_type=F32
            )
            total = jnp.sum(both, axis=1, keepdims=True)
            p = plane_s[b]
            p = jnp.where(p < PLANES, p, -1000)
            for n in range(3):
                low = low + jnp.where(lane == p + PLANES * n, total[8 * n : 8 * n + 8], 0.0)
            high = high + jnp.where(lane == p, total[24:32], 0.0)
        return low, high

    zero = jnp.zeros((8, 128), F32)
    low, high = lax.fori_loop(0, B // step, group, (zero, zero))
    parts[0, 0:8, :] = low
    parts[0, 8:16, :] = high


def sum_all(parts, out, held, send, recv):
    copies = []
    for at, (n, me, target) in enumerate(lines()):
        mine = []
        for d in range(1, n):
            c = pltpu.make_async_remote_copy(
                src_ref=parts.at[at],
                dst_ref=held.at[at, me],
                send_sem=send.at[at, d],
                recv_sem=recv.at[at, d],
                device_id=target(lax.rem(me + d, n)),
                device_id_type=MESH,
            )
            c.start()
            mine.append(c)
        held[at, me] = parts[at]
        for c in mine:
            c.wait_recv()
        total = held[at, 0]
        for i in range(1, n):
            total = total + held[at, i]
        if at < 3:
            parts[at + 1] = total
        else:
            out[...] = total
        copies += mine
    for c in copies:
        c.wait_send()


def scatter_kernel(B, K, copies, cells_s, plane_s, cells_v, weights, table, out, obs, values0, values1, *accs):
    cells = out.shape[1]

    @pl.loop(0, cells // 8192)
    def _(i):
        for acc in accs:
            acc[:, pl.ds(pl.multiple_of(i * 8192, 8192), 8192)] = jnp.zeros((1, 8192), F32)

    step = divisor(B, 8)
    sub, _ = ids((128, K))
    _, lane = ids((32, 128))
    packed = table[...]
    low = packed[0:8]
    po = jnp.concatenate(
        [low, pltpu.roll(low, 128 - PLANES, 1), pltpu.roll(low, 128 - 2 * PLANES, 1), packed[8:16]],
        axis=0,
    )
    po = jnp.where(lane < PLANES, po, 0.0)
    obs[...] = po[:, :PLANES]

    def spread(b, values):
        inner = cells_v[b // step] & 127
        row = jnp.zeros((1, K), jnp.int32)
        for j in range(step):
            row = jnp.where(b % step == j, inner[j : j + 1, :], row)
        mine = jnp.sum(jnp.where(lane == plane_s[b], po, 0.0), axis=1, keepdims=True)
        back = jnp.sum(weights[b].astype(F32) * mine, axis=0, keepdims=True)
        values[...] = jnp.where(sub == row, back, 0.0).T

    def add(b, values):
        for k in range(0, K, copies):
            at = [row_of(cells_s[b, k + j]) for j in range(copies)]
            new = [accs[j][:, at[j]] + values[pl.ds(k + j, 1), :] for j in range(copies)]
            for j in range(copies):
                accs[j][:, at[j]] = new[j]

    spread(0, values0)

    @pl.loop(0, B // 2)
    def _(i):
        spread(2 * i + 1, values1)
        add(2 * i, values0)
        spread(jnp.minimum(2 * i + 2, B - 1), values0)
        add(2 * i + 1, values1)

    @pl.loop(0, cells // 8192)
    def _(i):
        here = pl.ds(pl.multiple_of(i * 8192, 8192), 8192)
        total = accs[0][:, here]
        for acc in accs[1:]:
            total = total + acc[:, here]
        out[:, here] = total


def shards(velocity, yield_stress, stress_step, block_weights, block_cells, block_plane):
    CZ, CY, NX = velocity.shape
    B, S, K = block_weights.shape
    core, padded = (CZ, CY, 8, 128), (CZ + 2, CY + 2, 8, 128)
    tiles = (CZ * CY // 8, 64, 128)

    def tiled(field):
        return field.reshape(CZ, CY // 8, 8, 8, 128).transpose(0, 1, 3, 2, 4).reshape(tiles)

    def sds(shape):
        return jax.ShapeDtypeStruct(shape, F32)

    def vm(shape):
        return pltpu.VMEM(shape, F32)

    def params(n=None):
        if n is None:
            return pltpu.CompilerParams(vmem_limit_bytes=LIMIT)
        return pltpu.CompilerParams(vmem_limit_bytes=LIMIT, collective_id=n, has_side_effects=True)

    DMA = pltpu.SemaphoreType.DMA
    groups = divisor(B, 8)
    cells_v = block_cells.reshape(B // groups, groups, K)
    mu, vel, reg, table = pl.pallas_call(
        functools.partial(tangent_kernel, CZ, CY),
        out_shape=(sds(padded), sds(padded), sds(core), sds((16, 128))),
        in_specs=[SMEM, SMEM, VMEM] + [ANY] * 4,
        out_specs=(ANY, ANY, ANY, VMEM),
        scratch_shapes=[vm(tiles)] * 3 + [pltpu.VMEM((B, S, K), BF16)]
        + [vm(padded)] * 3 + [vm(core), vm((6,) + core), vm(core)] + [vm(padded)] * 3
        + [vm((1, CZ * CY * 1024)), vm((K, 128)), vm((K, 128))]
        + [vm((4, 4, 16, 128)), vm((4, 16, 128))]
        + [DMA((4,)), DMA((3,)), DMA((6, 4)), DMA((6, 4)), DMA((4, 4)), DMA((4, 4))],
        compiler_params=params(0),
        name="tangent",
    )(
        block_cells, block_plane, cells_v,
        tiled(velocity), tiled(yield_stress), tiled(stress_step), block_weights,
    )

    copies = 8
    adj, obs = pl.pallas_call(
        functools.partial(scatter_kernel, B, K, copies),
        out_shape=(sds((1, CZ * CY * 1024)), sds((S, PLANES))),
        in_specs=[SMEM, SMEM, VMEM, VMEM, VMEM],
        out_specs=(VMEM, VMEM),
        scratch_shapes=[vm((K, 128))] * 2 + [vm((1, CZ * CY * 1024))] * copies,
        compiler_params=params(),
        name="scatter",
    )(block_cells, block_plane, cells_v, block_weights, table)

    product = pl.pallas_call(
        functools.partial(adjoint_kernel, CZ, CY),
        out_shape=sds(core),
        in_specs=[ANY] * 4,
        out_specs=ANY,
        scratch_shapes=[vm(core), vm(padded), vm(padded), vm(core), vm((6,) + core), vm(core)]
        + [vm(padded)] * 4 + [vm(core), DMA((4,)), DMA, DMA((4, 4)), DMA((4, 4))],
        compiler_params=params(1),
        name="adjoint",
    )(adj.reshape(core), mu, vel, reg)
    return product.reshape(CZ, CY, NX), obs.T


def solution(mesh):
    placed = (
        P("gz", "xy", None),
        P("gz", "xy", None),
        P("gz", "xy", None),
        P(("gz", "xy"), None, None),
        P(("gz", "xy"), None),
        P(("gz", "xy")),
    )
    return jax.shard_map(
        shards, mesh=mesh, in_specs=placed, out_specs=(P("gz", "xy", None), P()), check_vma=False
    )
```

```python
import functools
import jax
import jax.numpy as jnp
from jax import lax
from jax.experimental import pallas as pl
from jax.experimental.pallas import tpu as pltpu
from jax.sharding import PartitionSpec as P

PLANES = 40
KEEP = 0.2
DAMP = 0.8
MESH = pl.DeviceIdType.MESH
F32 = jnp.float32
BF16 = jnp.bfloat16
VMEM = pl.BlockSpec(memory_space=pltpu.VMEM)
SMEM = pl.BlockSpec(memory_space=pltpu.SMEM)
ANY = pl.BlockSpec(memory_space=pl.ANY)
LIMIT = 56 * 1024 * 1024


def ids(shape):
    rank = len(shape)
    return (
        lax.broadcasted_iota(jnp.int32, shape, rank - 2),
        lax.broadcasted_iota(jnp.int32, shape, rank - 1),
    )


def x_next(a, wrap=True):
    sub, lane = ids(a.shape)
    r = pltpu.roll(a, 127, a.ndim - 1)
    r = jnp.where(lane == 127, pltpu.roll(r, 7, a.ndim - 2), r)
    return r if wrap else jnp.where((lane == 127) & (sub == 7), 0.0, r)


def x_prev(a, wrap=True):
    sub, lane = ids(a.shape)
    r = pltpu.roll(a, 1, a.ndim - 1)
    r = jnp.where(lane == 0, pltpu.roll(r, 1, a.ndim - 2), r)
    return r if wrap else jnp.where((lane == 0) & (sub == 0), 0.0, r)


def divisor(n, most):
    return max(d for d in range(1, most + 1) if n % d == 0)


class Faces:
    def __init__(self, CZ, CY, send, recv):
        self.CZ, self.CY, self.send, self.recv = CZ, CY, send, recv
        G, X = lax.axis_size("gz"), lax.axis_size("xy")
        g, x = lax.axis_index("gz"), lax.axis_index("xy")
        self.has = (g > 0, g < G - 1, x > 0, x < X - 1)
        lower, upper = jnp.maximum(g - 1, 0), jnp.minimum(g + 1, G - 1)
        left, right = jnp.maximum(x - 1, 0), jnp.minimum(x + 1, X - 1)
        self.to = ((lower, x), (upper, x), (g, left), (g, right))

    def copy(self, buf, e, d):
        CZ, CY = self.CZ, self.CY
        zs, ys = pl.ds(1, CZ), pl.ds(1, CY)
        src = (buf.at[1, ys], buf.at[CZ, ys], buf.at[zs, 1], buf.at[zs, CY])[d]
        dst = (buf.at[CZ + 1, ys], buf.at[0, ys], buf.at[zs, CY + 1], buf.at[zs, 0])[d]
        return pltpu.make_async_remote_copy(
            src_ref=src,
            dst_ref=dst,
            send_sem=self.send.at[e, d],
            recv_sem=self.recv.at[e, d],
            device_id=self.to[d],
            device_id_type=MESH,
        )

    def start(self, buf, e, which=(0, 1, 2, 3)):
        for d in which:

            @pl.when(self.has[d])
            def _():
                self.copy(buf, e, d).start()

    def arrive(self, buf, e):
        for d in range(4):

            @pl.when(self.has[d ^ 1])
            def _():
                self.copy(buf, e, d).wait_recv()

    def finish(self, buf, e):
        for d in range(4):

            @pl.when(self.has[d])
            def _():
                self.copy(buf, e, d).wait_send()


def lines():
    G, X = lax.axis_size("gz"), lax.axis_size("xy")
    g, x = lax.axis_index("gz"), lax.axis_index("xy")
    across = min(X, 4)
    return (
        (2, g % 2, lambda t: ((g // 2) * 2 + t, x)),
        (G // 2, g // 2, lambda t: (t * 2 + g % 2, x)),
        (across, x % across, lambda t: (g, (x // across) * across + t)),
        (X // across, x // across, lambda t: (g, t * across + x % across)),
    )


def greet(all_lines):
    G, X = lax.axis_size("gz"), lax.axis_size("xy")
    g, x = lax.axis_index("gz"), lax.axis_index("xy")
    sem = pltpu.get_barrier_semaphore()
    count = jnp.int32(0)
    for has, to in (
        (g > 0, (jnp.maximum(g - 1, 0), x)),
        (g < G - 1, (jnp.minimum(g + 1, G - 1), x)),
        (x > 0, (g, jnp.maximum(x - 1, 0))),
        (x < X - 1, (g, jnp.minimum(x + 1, X - 1))),
    ):
        count = count + has.astype(jnp.int32)

        @pl.when(has)
        def _():
            pl.semaphore_signal(sem, inc=1, device_id=to, device_id_type=MESH)

    if all_lines:
        for n, me, target in lines():
            for d in range(1, n):
                to = target(lax.rem(me + d, n))
                pl.semaphore_signal(sem, inc=1, device_id=to, device_id_type=MESH)
            count = count + (n - 1)
    pl.semaphore_wait(sem, count)


def clear_faces(bufs, CZ, CY):
    plane = jnp.zeros((CY + 2, 8, 128), F32)
    row = jnp.zeros((CZ, 8, 128), F32)
    for buf in bufs:
        buf[0] = plane
        buf[CZ + 1] = plane
        buf[pl.ds(1, CZ), 0] = row
        buf[pl.ds(1, CZ), CY + 1] = row


def interior(CZ, CY, f, planes):
    yn = divisor(CY - 2, 6)
    planes = divisor(CZ - 2, planes)

    @pl.loop(0, (CZ - 2) // planes)
    def _(i):
        for p in range(planes):
            for y in range(1, CY - 1, yn):
                f(1 + i * planes + p, y, 1, yn)


def boundary_z(CZ, CY, f):
    yn = divisor(CY, 8)

    @pl.loop(0, 2)
    def _(i):
        for y in range(0, CY, yn):
            f(i * (CZ - 1), y, 1, yn)


def boundary_y(CZ, CY, f):
    zn = divisor(CZ - 2, 8)
    for y in (0, CY - 1):
        for z in range(1, CZ - 1, zn):
            f(z, y, zn, 1)


def around(ref, z, y, zn, yn):
    zs, ys = pl.ds(z + 1, zn), pl.ds(y + 1, yn)
    if zn == 1:
        wide = ref[zs, pl.ds(y, yn + 2)]
        return (
            wide[:, 1 : yn + 1],
            wide[:, :yn],
            wide[:, 2:],
            ref[pl.ds(z, 1), ys],
            ref[pl.ds(z + 2, 1), ys],
        )
    wide = ref[pl.ds(z, zn + 2), ys]
    return (
        wide[1 : zn + 1],
        ref[zs, pl.ds(y, yn)],
        ref[zs, pl.ds(y + 2, yn)],
        wide[:zn],
        wide[2:],
    )


def coefficients(MU, z, y, zn, yn):
    m, ym, yp, zm, zp = around(MU, z, y, zn, yn)
    xm, xp = x_prev(m, False), x_next(m, False)
    total = ((xm + xp) + (ym + yp)) + (zm + zp)
    dinv = DAMP / (1.0 + (3.0 * m + 0.5 * total))
    half = 0.5 * dinv
    sub, lane = ids(m.shape)
    first, last = (sub == 0) & (lane == 0), (sub == 7) & (lane == 127)
    faces = (
        jnp.where(first, 0.0, half * (m + xm)),
        jnp.where(last, 0.0, half * (m + xp)),
        half * (m + ym),
        half * (m + yp),
        half * (m + zm),
        half * (m + zp),
    )
    return faces, dinv


def sweep(A, R, src, put, z, y, zn, yn):
    w, ym, yp, zm, zp = around(src, z, y, zn, yn)
    zs, ys = pl.ds(z, zn), pl.ds(y, yn)
    total = KEEP * w + R[zs, ys]
    for at, value in enumerate((x_prev(w), x_next(w), ym, yp, zm, zp)):
        total = total + A[at, zs, ys] * value
    put(total, z, y, zn, yn)


def put_padded(dst):
    def put(value, z, y, zn, yn):
        dst[pl.ds(z + 1, zn), pl.ds(y + 1, yn)] = value

    return put


def put_rows(dst, CY):
    def put(value, z, y, zn, yn):
        for i in range(zn):
            at = pl.multiple_of(((z + i) * CY + y) * 8, 8)
            dst[pl.ds(at, 8 * yn), :] = value[i].reshape(8 * yn, 128)

    return put


def by_row(ref):
    return ref.reshape(ref.shape[0], 1, 128)


def tangent_kernel(
    CZ, CY, cells_s, plane_s, cells_v, v_in, y_in, s_in, w_in, mu_out, v_out, reg_out, table,
    vin, yin, sin, weights, V, MU, DMU, REG, A, R, W1, W2, W3, T, rows0, rows1, held, parts,
    load, store, send, recv, sum_send, sum_recv,
):
    tiles = CY // 8
    loads = [
        pltpu.make_async_copy(src, dst, load.at[i])
        for i, (src, dst) in enumerate(
            ((v_in, vin), (y_in, yin), (s_in, sin), (w_in, weights))
        )
    ]
    for c in loads:
        c.start()
    faces = Faces(CZ, CY, send, recv)
    clear_faces((V, MU, DMU, W1, W2, W3), CZ, CY)
    greet(True)
    loads[0].wait()

    @pl.loop(0, CZ * tiles // 2)
    def _(j):
        for i in (2 * j, 2 * j + 1):
            z, y = i // tiles, (i % tiles) * 8
            for s in range(8):
                V[z + 1, y + 1 + s] = vin[i, pl.ds(s, 8, stride=8), :]

    faces.start(V, 0)
    loads[1].wait()
    loads[2].wait()

    def viscosity(z, t):
        i, y = z * tiles + t, t * 8
        here = pl.ds(y + 1, 8)
        c = V[z + 1, here]
        dz = V[z + 2, here] - c
        dy = V[z + 1, pl.ds(y + 2, 8)] - c
        dx = x_next(c, False) - c
        reg = lax.rsqrt((dz * dz + dy * dy + dx * dx) + 0.01)
        REG[z, pl.ds(y, 8)] = reg
        for s in range(8):
            MU[z + 1, y + 1 + s] = 1.0 + yin[i, pl.ds(s, 8, stride=8), :] * reg[s]
            DMU[z + 1, y + 1 + s] = sin[i, pl.ds(s, 8, stride=8), :] * reg[s]

    @pl.loop(0, CZ - 1)
    def _(z):
        for t in range(tiles - 1):
            viscosity(z, t)

    faces.arrive(V, 0)
    for t in range(tiles):
        viscosity(CZ - 1, t)

    pair = divisor(CZ - 1, 3)

    @pl.loop(0, (CZ - 1) // pair)
    def _(i):
        for j in range(pair):
            viscosity(i * pair + j, tiles - 1)

    faces.start(MU, 1)
    faces.start(DMU, 2)

    def source(z, y, zn, yn):
        zs, ys = pl.ds(z, zn), pl.ds(y, yn)
        face, dinv = coefficients(MU, z, y, zn, yn)
        for at in range(6):
            A[at, zs, ys] = face[at]
        d, *ds = around(DMU, z, y, zn, yn)
        v, *vs = around(V, z, y, zn, yn)
        ds += [x_prev(d, False), x_next(d, False)]
        vs += [x_prev(v, False), x_next(v, False)]
        total = (d + ds[0]) * (vs[0] - v)
        for dn, vn in zip(ds[1:], vs[1:]):
            total = total + (d + dn) * (vn - v)
        first = (0.5 * dinv) * total
        R[zs, ys] = first
        W1[pl.ds(z + 1, zn), pl.ds(y + 1, yn)] = first

    interior(CZ, CY, source, 1)
    faces.arrive(MU, 1)
    faces.arrive(DMU, 2)
    stores = [
        pltpu.make_async_copy(src, dst, store.at[i])
        for i, (src, dst) in enumerate(((MU, mu_out), (V, v_out), (REG, reg_out)))
    ]
    for c in stores:
        c.start()
    boundary_z(CZ, CY, source)
    faces.start(W1, 3, (0, 1))
    boundary_y(CZ, CY, source)
    faces.start(W1, 3, (2, 3))
    for step, (src, dst) in enumerate(((W1, W2), (W2, W3), (W3, None))):
        put = put_rows(T, CY) if dst is None else put_padded(dst)
        go = functools.partial(sweep, A, R, src, put)
        interior(CZ, CY, go, 2)
        faces.arrive(src, 3 + step)
        boundary_z(CZ, CY, go)
        if dst is not None:
            faces.start(dst, 4 + step, (0, 1))
        boundary_y(CZ, CY, go)
        if dst is not None:
            faces.start(dst, 4 + step, (2, 3))

    loads[3].wait()
    observe(cells_s, plane_s, cells_v, weights, T, parts, rows0, rows1)
    sum_all(parts, table, held, sum_send, sum_recv)
    for e, buf in enumerate((V, MU, DMU, W1, W2, W3)):
        faces.finish(buf, e)
    for c in stores:
        c.wait()


def adjoint_kernel(
    CZ, CY, q_in, mu_in, v_in, reg_in, out,
    Q, MU, V, REG, A, R, W1, W2, W3, W4, T, load, store, send, recv,
):
    loads = [
        pltpu.make_async_copy(src, dst, load.at[i])
        for i, (src, dst) in enumerate(((mu_in, MU), (q_in, Q), (v_in, V), (reg_in, REG)))
    ]
    for c in loads:
        c.start()
    faces = Faces(CZ, CY, send, recv)
    clear_faces((W1, W2, W3, W4), CZ, CY)
    greet(False)
    loads[0].wait()
    loads[1].wait()

    def begin(z, y, zn, yn):
        zs, ys = pl.ds(z, zn), pl.ds(y, yn)
        face, dinv = coefficients(MU, z, y, zn, yn)
        for at in range(6):
            A[at, zs, ys] = face[at]
        first = dinv * Q[zs, ys]
        R[zs, ys] = first
        W1[pl.ds(z + 1, zn), pl.ds(y + 1, yn)] = first

    def product(z, y, zn, yn):
        zs, ys = pl.ds(z, zn), pl.ds(y, yn)
        v, *vs = around(V, z, y, zn, yn)
        a, *many = around(W4, z, y, zn, yn)
        vs += [x_prev(v, False), x_next(v, False)]
        many += [x_prev(a, False), x_next(a, False)]
        total = (v - vs[0]) * (a - many[0])
        for vn, an in zip(vs[1:], many[1:]):
            total = total + (v - vn) * (a - an)
        total = (-0.5 * REG[zs, ys]) * total
        for i in range(zn):
            for j in range(yn):
                at = (z + i) * (CY // 8) + (y + j) // 8
                T[at, pl.ds((y + j) % 8, 8, stride=8), :] = total[i, j]

    boundary_z(CZ, CY, begin)
    faces.start(W1, 0, (0, 1))
    boundary_y(CZ, CY, begin)
    faces.start(W1, 0, (2, 3))
    interior(CZ, CY, begin, 1)
    for step, (src, dst) in enumerate(((W1, W2), (W2, W3), (W3, W4))):
        go = functools.partial(sweep, A, R, src, put_padded(dst))
        interior(CZ, CY, go, 2)
        faces.arrive(src, step)
        boundary_z(CZ, CY, go)
        faces.start(dst, step + 1, (0, 1))
        boundary_y(CZ, CY, go)
        faces.start(dst, step + 1, (2, 3))
    loads[2].wait()
    loads[3].wait()
    interior(CZ, CY, product, 1)
    faces.arrive(W4, 3)
    boundary_z(CZ, CY, product)
    boundary_y(CZ, CY, product)
    last = pltpu.make_async_copy(T, out, store)
    last.start()
    for e, buf in enumerate((W1, W2, W3, W4)):
        faces.finish(buf, e)
    last.wait()


def observe(cells_s, plane_s, cells_v, weights, field, parts, rows0, rows1):
    B, K = cells_s.shape
    step = cells_v.shape[1]
    sub, _ = ids((128, K))
    _, lane = ids((8, 128))

    def fetch(b, rows):
        for k in range(K):
            by_row(rows)[k] = by_row(field)[cells_s[b, k] >> 7]

    fetch(0, rows0)

    def group(g, acc):
        low, high = acc
        inner = cells_v[g] & 127
        for j in range(step):
            b = g * step + j
            rows, later = (rows0, rows1) if j % 2 == 0 else (rows1, rows0)
            fetch(jnp.minimum(b + 1, B - 1), later)
            hot = jnp.where(sub == inner[j : j + 1, :], 1.0, 0.0).T
            picked = rows[...] * hot
            main = picked.astype(BF16)
            rest = (picked - main.astype(F32)).astype(BF16)
            w = weights[b]
            both = jnp.dot(w, main, preferred_element_type=F32) + jnp.dot(
                w, rest, preferred_element_type=F32
            )
            total = jnp.sum(both, axis=1, keepdims=True)
            p = plane_s[b]
            p = jnp.where(p < PLANES, p, -1000)
            for n in range(3):
                low = low + jnp.where(lane == p + PLANES * n, total[8 * n : 8 * n + 8], 0.0)
            high = high + jnp.where(lane == p, total[24:32], 0.0)
        return low, high

    zero = jnp.zeros((8, 128), F32)
    low, high = lax.fori_loop(0, B // step, group, (zero, zero))
    parts[0, 0:8, :] = low
    parts[0, 8:16, :] = high


def sum_all(parts, out, held, send, recv):
    copies = []
    for at, (n, me, target) in enumerate(lines()):
        mine = []
        for d in range(1, n):
            c = pltpu.make_async_remote_copy(
                src_ref=parts.at[at],
                dst_ref=held.at[at, me],
                send_sem=send.at[at, d],
                recv_sem=recv.at[at, d],
                device_id=target(lax.rem(me + d, n)),
                device_id_type=MESH,
            )
            c.start()
            mine.append(c)
        held[at, me] = parts[at]
        for c in mine:
            c.wait_recv()
        total = held[at, 0]
        for i in range(1, n):
            total = total + held[at, i]
        if at < 3:
            parts[at + 1] = total
        else:
            out[...] = total
        copies += mine
    for c in copies:
        c.wait_send()


def scatter_kernel(B, K, copies, cells_s, plane_s, cells_v, weights, table, out, obs, values0, values1, *accs):
    size = out.shape[0]
    accs3 = [by_row(acc) for acc in accs]

    @pl.loop(0, size // 64)
    def _(i):
        for acc in accs:
            acc[pl.ds(pl.multiple_of(i * 64, 64), 64), :] = jnp.zeros((64, 128), F32)

    step = divisor(B, 8)
    sub, _ = ids((128, K))
    _, lane = ids((32, 128))
    packed = table[...]
    low = packed[0:8]
    po = jnp.concatenate(
        [low, pltpu.roll(low, 128 - PLANES, 1), pltpu.roll(low, 128 - 2 * PLANES, 1), packed[8:16]],
        axis=0,
    )
    po = jnp.where(lane < PLANES, po, 0.0)
    obs[...] = po[:, :PLANES]

    def spread(b, values):
        inner = cells_v[b // step] & 127
        row = jnp.zeros((1, K), jnp.int32)
        for j in range(step):
            row = jnp.where(b % step == j, inner[j : j + 1, :], row)
        mine = jnp.sum(jnp.where(lane == plane_s[b], po, 0.0), axis=1, keepdims=True)
        back = jnp.sum(weights[b].astype(F32) * mine, axis=0, keepdims=True)
        values[...] = jnp.where(sub == row, back, 0.0).T

    def add(b, values):
        for k in range(0, K, copies):
            at = [cells_s[b, k + j] >> 7 for j in range(copies)]
            new = [accs3[j][at[j]] + by_row(values)[k + j] for j in range(copies)]
            for j in range(copies):
                accs3[j][at[j]] = new[j]

    spread(0, values0)

    @pl.loop(0, B // 2)
    def _(i):
        spread(2 * i + 1, values1)
        add(2 * i, values0)
        spread(jnp.minimum(2 * i + 2, B - 1), values0)
        add(2 * i + 1, values1)

    @pl.loop(0, size // 64)
    def _(i):
        here = pl.ds(pl.multiple_of(i * 64, 64), 64)
        total = accs[0][here, :]
        for acc in accs[1:]:
            total = total + acc[here, :]
        out[here, :] = total


def shards(velocity, yield_stress, stress_step, block_weights, block_cells, block_plane):
    CZ, CY, NX = velocity.shape
    B, S, K = block_weights.shape
    core, padded = (CZ, CY, 8, 128), (CZ + 2, CY + 2, 8, 128)
    tiles = (CZ * CY // 8, 64, 128)

    def tiled(field):
        return field.reshape(CZ, CY // 8, 8, 8, 128).transpose(0, 1, 3, 2, 4).reshape(tiles)

    def sds(shape):
        return jax.ShapeDtypeStruct(shape, F32)

    def vm(shape):
        return pltpu.VMEM(shape, F32)

    def params(n=None):
        if n is None:
            return pltpu.CompilerParams(vmem_limit_bytes=LIMIT)
        return pltpu.CompilerParams(vmem_limit_bytes=LIMIT, collective_id=n, has_side_effects=True)

    DMA = pltpu.SemaphoreType.DMA
    groups = divisor(B, 8)
    cells_v = block_cells.reshape(B // groups, groups, K)
    mu, vel, reg, table = pl.pallas_call(
        functools.partial(tangent_kernel, CZ, CY),
        out_shape=(sds(padded), sds(padded), sds(core), sds((16, 128))),
        in_specs=[SMEM, SMEM, VMEM] + [ANY] * 4,
        out_specs=(ANY, ANY, ANY, VMEM),
        scratch_shapes=[vm(tiles)] * 3 + [pltpu.VMEM((B, S, K), BF16)]
        + [vm(padded)] * 3 + [vm(core), vm((6,) + core), vm(core)] + [vm(padded)] * 3
        + [vm((CZ * CY * 8, 128)), vm((K, 128)), vm((K, 128))]
        + [vm((4, 4, 16, 128)), vm((4, 16, 128))]
        + [DMA((4,)), DMA((3,)), DMA((6, 4)), DMA((6, 4)), DMA((4, 4)), DMA((4, 4))],
        compiler_params=params(0),
        name="tangent",
    )(
        block_cells, block_plane, cells_v,
        tiled(velocity), tiled(yield_stress), tiled(stress_step), block_weights,
    )

    copies = 8
    adj, obs = pl.pallas_call(
        functools.partial(scatter_kernel, B, K, copies),
        out_shape=(sds((CZ * CY * 8, 128)), sds((S, PLANES))),
        in_specs=[SMEM, SMEM, VMEM, VMEM, VMEM],
        out_specs=(VMEM, VMEM),
        scratch_shapes=[vm((K, 128))] * 2 + [vm((CZ * CY * 8, 128))] * copies,
        compiler_params=params(),
        name="scatter",
    )(block_cells, block_plane, cells_v, block_weights, table)

    product = pl.pallas_call(
        functools.partial(adjoint_kernel, CZ, CY),
        out_shape=sds(tiles),
        in_specs=[ANY] * 4,
        out_specs=ANY,
        scratch_shapes=[vm(core), vm(padded), vm(padded), vm(core), vm((6,) + core), vm(core)]
        + [vm(padded)] * 4 + [vm(tiles), DMA((4,)), DMA, DMA((4, 4)), DMA((4, 4))],
        compiler_params=params(1),
        name="adjoint",
    )(adj.reshape(core), mu, vel, reg)
    product = product.reshape(CZ, CY // 8, 8, 8, 128).transpose(0, 1, 3, 2, 4)
    return product.reshape(CZ, CY, NX), obs.T


def solution(mesh):
    placed = (
        P("gz", "xy", None),
        P("gz", "xy", None),
        P("gz", "xy", None),
        P(("gz", "xy"), None, None),
        P(("gz", "xy"), None),
        P(("gz", "xy")),
    )
    return jax.shard_map(
        shards, mesh=mesh, in_specs=placed, out_specs=(P("gz", "xy", None), P()), check_vma=False
    )
```

```python
import functools
import jax
import jax.numpy as jnp
from jax import lax
from jax.experimental import pallas as pl
from jax.experimental.pallas import tpu as pltpu
from jax.sharding import PartitionSpec as P

PLANES = 40
KEEP = 0.2
DAMP = 0.8
MESH = pl.DeviceIdType.MESH
F32 = jnp.float32
BF16 = jnp.bfloat16
VMEM = pl.BlockSpec(memory_space=pltpu.VMEM)
SMEM = pl.BlockSpec(memory_space=pltpu.SMEM)
ANY = pl.BlockSpec(memory_space=pl.ANY)
HBM = pl.BlockSpec(memory_space=pltpu.HBM)
MIB = 1024 * 1024
BATCH = 16


def ids(shape):
    rank = len(shape)
    return (
        lax.broadcasted_iota(jnp.int32, shape, rank - 2),
        lax.broadcasted_iota(jnp.int32, shape, rank - 1),
    )


def x_next(a, wrap=True):
    sub, lane = ids(a.shape)
    r = pltpu.roll(a, 127, a.ndim - 1)
    r = jnp.where(lane == 127, pltpu.roll(r, 7, a.ndim - 2), r)
    return r if wrap else jnp.where((lane == 127) & (sub == 7), 0.0, r)


def x_prev(a, wrap=True):
    sub, lane = ids(a.shape)
    r = pltpu.roll(a, 1, a.ndim - 1)
    r = jnp.where(lane == 0, pltpu.roll(r, 1, a.ndim - 2), r)
    return r if wrap else jnp.where((lane == 0) & (sub == 0), 0.0, r)


def divisor(n, most):
    return max(d for d in range(1, most + 1) if n % d == 0)


class Faces:
    def __init__(self, CZ, CY, send, recv):
        self.CZ, self.CY, self.send, self.recv = CZ, CY, send, recv
        G, X = lax.axis_size("gz"), lax.axis_size("xy")
        g, x = lax.axis_index("gz"), lax.axis_index("xy")
        self.has = (g > 0, g < G - 1, x > 0, x < X - 1)
        lower, upper = jnp.maximum(g - 1, 0), jnp.minimum(g + 1, G - 1)
        left, right = jnp.maximum(x - 1, 0), jnp.minimum(x + 1, X - 1)
        self.to = ((lower, x), (upper, x), (g, left), (g, right))

    def copy(self, buf, e, d):
        CZ, CY = self.CZ, self.CY
        zs, ys = pl.ds(1, CZ), pl.ds(1, CY)
        src = (buf.at[1, ys], buf.at[CZ, ys], buf.at[zs, 1], buf.at[zs, CY])[d]
        dst = (buf.at[CZ + 1, ys], buf.at[0, ys], buf.at[zs, CY + 1], buf.at[zs, 0])[d]
        return pltpu.make_async_remote_copy(
            src_ref=src,
            dst_ref=dst,
            send_sem=self.send.at[e, d],
            recv_sem=self.recv.at[e, d],
            device_id=self.to[d],
            device_id_type=MESH,
        )

    def start(self, buf, e, which=(0, 1, 2, 3)):
        for d in which:

            @pl.when(self.has[d])
            def _():
                self.copy(buf, e, d).start()

    def arrive(self, buf, e):
        for d in range(4):

            @pl.when(self.has[d ^ 1])
            def _():
                self.copy(buf, e, d).wait_recv()

    def finish(self, buf, e):
        for d in range(4):

            @pl.when(self.has[d])
            def _():
                self.copy(buf, e, d).wait_send()


def lines():
    G, X = lax.axis_size("gz"), lax.axis_size("xy")
    g, x = lax.axis_index("gz"), lax.axis_index("xy")
    across = min(X, 4)
    return (
        (2, g % 2, lambda t: ((g // 2) * 2 + t, x)),
        (G // 2, g // 2, lambda t: (t * 2 + g % 2, x)),
        (across, x % across, lambda t: (g, (x // across) * across + t)),
        (X // across, x // across, lambda t: (g, t * across + x % across)),
    )


def greet(all_lines):
    G, X = lax.axis_size("gz"), lax.axis_size("xy")
    g, x = lax.axis_index("gz"), lax.axis_index("xy")
    sem = pltpu.get_barrier_semaphore()
    count = jnp.int32(0)
    for has, to in (
        (g > 0, (jnp.maximum(g - 1, 0), x)),
        (g < G - 1, (jnp.minimum(g + 1, G - 1), x)),
        (x > 0, (g, jnp.maximum(x - 1, 0))),
        (x < X - 1, (g, jnp.minimum(x + 1, X - 1))),
    ):
        count = count + has.astype(jnp.int32)

        @pl.when(has)
        def _():
            pl.semaphore_signal(sem, inc=1, device_id=to, device_id_type=MESH)

    if all_lines:
        for n, me, target in lines():
            for d in range(1, n):
                to = target(lax.rem(me + d, n))
                pl.semaphore_signal(sem, inc=1, device_id=to, device_id_type=MESH)
            count = count + (n - 1)
    pl.semaphore_wait(sem, count)


def clear_faces(bufs, CZ, CY):
    plane = jnp.zeros((CY + 2, 8, 128), F32)
    row = jnp.zeros((CZ, 8, 128), F32)
    for buf in bufs:
        buf[0] = plane
        buf[CZ + 1] = plane
        buf[pl.ds(1, CZ), 0] = row
        buf[pl.ds(1, CZ), CY + 1] = row


def interior(CZ, CY, f, planes):
    yn = divisor(CY - 2, 6)
    planes = divisor(CZ - 2, planes)

    @pl.loop(0, (CZ - 2) // planes)
    def _(i):
        for p in range(planes):
            for y in range(1, CY - 1, yn):
                f(1 + i * planes + p, y, 1, yn)


def boundary_z(CZ, CY, f):
    yn = divisor(CY, 8)

    @pl.loop(0, 2)
    def _(i):
        for y in range(0, CY, yn):
            f(i * (CZ - 1), y, 1, yn)


def boundary_y(CZ, CY, f):
    zn = divisor(CZ - 2, 8)
    for y in (0, CY - 1):
        for z in range(1, CZ - 1, zn):
            f(z, y, zn, 1)


def around(ref, z, y, zn, yn):
    zs, ys = pl.ds(z + 1, zn), pl.ds(y + 1, yn)
    if zn == 1:
        wide = ref[zs, pl.ds(y, yn + 2)]
        return (
            wide[:, 1 : yn + 1],
            wide[:, :yn],
            wide[:, 2:],
            ref[pl.ds(z, 1), ys],
            ref[pl.ds(z + 2, 1), ys],
        )
    wide = ref[pl.ds(z, zn + 2), ys]
    return (
        wide[1 : zn + 1],
        ref[zs, pl.ds(y, yn)],
        ref[zs, pl.ds(y + 2, yn)],
        wide[:zn],
        wide[2:],
    )


def regularized(dz, dy, dx):
    return lax.rsqrt((dz * dz + dy * dy + dx * dx) + 0.01)


def coefficients(MU, z, y, zn, yn):
    m, ym, yp, zm, zp = around(MU, z, y, zn, yn)
    xm, xp = x_prev(m, False), x_next(m, False)
    total = ((xm + xp) + (ym + yp)) + (zm + zp)
    dinv = DAMP / (1.0 + (3.0 * m + 0.5 * total))
    half = 0.5 * dinv
    sub, lane = ids(m.shape)
    first, last = (sub == 0) & (lane == 0), (sub == 7) & (lane == 127)
    faces = (
        jnp.where(first, 0.0, half * (m + xm)),
        jnp.where(last, 0.0, half * (m + xp)),
        half * (m + ym),
        half * (m + yp),
        half * (m + zm),
        half * (m + zp),
    )
    return faces, dinv


def sweep(A, R, src, put, z, y, zn, yn):
    w, ym, yp, zm, zp = around(src, z, y, zn, yn)
    zs, ys = pl.ds(z, zn), pl.ds(y, yn)
    total = KEEP * w + R[zs, ys]
    for at, value in enumerate((x_prev(w), x_next(w), ym, yp, zm, zp)):
        total = total + A[at, zs, ys] * value
    put(total, z, y, zn, yn)


def put_padded(dst):
    def put(value, z, y, zn, yn):
        dst[pl.ds(z + 1, zn), pl.ds(y + 1, yn)] = value

    return put


def put_rows(dst, CY):
    def put(value, z, y, zn, yn):
        for i in range(zn):
            at = pl.multiple_of(((z + i) * CY + y) * 8, 8)
            dst[pl.ds(at, 8 * yn), :] = value[i].reshape(8 * yn, 128)

    return put


def by_row(ref):
    return ref.reshape(ref.shape[0], 1, 128)


def tangent_kernel(
    CZ, CY, c_in, p_in, q_in, v_in, y_in, s_in, w_in, mu_out, v_out, table,
    cells_s, plane_s, cells_v, vin, yin, sin, weights, V, MU, DMU, A, R, W1, W2, W3, T, rows0, rows1, held, parts,
    load, store, send, recv, sum_send, sum_recv,
):
    tiles = CY // 8
    loads = [
        pltpu.make_async_copy(src, dst, load.at[i])
        for i, (src, dst) in enumerate(
            (
                (v_in, vin), (y_in, yin), (s_in, sin), (w_in, weights),
                (c_in, cells_s), (p_in, plane_s), (q_in, cells_v),
            )
        )
    ]
    for c in loads:
        c.start()
    faces = Faces(CZ, CY, send, recv)
    clear_faces((V, MU, DMU, W1, W2, W3), CZ, CY)
    greet(True)
    loads[0].wait()

    @pl.loop(0, CZ * tiles // 2)
    def _(j):
        for i in (2 * j, 2 * j + 1):
            z, y = i // tiles, (i % tiles) * 8
            for s in range(8):
                V[z + 1, y + 1 + s] = vin[i, pl.ds(s, 8, stride=8), :]

    faces.start(V, 0)
    loads[1].wait()
    loads[2].wait()

    def viscosity(z, t):
        i, y = z * tiles + t, t * 8
        here = pl.ds(y + 1, 8)
        c = V[z + 1, here]
        dz = V[z + 2, here] - c
        dy = V[z + 1, pl.ds(y + 2, 8)] - c
        dx = x_next(c, False) - c
        reg = regularized(dz, dy, dx)
        for s in range(8):
            MU[z + 1, y + 1 + s] = 1.0 + yin[i, pl.ds(s, 8, stride=8), :] * reg[s]
            DMU[z + 1, y + 1 + s] = sin[i, pl.ds(s, 8, stride=8), :] * reg[s]

    @pl.loop(0, CZ - 1)
    def _(z):
        for t in range(tiles - 1):
            viscosity(z, t)

    faces.arrive(V, 0)
    for t in range(tiles):
        viscosity(CZ - 1, t)

    pair = divisor(CZ - 1, 3)

    @pl.loop(0, (CZ - 1) // pair)
    def _(i):
        for j in range(pair):
            viscosity(i * pair + j, tiles - 1)

    faces.start(MU, 1)
    faces.start(DMU, 2)

    def source(z, y, zn, yn):
        zs, ys = pl.ds(z, zn), pl.ds(y, yn)
        face, dinv = coefficients(MU, z, y, zn, yn)
        for at in range(6):
            A[at, zs, ys] = face[at]
        d, *ds = around(DMU, z, y, zn, yn)
        v, *vs = around(V, z, y, zn, yn)
        ds += [x_prev(d, False), x_next(d, False)]
        vs += [x_prev(v, False), x_next(v, False)]
        total = (d + ds[0]) * (vs[0] - v)
        for dn, vn in zip(ds[1:], vs[1:]):
            total = total + (d + dn) * (vn - v)
        first = (0.5 * dinv) * total
        R[zs, ys] = first
        W1[pl.ds(z + 1, zn), pl.ds(y + 1, yn)] = first

    interior(CZ, CY, source, 1)
    faces.arrive(MU, 1)
    faces.arrive(DMU, 2)
    stores = [
        pltpu.make_async_copy(src, dst, store.at[i])
        for i, (src, dst) in enumerate(((MU, mu_out), (V, v_out)))
    ]
    for c in stores:
        c.start()
    boundary_z(CZ, CY, source)
    faces.start(W1, 3, (0, 1))
    boundary_y(CZ, CY, source)
    faces.start(W1, 3, (2, 3))
    for step, (src, dst) in enumerate(((W1, W2), (W2, W3), (W3, None))):
        put = put_rows(T, CY) if dst is None else put_padded(dst)
        go = functools.partial(sweep, A, R, src, put)
        interior(CZ, CY, go, 2)
        faces.arrive(src, 3 + step)
        boundary_z(CZ, CY, go)
        if dst is not None:
            faces.start(dst, 4 + step, (0, 1))
        boundary_y(CZ, CY, go)
        if dst is not None:
            faces.start(dst, 4 + step, (2, 3))

    for c in loads[3:]:
        c.wait()
    observe(cells_s, plane_s, cells_v, weights, T, parts, (rows0, rows1))
    sum_all(parts, table, held, sum_send, sum_recv)
    for e, buf in enumerate((V, MU, DMU, W1, W2, W3)):
        faces.finish(buf, e)
    for c in stores:
        c.wait()


def adjoint_kernel(
    CZ, CY, q_in, mu_in, v_in, out,
    Q, MU, V, A, R, W1, W2, W3, W4, T, load, store, send, recv,
):
    loads = [
        pltpu.make_async_copy(src, dst, load.at[i])
        for i, (src, dst) in enumerate(((mu_in, MU), (q_in, Q), (v_in, V)))
    ]
    for c in loads:
        c.start()
    faces = Faces(CZ, CY, send, recv)
    clear_faces((W1, W2, W3, W4), CZ, CY)
    greet(False)
    loads[0].wait()
    loads[1].wait()

    def begin(z, y, zn, yn):
        zs, ys = pl.ds(z, zn), pl.ds(y, yn)
        face, dinv = coefficients(MU, z, y, zn, yn)
        for at in range(6):
            A[at, zs, ys] = face[at]
        first = dinv * Q[zs, ys]
        R[zs, ys] = first
        W1[pl.ds(z + 1, zn), pl.ds(y + 1, yn)] = first

    def product(z, y, zn, yn):
        zs, ys = pl.ds(z, zn), pl.ds(y, yn)
        v, *vs = around(V, z, y, zn, yn)
        a, *many = around(W4, z, y, zn, yn)
        vs += [x_prev(v, False), x_next(v, False)]
        many += [x_prev(a, False), x_next(a, False)]
        total = (v - vs[0]) * (a - many[0])
        for vn, an in zip(vs[1:], many[1:]):
            total = total + (v - vn) * (a - an)
        dy, dz, dx = vs[1] - v, vs[3] - v, vs[5] - v
        T[zs, ys] = (-0.5 * regularized(dz, dy, dx)) * total

    boundary_z(CZ, CY, begin)
    faces.start(W1, 0, (0, 1))
    boundary_y(CZ, CY, begin)
    faces.start(W1, 0, (2, 3))
    interior(CZ, CY, begin, 1)
    for step, (src, dst) in enumerate(((W1, W2), (W2, W3), (W3, W4))):
        go = functools.partial(sweep, A, R, src, put_padded(dst))
        interior(CZ, CY, go, 2)
        faces.arrive(src, step)
        boundary_z(CZ, CY, go)
        faces.start(dst, step + 1, (0, 1))
        boundary_y(CZ, CY, go)
        faces.start(dst, step + 1, (2, 3))
    loads[2].wait()
    interior(CZ, CY, product, 1)
    faces.arrive(W4, 3)
    boundary_z(CZ, CY, product)
    boundary_y(CZ, CY, product)
    last = pltpu.make_async_copy(T, out, store)
    last.start()
    for e, buf in enumerate((W1, W2, W3, W4)):
        faces.finish(buf, e)
    last.wait()


def observe(cells_s, plane_s, cells_v, weights, field, parts, rows):
    B, K = cells_s.shape
    group = rows[0].shape[0] // K
    sub, _ = ids((128, K))
    _, lane = ids((8, 128))
    source = by_row(field)

    def fetch(g, held):
        target = by_row(held)
        for j in range(group):
            for k in range(0, K, BATCH):
                got = [source[cells_s[g * group + j, k + i] >> 7] for i in range(BATCH)]
                for i in range(BATCH):
                    target[j * K + k + i] = got[i]

    def share(g, held, acc):
        low, high = acc
        inner = cells_v[g] & 127
        for j in range(group):
            b = g * group + j
            across = held[j * K : (j + 1) * K, :].T
            cells = jnp.sum(jnp.where(sub == inner[j : j + 1, :], across, 0.0), axis=0, keepdims=True)
            total = jnp.sum(weights[b].astype(F32) * cells, axis=1, keepdims=True)
            p = plane_s[b]
            p = jnp.where(p < PLANES, p, -1000)
            for n in range(3):
                low = low + jnp.where(lane == p + PLANES * n, total[8 * n : 8 * n + 8], 0.0)
            high = high + jnp.where(lane == p, total[24:32], 0.0)
        return low, high

    fetch(0, rows[0])

    def body(i, acc):
        fetch(2 * i + 1, rows[1])
        acc = share(2 * i, rows[0], acc)
        fetch(jnp.minimum(2 * i + 2, B // group - 1), rows[0])
        return share(2 * i + 1, rows[1], acc)

    zero = jnp.zeros((8, 128), F32)
    low, high = lax.fori_loop(0, B // (2 * group), body, (zero, zero))
    parts[0, 0:8, :] = low
    parts[0, 8:16, :] = high


def sum_all(parts, out, held, send, recv):
    copies = []
    for at, (n, me, target) in enumerate(lines()):
        mine = []
        for d in range(1, n):
            c = pltpu.make_async_remote_copy(
                src_ref=parts.at[at],
                dst_ref=held.at[at, me],
                send_sem=send.at[at, d],
                recv_sem=recv.at[at, d],
                device_id=target(lax.rem(me + d, n)),
                device_id_type=MESH,
            )
            c.start()
            mine.append(c)
        held[at, me] = parts[at]
        for c in mine:
            c.wait_recv()
        total = held[at, 0]
        for i in range(1, n):
            total = total + held[at, i]
        if at < 3:
            parts[at + 1] = total
        else:
            out[...] = total
        copies += mine
    for c in copies:
        c.wait_send()


def scatter_kernel(
    copies, c_in, p_in, q_in, w_in, t_in, out, obs,
    cells_s, plane_s, cells_v, weights, table, values0, values1, total, load, store, *accs,
):
    B, K = cells_s.shape
    group = values0.shape[0] // K
    size = total.shape[0]
    loads = [
        pltpu.make_async_copy(src, dst, load.at[i])
        for i, (src, dst) in enumerate(
            ((c_in, cells_s), (p_in, plane_s), (q_in, cells_v), (w_in, weights), (t_in, table))
        )
    ]
    for c in loads:
        c.start()
    accs3 = [by_row(acc) for acc in accs]

    @pl.loop(0, size // 64)
    def _(i):
        for acc in accs:
            acc[pl.ds(pl.multiple_of(i * 64, 64), 64), :] = jnp.zeros((64, 128), F32)

    for c in loads:
        c.wait()
    sub, _ = ids((128, K))
    _, lane = ids((32, 128))
    packed = table[...]
    low = packed[0:8]
    po = jnp.concatenate(
        [low, pltpu.roll(low, 128 - PLANES, 1), pltpu.roll(low, 128 - 2 * PLANES, 1), packed[8:16]],
        axis=0,
    )
    po = jnp.where(lane < PLANES, po, 0.0)
    obs[...] = po[:, :PLANES]

    def spread(g, values):
        inner = cells_v[g] & 127
        for j in range(group):
            b = g * group + j
            mine = jnp.sum(jnp.where(lane == plane_s[b], po, 0.0), axis=1, keepdims=True)
            back = jnp.sum(weights[b].astype(F32) * mine, axis=0, keepdims=True)
            values[j * K : (j + 1) * K, :] = jnp.where(sub == inner[j : j + 1, :], back, 0.0).T

    def add(g, values):
        held = by_row(values)
        for j in range(group):
            for k in range(0, K, copies):
                at = [cells_s[g * group + j, k + i] >> 7 for i in range(copies)]
                new = [accs3[i][at[i]] + held[j * K + k + i] for i in range(copies)]
                for i in range(copies):
                    accs3[i][at[i]] = new[i]

    spread(0, values0)

    @pl.loop(0, B // (2 * group))
    def _(i):
        spread(2 * i + 1, values1)
        add(2 * i, values0)
        spread(jnp.minimum(2 * i + 2, B // group - 1), values0)
        add(2 * i + 1, values1)

    parts = store.shape[0]
    step = size // parts
    stores = []
    for n in range(parts):

        @pl.loop(0, step // 64)
        def _(i):
            here = pl.ds(pl.multiple_of(n * step + i * 64, 64), 64)
            value = accs[0][here, :]
            for acc in accs[1:]:
                value = value + acc[here, :]
            total[here, :] = value

        here = pl.ds(n * step, step)
        stores.append(pltpu.make_async_copy(total.at[here], out.at[here], store.at[n]))
        stores[-1].start()
    for c in stores:
        c.wait()


def shards(velocity, yield_stress, stress_step, block_weights, block_cells, block_plane):
    CZ, CY, NX = velocity.shape
    B, S, K = block_weights.shape
    core, padded = (CZ, CY, 8, 128), (CZ + 2, CY + 2, 8, 128)
    tiles = (CZ * CY // 8, 64, 128)

    def tiled(field):
        return field.reshape(CZ, CY // 8, 8, 8, 128).transpose(0, 1, 3, 2, 4).reshape(tiles)

    def sds(shape):
        return jax.ShapeDtypeStruct(shape, F32)

    def vm(shape):
        return pltpu.VMEM(shape, F32)

    def params(limit, n=None):
        if n is None:
            return pltpu.CompilerParams(vmem_limit_bytes=limit * MIB)
        return pltpu.CompilerParams(
            vmem_limit_bytes=limit * MIB, collective_id=n, has_side_effects=True
        )

    DMA = pltpu.SemaphoreType.DMA
    group = divisor(B // 2, 4)
    cells_v = block_cells.reshape(B // group, group, K)
    small = [pltpu.SMEM((B, K), jnp.int32), pltpu.SMEM((B,), jnp.int32)]
    small += [pltpu.VMEM(cells_v.shape, jnp.int32)]
    held = [vm((group * K, 128))] * 2
    mu, vel, table = pl.pallas_call(
        functools.partial(tangent_kernel, CZ, CY),
        out_shape=(sds(padded), sds(padded), sds((16, 128))),
        in_specs=[HBM] * 7,
        out_specs=(ANY, ANY, VMEM),
        scratch_shapes=small + [vm(tiles)] * 3 + [pltpu.VMEM((B, S, K), BF16)]
        + [vm(padded)] * 3 + [vm((6,) + core), vm(core)] + [vm(padded)] * 3
        + [vm((CZ * CY * 8, 128))] + held
        + [vm((4, 4, 16, 128)), vm((4, 16, 128))]
        + [DMA((7,)), DMA((2,)), DMA((6, 4)), DMA((6, 4)), DMA((4, 4)), DMA((4, 4))],
        compiler_params=params(56, 0),
        name="tangent",
    )(
        block_cells, block_plane, cells_v,
        tiled(velocity), tiled(yield_stress), tiled(stress_step), block_weights,
    )

    copies = 8
    adj, obs = pl.pallas_call(
        functools.partial(scatter_kernel, copies),
        out_shape=(sds((CZ * CY * 8, 128)), sds((S, PLANES))),
        in_specs=[HBM] * 4 + [ANY],
        out_specs=(ANY, VMEM),
        scratch_shapes=small + [pltpu.VMEM((B, S, K), BF16), vm((16, 128))] + held
        + [vm((CZ * CY * 8, 128)), DMA((5,)), DMA((4,))]
        + [vm((CZ * CY * 8, 128))] * copies,
        compiler_params=params(24),
        name="scatter",
    )(block_cells, block_plane, cells_v, block_weights, table)

    product = pl.pallas_call(
        functools.partial(adjoint_kernel, CZ, CY),
        out_shape=sds(core),
        in_specs=[ANY] * 3,
        out_specs=ANY,
        scratch_shapes=[vm(core), vm(padded), vm(padded), vm((6,) + core), vm(core)]
        + [vm(padded)] * 4 + [vm(core), DMA((3,)), DMA, DMA((4, 4)), DMA((4, 4))],
        compiler_params=params(48, 1),
        name="adjoint",
    )(adj.reshape(core), mu, vel)
    return product.reshape(CZ, CY, NX), obs.T


def solution(mesh):
    placed = (
        P("gz", "xy", None),
        P("gz", "xy", None),
        P("gz", "xy", None),
        P(("gz", "xy"), None, None),
        P(("gz", "xy"), None),
        P(("gz", "xy")),
    )
    return jax.shard_map(
        shards, mesh=mesh, in_specs=placed, out_specs=(P("gz", "xy", None), P()), check_vma=False
    )
```

```python
import functools
import jax
import jax.numpy as jnp
from jax import lax
from jax.experimental import pallas as pl
from jax.experimental.pallas import tpu as pltpu
from jax.sharding import PartitionSpec as P

PLANES = 40
KEEP = 0.2
DAMP = 0.8
MESH = pl.DeviceIdType.MESH
F32 = jnp.float32
BF16 = jnp.bfloat16
VMEM = pl.BlockSpec(memory_space=pltpu.VMEM)
SMEM = pl.BlockSpec(memory_space=pltpu.SMEM)
ANY = pl.BlockSpec(memory_space=pl.ANY)
HBM = pl.BlockSpec(memory_space=pltpu.HBM)
MIB = 1024 * 1024
BATCH = 16


def ids(shape):
    rank = len(shape)
    return (
        lax.broadcasted_iota(jnp.int32, shape, rank - 2),
        lax.broadcasted_iota(jnp.int32, shape, rank - 1),
    )


def x_next(a, wrap=True):
    sub, lane = ids(a.shape)
    r = pltpu.roll(a, 127, a.ndim - 1)
    r = jnp.where(lane == 127, pltpu.roll(r, 7, a.ndim - 2), r)
    return r if wrap else jnp.where((lane == 127) & (sub == 7), 0.0, r)


def x_prev(a, wrap=True):
    sub, lane = ids(a.shape)
    r = pltpu.roll(a, 1, a.ndim - 1)
    r = jnp.where(lane == 0, pltpu.roll(r, 1, a.ndim - 2), r)
    return r if wrap else jnp.where((lane == 0) & (sub == 0), 0.0, r)


def divisor(n, most):
    return max(d for d in range(1, most + 1) if n % d == 0)


class Faces:
    def __init__(self, CZ, CY, send, recv):
        self.CZ, self.CY, self.send, self.recv = CZ, CY, send, recv
        G, X = lax.axis_size("gz"), lax.axis_size("xy")
        g, x = lax.axis_index("gz"), lax.axis_index("xy")
        self.has = (g > 0, g < G - 1, x > 0, x < X - 1)
        lower, upper = jnp.maximum(g - 1, 0), jnp.minimum(g + 1, G - 1)
        left, right = jnp.maximum(x - 1, 0), jnp.minimum(x + 1, X - 1)
        self.to = ((lower, x), (upper, x), (g, left), (g, right))

    def copy(self, buf, e, d):
        CZ, CY = self.CZ, self.CY
        zs, ys = pl.ds(1, CZ), pl.ds(1, CY)
        src = (buf.at[1, ys], buf.at[CZ, ys], buf.at[zs, 1], buf.at[zs, CY])[d]
        dst = (buf.at[CZ + 1, ys], buf.at[0, ys], buf.at[zs, CY + 1], buf.at[zs, 0])[d]
        return pltpu.make_async_remote_copy(
            src_ref=src,
            dst_ref=dst,
            send_sem=self.send.at[e, d],
            recv_sem=self.recv.at[e, d],
            device_id=self.to[d],
            device_id_type=MESH,
        )

    def start(self, buf, e, which=(0, 1, 2, 3)):
        for d in which:

            @pl.when(self.has[d])
            def _():
                self.copy(buf, e, d).start()

    def arrive(self, buf, e):
        for d in range(4):

            @pl.when(self.has[d ^ 1])
            def _():
                self.copy(buf, e, d).wait_recv()

    def finish(self, buf, e):
        for d in range(4):

            @pl.when(self.has[d])
            def _():
                self.copy(buf, e, d).wait_send()


def lines():
    G, X = lax.axis_size("gz"), lax.axis_size("xy")
    g, x = lax.axis_index("gz"), lax.axis_index("xy")
    across = min(X, 4)
    return (
        (G, g, lambda t: (t, x)),
        (across, x % across, lambda t: (g, (x // across) * across + t)),
        (X // across, x // across, lambda t: (g, t * across + x % across)),
    )


def greet(all_lines):
    G, X = lax.axis_size("gz"), lax.axis_size("xy")
    g, x = lax.axis_index("gz"), lax.axis_index("xy")
    sem = pltpu.get_barrier_semaphore()
    count = jnp.int32(0)
    for has, to in (
        (g > 0, (jnp.maximum(g - 1, 0), x)),
        (g < G - 1, (jnp.minimum(g + 1, G - 1), x)),
        (x > 0, (g, jnp.maximum(x - 1, 0))),
        (x < X - 1, (g, jnp.minimum(x + 1, X - 1))),
    ):
        count = count + has.astype(jnp.int32)

        @pl.when(has)
        def _():
            pl.semaphore_signal(sem, inc=1, device_id=to, device_id_type=MESH)

    if all_lines:
        for n, me, target in lines():
            for d in range(1, n):
                to = target(lax.rem(me + d, n))
                pl.semaphore_signal(sem, inc=1, device_id=to, device_id_type=MESH)
            count = count + (n - 1)
    pl.semaphore_wait(sem, count)


def clear_faces(bufs, CZ, CY):
    plane = jnp.zeros((CY + 2, 8, 128), F32)
    row = jnp.zeros((CZ, 8, 128), F32)
    for buf in bufs:
        buf[0] = plane
        buf[CZ + 1] = plane
        buf[pl.ds(1, CZ), 0] = row
        buf[pl.ds(1, CZ), CY + 1] = row


def interior(CZ, CY, f, planes):
    yn = divisor(CY - 2, 6)
    planes = divisor(CZ - 2, planes)

    @pl.loop(0, (CZ - 2) // planes)
    def _(i):
        for p in range(planes):
            for y in range(1, CY - 1, yn):
                f(1 + i * planes + p, y, 1, yn)


def boundary_z(CZ, CY, f):
    yn = divisor(CY, 8)

    @pl.loop(0, 2)
    def _(i):
        for y in range(0, CY, yn):
            f(i * (CZ - 1), y, 1, yn)


def boundary_y(CZ, CY, f):
    zn = divisor(CZ - 2, 8)
    for y in (0, CY - 1):
        for z in range(1, CZ - 1, zn):
            f(z, y, zn, 1)


def around(ref, z, y, zn, yn):
    zs, ys = pl.ds(z + 1, zn), pl.ds(y + 1, yn)
    if zn == 1:
        wide = ref[zs, pl.ds(y, yn + 2)]
        return (
            wide[:, 1 : yn + 1],
            wide[:, :yn],
            wide[:, 2:],
            ref[pl.ds(z, 1), ys],
            ref[pl.ds(z + 2, 1), ys],
        )
    wide = ref[pl.ds(z, zn + 2), ys]
    return (
        wide[1 : zn + 1],
        ref[zs, pl.ds(y, yn)],
        ref[zs, pl.ds(y + 2, yn)],
        wide[:zn],
        wide[2:],
    )


def regularized(dz, dy, dx):
    return lax.rsqrt((dz * dz + dy * dy + dx * dx) + 0.01)


def coefficients(MU, z, y, zn, yn):
    m, ym, yp, zm, zp = around(MU, z, y, zn, yn)
    xm, xp = x_prev(m, False), x_next(m, False)
    total = ((xm + xp) + (ym + yp)) + (zm + zp)
    dinv = DAMP / (1.0 + (3.0 * m + 0.5 * total))
    half = 0.5 * dinv
    sub, lane = ids(m.shape)
    first, last = (sub == 0) & (lane == 0), (sub == 7) & (lane == 127)
    faces = (
        jnp.where(first, 0.0, half * (m + xm)),
        jnp.where(last, 0.0, half * (m + xp)),
        half * (m + ym),
        half * (m + yp),
        half * (m + zm),
        half * (m + zp),
    )
    return faces, dinv


def sweep(A, R, src, put, z, y, zn, yn):
    w, ym, yp, zm, zp = around(src, z, y, zn, yn)
    zs, ys = pl.ds(z, zn), pl.ds(y, yn)
    total = KEEP * w + R[zs, ys]
    for at, value in enumerate((x_prev(w), x_next(w), ym, yp, zm, zp)):
        total = total + A[at, zs, ys] * value
    put(total, z, y, zn, yn)


def put_padded(dst):
    def put(value, z, y, zn, yn):
        dst[pl.ds(z + 1, zn), pl.ds(y + 1, yn)] = value

    return put


def put_rows(dst, CY):
    def put(value, z, y, zn, yn):
        for i in range(zn):
            at = pl.multiple_of(((z + i) * CY + y) * 8, 8)
            dst[pl.ds(at, 8 * yn), :] = value[i].reshape(8 * yn, 128)

    return put


def by_row(ref):
    return ref.reshape(ref.shape[0], 1, 128)


def tangent_kernel(
    CZ, CY, c_in, p_in, v_in, y_in, s_in, w_in, mu_out, v_out, rows_out, table,
    rows_s, plane_s, cells_v, rows_v, vin, yin, sin, weights, V, MU, DMU, A, R, W1, W2, W3, T, rows0, rows1, held, parts,
    load, store, send, recv, sum_send, sum_recv,
):
    tiles = CY // 8
    loads = [
        pltpu.make_async_copy(src, dst, load.at[i])
        for i, (src, dst) in enumerate(
            (
                (v_in, vin), (y_in, yin), (s_in, sin), (w_in, weights),
                (c_in, cells_v), (p_in, plane_s),
            )
        )
    ]
    for c in loads:
        c.start()
    faces = Faces(CZ, CY, send, recv)
    clear_faces((V, MU, DMU, W1, W2, W3), CZ, CY)
    greet(True)
    loads[0].wait()

    @pl.loop(0, CZ * tiles // 2)
    def _(j):
        for i in (2 * j, 2 * j + 1):
            z, y = i // tiles, (i % tiles) * 8
            for s in range(8):
                V[z + 1, y + 1 + s] = vin[i, pl.ds(s, 8, stride=8), :]

    faces.start(V, 0)
    loads[1].wait()
    loads[2].wait()

    def viscosity(z, t):
        i, y = z * tiles + t, t * 8
        here = pl.ds(y + 1, 8)
        c = V[z + 1, here]
        dz = V[z + 2, here] - c
        dy = V[z + 1, pl.ds(y + 2, 8)] - c
        dx = x_next(c, False) - c
        reg = regularized(dz, dy, dx)
        for s in range(8):
            MU[z + 1, y + 1 + s] = 1.0 + yin[i, pl.ds(s, 8, stride=8), :] * reg[s]
            DMU[z + 1, y + 1 + s] = sin[i, pl.ds(s, 8, stride=8), :] * reg[s]

    @pl.loop(0, CZ - 1)
    def _(z):
        for t in range(tiles - 1):
            viscosity(z, t)

    faces.arrive(V, 0)
    for t in range(tiles):
        viscosity(CZ - 1, t)

    pair = divisor(CZ - 1, 3)

    @pl.loop(0, (CZ - 1) // pair)
    def _(i):
        for j in range(pair):
            viscosity(i * pair + j, tiles - 1)

    faces.start(MU, 1)
    faces.start(DMU, 2)
    loads[4].wait()
    rows_v[...] = cells_v[...] >> 7
    numbers = [
        pltpu.make_async_copy(rows_v, dst, store.at[2 + i])
        for i, dst in enumerate((rows_s, rows_out))
    ]
    for c in numbers:
        c.start()

    def source(z, y, zn, yn):
        zs, ys = pl.ds(z, zn), pl.ds(y, yn)
        face, dinv = coefficients(MU, z, y, zn, yn)
        for at in range(6):
            A[at, zs, ys] = face[at]
        d, *ds = around(DMU, z, y, zn, yn)
        v, *vs = around(V, z, y, zn, yn)
        ds += [x_prev(d, False), x_next(d, False)]
        vs += [x_prev(v, False), x_next(v, False)]
        total = (d + ds[0]) * (vs[0] - v)
        for dn, vn in zip(ds[1:], vs[1:]):
            total = total + (d + dn) * (vn - v)
        first = (0.5 * dinv) * total
        R[zs, ys] = first
        W1[pl.ds(z + 1, zn), pl.ds(y + 1, yn)] = first

    interior(CZ, CY, source, 1)
    faces.arrive(MU, 1)
    faces.arrive(DMU, 2)
    stores = [
        pltpu.make_async_copy(src, dst, store.at[i])
        for i, (src, dst) in enumerate(((MU, mu_out), (V, v_out)))
    ]
    for c in stores:
        c.start()
    boundary_z(CZ, CY, source)
    faces.start(W1, 3, (0, 1))
    boundary_y(CZ, CY, source)
    faces.start(W1, 3, (2, 3))
    for step, (src, dst) in enumerate(((W1, W2), (W2, W3), (W3, None))):
        put = put_rows(T, CY) if dst is None else put_padded(dst)
        go = functools.partial(sweep, A, R, src, put)
        interior(CZ, CY, go, 2)
        faces.arrive(src, 3 + step)
        boundary_z(CZ, CY, go)
        if dst is not None:
            faces.start(dst, 4 + step, (0, 1))
        boundary_y(CZ, CY, go)
        if dst is not None:
            faces.start(dst, 4 + step, (2, 3))

    loads[3].wait()
    loads[5].wait()
    numbers[0].wait()
    observe(rows_s, plane_s, cells_v, weights, T, parts, (rows0, rows1))
    sum_all(parts, table, held, sum_send, sum_recv)
    for e, buf in enumerate((V, MU, DMU, W1, W2, W3)):
        faces.finish(buf, e)
    for c in stores + numbers[1:]:
        c.wait()


def adjoint_kernel(
    CZ, CY, q_in, mu_in, v_in, out,
    Q, MU, V, A, R, W1, W2, W3, W4, T, load, store, send, recv,
):
    loads = [
        pltpu.make_async_copy(src, dst, load.at[i])
        for i, (src, dst) in enumerate(((mu_in, MU), (q_in, Q), (v_in, V)))
    ]
    for c in loads:
        c.start()
    faces = Faces(CZ, CY, send, recv)
    clear_faces((W1, W2, W3, W4), CZ, CY)
    greet(False)
    loads[0].wait()
    loads[1].wait()

    def begin(z, y, zn, yn):
        zs, ys = pl.ds(z, zn), pl.ds(y, yn)
        face, dinv = coefficients(MU, z, y, zn, yn)
        for at in range(6):
            A[at, zs, ys] = face[at]
        first = dinv * Q[zs, ys]
        R[zs, ys] = first
        W1[pl.ds(z + 1, zn), pl.ds(y + 1, yn)] = first

    def product(z, y, zn, yn):
        zs, ys = pl.ds(z, zn), pl.ds(y, yn)
        v, *vs = around(V, z, y, zn, yn)
        a, *many = around(W4, z, y, zn, yn)
        vs += [x_prev(v, False), x_next(v, False)]
        many += [x_prev(a, False), x_next(a, False)]
        total = (v - vs[0]) * (a - many[0])
        for vn, an in zip(vs[1:], many[1:]):
            total = total + (v - vn) * (a - an)
        dy, dz, dx = vs[1] - v, vs[3] - v, vs[5] - v
        T[zs, ys] = (-0.5 * regularized(dz, dy, dx)) * total

    boundary_z(CZ, CY, begin)
    faces.start(W1, 0, (0, 1))
    boundary_y(CZ, CY, begin)
    faces.start(W1, 0, (2, 3))
    interior(CZ, CY, begin, 1)
    for step, (src, dst) in enumerate(((W1, W2), (W2, W3), (W3, W4))):
        go = functools.partial(sweep, A, R, src, put_padded(dst))
        interior(CZ, CY, go, 2)
        faces.arrive(src, step)
        boundary_z(CZ, CY, go)
        faces.start(dst, step + 1, (0, 1))
        boundary_y(CZ, CY, go)
        faces.start(dst, step + 1, (2, 3))
    loads[2].wait()
    interior(CZ, CY, product, 1)
    faces.arrive(W4, 3)
    boundary_z(CZ, CY, product)
    boundary_y(CZ, CY, product)
    last = pltpu.make_async_copy(T, out, store)
    last.start()
    for e, buf in enumerate((W1, W2, W3, W4)):
        faces.finish(buf, e)
    last.wait()


def observe(rows_s, plane_s, cells_v, weights, field, parts, rows):
    B, K = rows_s.shape
    group = rows[0].shape[0] // K
    sub, _ = ids((128, K))
    _, lane = ids((8, 128))
    source = by_row(field)

    def fetch(g, held):
        target = by_row(held)
        for j in range(group):
            for k in range(0, K, BATCH):
                got = [source[rows_s[g * group + j, k + i]] for i in range(BATCH)]
                for i in range(BATCH):
                    target[j * K + k + i] = got[i]

    def share(g, held, acc):
        low, high = acc
        for j in range(group):
            b = g * group + j
            inner = by_row(cells_v)[b] & 127
            across = held[j * K : (j + 1) * K, :].T
            cells = jnp.sum(jnp.where(sub == inner, across, 0.0), axis=0, keepdims=True)
            total = jnp.sum(weights[b].astype(F32) * cells, axis=1, keepdims=True)
            p = plane_s[b]
            p = jnp.where(p < PLANES, p, -1000)
            for n in range(3):
                low = low + jnp.where(lane == p + PLANES * n, total[8 * n : 8 * n + 8], 0.0)
            high = high + jnp.where(lane == p, total[24:32], 0.0)
        return low, high

    fetch(0, rows[0])

    def body(i, acc):
        fetch(2 * i + 1, rows[1])
        acc = share(2 * i, rows[0], acc)
        fetch(jnp.minimum(2 * i + 2, B // group - 1), rows[0])
        return share(2 * i + 1, rows[1], acc)

    zero = jnp.zeros((8, 128), F32)
    low, high = lax.fori_loop(0, B // (2 * group), body, (zero, zero))
    parts[0, 0:8, :] = low
    parts[0, 8:16, :] = high


def sum_all(parts, out, held, send, recv):
    copies = []
    for at, (n, me, target) in enumerate(lines()):
        mine = []
        for d in range(1, n):
            c = pltpu.make_async_remote_copy(
                src_ref=parts.at[at],
                dst_ref=held.at[at, me],
                send_sem=send.at[at, d],
                recv_sem=recv.at[at, d],
                device_id=target(lax.rem(me + d, n)),
                device_id_type=MESH,
            )
            c.start()
            mine.append(c)
        held[at, me] = parts[at]
        for c in mine:
            c.wait_recv()
        total = held[at, 0]
        for i in range(1, n):
            total = total + held[at, i]
        if at < 2:
            parts[at + 1] = total
        else:
            out[...] = total
        copies += mine
    for c in copies:
        c.wait_send()


def scatter_kernel(copies, rows_s, plane_s, cells_v, weights, table, out, obs, values0, values1, *accs):
    B, K = rows_s.shape
    group = values0.shape[0] // K
    size = out.shape[0]
    accs3 = [by_row(acc) for acc in accs]

    @pl.loop(0, size // 64)
    def _(i):
        for acc in accs:
            acc[pl.ds(pl.multiple_of(i * 64, 64), 64), :] = jnp.zeros((64, 128), F32)

    sub, _ = ids((128, K))
    _, lane = ids((32, 128))
    packed = table[...]
    low = packed[0:8]
    po = jnp.concatenate(
        [low, pltpu.roll(low, 128 - PLANES, 1), pltpu.roll(low, 128 - 2 * PLANES, 1), packed[8:16]],
        axis=0,
    )
    po = jnp.where(lane < PLANES, po, 0.0)
    obs[...] = po[:, :PLANES]

    def spread(g, values):
        for j in range(group):
            b = g * group + j
            inner = by_row(cells_v)[b] & 127
            mine = jnp.sum(jnp.where(lane == plane_s[b], po, 0.0), axis=1, keepdims=True)
            back = jnp.sum(weights[b].astype(F32) * mine, axis=0, keepdims=True)
            values[j * K : (j + 1) * K, :] = jnp.where(sub == inner, back, 0.0).T

    def add(g, values):
        held = by_row(values)
        for j in range(group):
            for k in range(0, K, copies):
                at = [rows_s[g * group + j, k + i] for i in range(copies)]
                new = [accs3[i][at[i]] + held[j * K + k + i] for i in range(copies)]
                for i in range(copies):
                    accs3[i][at[i]] = new[i]

    spread(0, values0)

    @pl.loop(0, B // (2 * group))
    def _(i):
        spread(2 * i + 1, values1)
        add(2 * i, values0)
        spread(jnp.minimum(2 * i + 2, B // group - 1), values0)
        add(2 * i + 1, values1)

    @pl.loop(0, size // 64)
    def _(i):
        here = pl.ds(pl.multiple_of(i * 64, 64), 64)
        value = accs[0][here, :]
        for acc in accs[1:]:
            value = value + acc[here, :]
        out[here, :] = value


def shards(velocity, yield_stress, stress_step, block_weights, block_cells, block_plane):
    CZ, CY, NX = velocity.shape
    B, S, K = block_weights.shape
    core, padded = (CZ, CY, 8, 128), (CZ + 2, CY + 2, 8, 128)
    tiles = (CZ * CY // 8, 64, 128)

    def tiled(field):
        return field.reshape(CZ, CY // 8, 8, 8, 128).transpose(0, 1, 3, 2, 4).reshape(tiles)

    def sds(shape):
        return jax.ShapeDtypeStruct(shape, F32)

    def vm(shape):
        return pltpu.VMEM(shape, F32)

    def params(limit, n=None):
        if n is None:
            return pltpu.CompilerParams(vmem_limit_bytes=limit * MIB)
        return pltpu.CompilerParams(
            vmem_limit_bytes=limit * MIB, collective_id=n, has_side_effects=True
        )

    DMA = pltpu.SemaphoreType.DMA
    numbers = jax.ShapeDtypeStruct((B, K), jnp.int32)
    held = [vm((K, 128))] * 2
    mu, vel, rows, table = pl.pallas_call(
        functools.partial(tangent_kernel, CZ, CY),
        out_shape=(sds(padded), sds(padded), numbers, sds((16, 128))),
        in_specs=[HBM] * 6,
        out_specs=(ANY, ANY, ANY, VMEM),
        scratch_shapes=[pltpu.SMEM((B, K), jnp.int32), pltpu.SMEM((B,), jnp.int32)]
        + [pltpu.VMEM((B, K), jnp.int32)] * 2 + [vm(tiles)] * 3 + [pltpu.VMEM((B, S, K), BF16)]
        + [vm(padded)] * 3 + [vm((6,) + core), vm(core)] + [vm(padded)] * 3
        + [vm((CZ * CY * 8, 128))] + held
        + [vm((3, 8, 16, 128)), vm((3, 16, 128))]
        + [DMA((6,)), DMA((4,)), DMA((6, 4)), DMA((6, 4)), DMA((3, 8)), DMA((3, 8))],
        compiler_params=params(56, 0),
        name="tangent",
    )(
        block_cells, block_plane,
        tiled(velocity), tiled(yield_stress), tiled(stress_step), block_weights,
    )

    copies = 8
    adj, obs = pl.pallas_call(
        functools.partial(scatter_kernel, copies),
        out_shape=(sds((CZ * CY * 8, 128)), sds((S, PLANES))),
        in_specs=[SMEM, SMEM, VMEM, VMEM, VMEM],
        out_specs=(VMEM, VMEM),
        scratch_shapes=held + [vm((CZ * CY * 8, 128))] * copies,
        compiler_params=params(24),
        name="scatter",
    )(rows, block_plane, block_cells, block_weights, table)

    product = pl.pallas_call(
        functools.partial(adjoint_kernel, CZ, CY),
        out_shape=sds(core),
        in_specs=[ANY] * 3,
        out_specs=ANY,
        scratch_shapes=[vm(core), vm(padded), vm(padded), vm((6,) + core), vm(core)]
        + [vm(padded)] * 4 + [vm(core), DMA((3,)), DMA, DMA((4, 4)), DMA((4, 4))],
        compiler_params=params(48, 1),
        name="adjoint",
    )(adj.reshape(core), mu, vel)
    return product.reshape(CZ, CY, NX), obs.T


def solution(mesh):
    placed = (
        P("gz", "xy", None),
        P("gz", "xy", None),
        P("gz", "xy", None),
        P(("gz", "xy"), None, None),
        P(("gz", "xy"), None),
        P(("gz", "xy")),
    )
    return jax.shard_map(
        shards, mesh=mesh, in_specs=placed, out_specs=(P("gz", "xy", None), P()), check_vma=False
    )
```

```python
import functools
import jax
import jax.numpy as jnp
from jax import lax
from jax.experimental import pallas as pl
from jax.experimental.pallas import tpu as pltpu
from jax.sharding import PartitionSpec as P

PLANES = 40
KEEP = 0.2
DAMP = 0.8
MESH = pl.DeviceIdType.MESH
F32 = jnp.float32
BF16 = jnp.bfloat16
VMEM = pl.BlockSpec(memory_space=pltpu.VMEM)
SMEM = pl.BlockSpec(memory_space=pltpu.SMEM)
ANY = pl.BlockSpec(memory_space=pl.ANY)
HBM = pl.BlockSpec(memory_space=pltpu.HBM)
MIB = 1024 * 1024
BATCH = 16


def ids(shape):
    rank = len(shape)
    return (
        lax.broadcasted_iota(jnp.int32, shape, rank - 2),
        lax.broadcasted_iota(jnp.int32, shape, rank - 1),
    )


def x_next(a, wrap=True):
    sub, lane = ids(a.shape)
    r = pltpu.roll(a, 127, a.ndim - 1)
    r = jnp.where(lane == 127, pltpu.roll(r, 7, a.ndim - 2), r)
    return r if wrap else jnp.where((lane == 127) & (sub == 7), 0.0, r)


def x_prev(a, wrap=True):
    sub, lane = ids(a.shape)
    r = pltpu.roll(a, 1, a.ndim - 1)
    r = jnp.where(lane == 0, pltpu.roll(r, 1, a.ndim - 2), r)
    return r if wrap else jnp.where((lane == 0) & (sub == 0), 0.0, r)


def divisor(n, most):
    return max(d for d in range(1, most + 1) if n % d == 0)


class Faces:
    def __init__(self, CZ, CY, send, recv):
        self.CZ, self.CY, self.send, self.recv = CZ, CY, send, recv
        G, X = lax.axis_size("gz"), lax.axis_size("xy")
        g, x = lax.axis_index("gz"), lax.axis_index("xy")
        self.has = (g > 0, g < G - 1, x > 0, x < X - 1)
        lower, upper = jnp.maximum(g - 1, 0), jnp.minimum(g + 1, G - 1)
        left, right = jnp.maximum(x - 1, 0), jnp.minimum(x + 1, X - 1)
        self.to = ((lower, x), (upper, x), (g, left), (g, right))

    def copy(self, buf, e, d):
        CZ, CY = self.CZ, self.CY
        zs, ys = pl.ds(1, CZ), pl.ds(1, CY)
        src = (buf.at[1, ys], buf.at[CZ, ys], buf.at[zs, 1], buf.at[zs, CY])[d]
        dst = (buf.at[CZ + 1, ys], buf.at[0, ys], buf.at[zs, CY + 1], buf.at[zs, 0])[d]
        return pltpu.make_async_remote_copy(
            src_ref=src,
            dst_ref=dst,
            send_sem=self.send.at[e, d],
            recv_sem=self.recv.at[e, d],
            device_id=self.to[d],
            device_id_type=MESH,
        )

    def leave(self, buf, e, d):
        @pl.when(self.has[d])
        def _():
            self.copy(buf, e, d).start()

    def start(self, buf, e):
        for d in range(4):
            self.leave(buf, e, d)

    def arrive(self, buf, e):
        for d in range(4):

            @pl.when(self.has[d ^ 1])
            def _():
                self.copy(buf, e, d).wait_recv()

    def finish(self, buf, e):
        for d in range(4):

            @pl.when(self.has[d])
            def _():
                self.copy(buf, e, d).wait_send()


def lines():
    G, X = lax.axis_size("gz"), lax.axis_size("xy")
    g, x = lax.axis_index("gz"), lax.axis_index("xy")
    across = min(X, 4)
    return (
        (G, g, lambda t: (t, x)),
        (across, x % across, lambda t: (g, (x // across) * across + t)),
        (X // across, x // across, lambda t: (g, t * across + x % across)),
    )


def greet(all_lines):
    G, X = lax.axis_size("gz"), lax.axis_size("xy")
    g, x = lax.axis_index("gz"), lax.axis_index("xy")
    sem = pltpu.get_barrier_semaphore()
    count = jnp.int32(0)
    for has, to in (
        (g > 0, (jnp.maximum(g - 1, 0), x)),
        (g < G - 1, (jnp.minimum(g + 1, G - 1), x)),
        (x > 0, (g, jnp.maximum(x - 1, 0))),
        (x < X - 1, (g, jnp.minimum(x + 1, X - 1))),
    ):
        count = count + has.astype(jnp.int32)

        @pl.when(has)
        def _():
            pl.semaphore_signal(sem, inc=1, device_id=to, device_id_type=MESH)

    if all_lines:
        for n, me, target in lines():
            for d in range(1, n):
                to = target(lax.rem(me + d, n))
                pl.semaphore_signal(sem, inc=1, device_id=to, device_id_type=MESH)
            count = count + (n - 1)
    pl.semaphore_wait(sem, count)


def clear_faces(bufs, CZ, CY):
    plane = jnp.zeros((CY + 2, 8, 128), F32)
    row = jnp.zeros((CZ, 8, 128), F32)
    for buf in bufs:
        buf[0] = plane
        buf[CZ + 1] = plane
        buf[pl.ds(1, CZ), 0] = row
        buf[pl.ds(1, CZ), CY + 1] = row


def interior(CZ, CY, f, planes):
    yn = divisor(CY - 2, 6)
    planes = divisor(CZ - 2, planes)

    @pl.loop(0, (CZ - 2) // planes)
    def _(i):
        for p in range(planes):
            for y in range(1, CY - 1, yn):
                f(1 + i * planes + p, y, 1, yn)


def boundary(CZ, CY, f, leave=None):
    yn, zn = divisor(CY, 8), divisor(CZ - 2, 8)
    for d, z in enumerate((0, CZ - 1)):
        for y in range(0, CY, yn):
            f(z, y, 1, yn)
        if leave:
            leave(d)
    for d, y in enumerate((0, CY - 1)):
        for z in range(1, CZ - 1, zn):
            f(z, y, zn, 1)
        if leave:
            leave(2 + d)


def around(ref, z, y, zn, yn):
    zs, ys = pl.ds(z + 1, zn), pl.ds(y + 1, yn)
    if zn == 1:
        wide = ref[zs, pl.ds(y, yn + 2)]
        return (
            wide[:, 1 : yn + 1],
            wide[:, :yn],
            wide[:, 2:],
            ref[pl.ds(z, 1), ys],
            ref[pl.ds(z + 2, 1), ys],
        )
    wide = ref[pl.ds(z, zn + 2), ys]
    return (
        wide[1 : zn + 1],
        ref[zs, pl.ds(y, yn)],
        ref[zs, pl.ds(y + 2, yn)],
        wide[:zn],
        wide[2:],
    )


def regularized(dz, dy, dx):
    return lax.rsqrt((dz * dz + dy * dy + dx * dx) + 0.01)


def coefficients(MU, z, y, zn, yn):
    m, ym, yp, zm, zp = around(MU, z, y, zn, yn)
    xm, xp = x_prev(m, False), x_next(m, False)
    total = ((xm + xp) + (ym + yp)) + (zm + zp)
    dinv = DAMP / (1.0 + (3.0 * m + 0.5 * total))
    half = 0.5 * dinv
    sub, lane = ids(m.shape)
    first, last = (sub == 0) & (lane == 0), (sub == 7) & (lane == 127)
    faces = (
        jnp.where(first, 0.0, half * (m + xm)),
        jnp.where(last, 0.0, half * (m + xp)),
        half * (m + ym),
        half * (m + yp),
        half * (m + zm),
        half * (m + zp),
    )
    return faces, dinv


def sweep(A, R, src, put, z, y, zn, yn):
    w, ym, yp, zm, zp = around(src, z, y, zn, yn)
    zs, ys = pl.ds(z, zn), pl.ds(y, yn)
    total = KEEP * w + R[zs, ys]
    for at, value in enumerate((x_prev(w), x_next(w), ym, yp, zm, zp)):
        total = total + A[at, zs, ys] * value
    put(total, z, y, zn, yn)


def put_padded(dst):
    def put(value, z, y, zn, yn):
        dst[pl.ds(z + 1, zn), pl.ds(y + 1, yn)] = value

    return put


def put_rows(dst, CY):
    def put(value, z, y, zn, yn):
        for i in range(zn):
            at = pl.multiple_of(((z + i) * CY + y) * 8, 8)
            dst[pl.ds(at, 8 * yn), :] = value[i].reshape(8 * yn, 128)

    return put


def by_row(ref):
    return ref.reshape(ref.shape[0], 1, 128)


def tangent_kernel(
    CZ, CY, c_in, p_in, v_in, y_in, s_in, w_in, mu_out, v_out, rows_out, table,
    rows_s, plane_s, cells_v, rows_v, vin, yin, sin, weights, V, MU, DMU, A, R, W1, W2, W3, T, rows0, rows1, held, parts,
    load, store, send, recv, sum_send, sum_recv,
):
    tiles = CY // 8
    loads = [
        pltpu.make_async_copy(src, dst, load.at[i])
        for i, (src, dst) in enumerate(
            (
                (v_in, vin), (y_in, yin), (s_in, sin), (w_in, weights),
                (c_in, cells_v), (p_in, plane_s),
            )
        )
    ]
    for c in loads:
        c.start()
    faces = Faces(CZ, CY, send, recv)
    clear_faces((V, MU, DMU, W1, W2, W3), CZ, CY)
    greet(True)
    loads[0].wait()

    @pl.loop(0, CZ * tiles // 2)
    def _(j):
        for i in (2 * j, 2 * j + 1):
            z, y = i // tiles, (i % tiles) * 8
            for s in range(8):
                V[z + 1, y + 1 + s] = vin[i, pl.ds(s, 8, stride=8), :]

    faces.start(V, 0)
    loads[1].wait()
    loads[2].wait()

    def viscosity(z, t):
        i, y = z * tiles + t, t * 8
        here = pl.ds(y + 1, 8)
        c = V[z + 1, here]
        dz = V[z + 2, here] - c
        dy = V[z + 1, pl.ds(y + 2, 8)] - c
        dx = x_next(c, False) - c
        reg = regularized(dz, dy, dx)
        for s in range(8):
            MU[z + 1, y + 1 + s] = 1.0 + yin[i, pl.ds(s, 8, stride=8), :] * reg[s]
            DMU[z + 1, y + 1 + s] = sin[i, pl.ds(s, 8, stride=8), :] * reg[s]

    @pl.loop(0, CZ - 1)
    def _(z):
        for t in range(tiles - 1):
            viscosity(z, t)

    faces.arrive(V, 0)
    for t in range(tiles):
        viscosity(CZ - 1, t)

    pair = divisor(CZ - 1, 3)

    @pl.loop(0, (CZ - 1) // pair)
    def _(i):
        for j in range(pair):
            viscosity(i * pair + j, tiles - 1)

    faces.start(MU, 1)
    faces.start(DMU, 2)
    loads[4].wait()
    rows_v[...] = cells_v[...] >> 7
    numbers = [
        pltpu.make_async_copy(rows_v, dst, store.at[2 + i])
        for i, dst in enumerate((rows_s, rows_out))
    ]
    for c in numbers:
        c.start()

    def source(z, y, zn, yn):
        zs, ys = pl.ds(z, zn), pl.ds(y, yn)
        face, dinv = coefficients(MU, z, y, zn, yn)
        for at in range(6):
            A[at, zs, ys] = face[at]
        d, *ds = around(DMU, z, y, zn, yn)
        v, *vs = around(V, z, y, zn, yn)
        ds += [x_prev(d, False), x_next(d, False)]
        vs += [x_prev(v, False), x_next(v, False)]
        total = (d + ds[0]) * (vs[0] - v)
        for dn, vn in zip(ds[1:], vs[1:]):
            total = total + (d + dn) * (vn - v)
        first = (0.5 * dinv) * total
        R[zs, ys] = first
        W1[pl.ds(z + 1, zn), pl.ds(y + 1, yn)] = first

    interior(CZ, CY, source, 1)
    faces.arrive(MU, 1)
    faces.arrive(DMU, 2)
    stores = [
        pltpu.make_async_copy(src, dst, store.at[i])
        for i, (src, dst) in enumerate(((MU, mu_out), (V, v_out)))
    ]
    for c in stores:
        c.start()
    boundary(CZ, CY, source, functools.partial(faces.leave, W1, 3))
    for step, (src, dst) in enumerate(((W1, W2), (W2, W3), (W3, None))):
        put = put_rows(T, CY) if dst is None else put_padded(dst)
        go = functools.partial(sweep, A, R, src, put)
        interior(CZ, CY, go, 2)
        faces.arrive(src, 3 + step)
        boundary(CZ, CY, go, dst is not None and functools.partial(faces.leave, dst, 4 + step))

    loads[3].wait()
    loads[5].wait()
    numbers[0].wait()
    observe(rows_s, plane_s, cells_v, weights, T, parts, (rows0, rows1))
    sum_all(parts, table, held, sum_send, sum_recv)
    for e, buf in enumerate((V, MU, DMU, W1, W2, W3)):
        faces.finish(buf, e)
    for c in stores + numbers[1:]:
        c.wait()


def adjoint_kernel(
    CZ, CY, q_in, mu_in, v_in, out,
    Q, MU, V, A, R, W1, W2, W3, W4, T, load, store, send, recv,
):
    loads = [
        pltpu.make_async_copy(src, dst, load.at[i])
        for i, (src, dst) in enumerate(((mu_in, MU), (q_in, Q), (v_in, V)))
    ]
    for c in loads:
        c.start()
    faces = Faces(CZ, CY, send, recv)
    clear_faces((W1, W2, W3, W4), CZ, CY)
    greet(False)
    loads[0].wait()
    loads[1].wait()

    def begin(z, y, zn, yn):
        zs, ys = pl.ds(z, zn), pl.ds(y, yn)
        face, dinv = coefficients(MU, z, y, zn, yn)
        for at in range(6):
            A[at, zs, ys] = face[at]
        first = dinv * Q[zs, ys]
        R[zs, ys] = first
        W1[pl.ds(z + 1, zn), pl.ds(y + 1, yn)] = first

    def product(z, y, zn, yn):
        zs, ys = pl.ds(z, zn), pl.ds(y, yn)
        v, *vs = around(V, z, y, zn, yn)
        a, *many = around(W4, z, y, zn, yn)
        vs += [x_prev(v, False), x_next(v, False)]
        many += [x_prev(a, False), x_next(a, False)]
        total = (v - vs[0]) * (a - many[0])
        for vn, an in zip(vs[1:], many[1:]):
            total = total + (v - vn) * (a - an)
        dy, dz, dx = vs[1] - v, vs[3] - v, vs[5] - v
        T[zs, ys] = (-0.5 * regularized(dz, dy, dx)) * total

    boundary(CZ, CY, begin, functools.partial(faces.leave, W1, 0))
    interior(CZ, CY, begin, 1)
    for step, (src, dst) in enumerate(((W1, W2), (W2, W3), (W3, W4))):
        go = functools.partial(sweep, A, R, src, put_padded(dst))
        interior(CZ, CY, go, 2)
        faces.arrive(src, step)
        boundary(CZ, CY, go, functools.partial(faces.leave, dst, step + 1))
    loads[2].wait()
    interior(CZ, CY, product, 1)
    faces.arrive(W4, 3)
    boundary(CZ, CY, product)
    last = pltpu.make_async_copy(T, out, store)
    last.start()
    for e, buf in enumerate((W1, W2, W3, W4)):
        faces.finish(buf, e)
    last.wait()


def observe(rows_s, plane_s, cells_v, weights, field, parts, rows):
    B, K = rows_s.shape
    group = rows[0].shape[0] // K
    sub, _ = ids((128, K))
    _, lane = ids((8, 128))
    source = by_row(field)

    def fetch(g, held):
        target = by_row(held)
        for j in range(group):
            for k in range(0, K, BATCH):
                got = [source[rows_s[g * group + j, k + i]] for i in range(BATCH)]
                for i in range(BATCH):
                    target[j * K + k + i] = got[i]

    def share(g, held, acc):
        low, high = acc
        for j in range(group):
            b = g * group + j
            inner = by_row(cells_v)[b] & 127
            across = held[j * K : (j + 1) * K, :].T
            cells = jnp.sum(jnp.where(sub == inner, across, 0.0), axis=0, keepdims=True)
            total = jnp.sum(weights[b].astype(F32) * cells, axis=1, keepdims=True)
            p = plane_s[b]
            p = jnp.where(p < PLANES, p, -1000)
            for n in range(3):
                low = low + jnp.where(lane == p + PLANES * n, total[8 * n : 8 * n + 8], 0.0)
            high = high + jnp.where(lane == p, total[24:32], 0.0)
        return low, high

    fetch(0, rows[0])

    def body(i, acc):
        acc = share(2 * i, rows[0], acc)
        fetch(2 * i + 1, rows[1])
        acc = share(2 * i + 1, rows[1], acc)
        fetch(jnp.minimum(2 * i + 2, B // group - 1), rows[0])
        return acc

    zero = jnp.zeros((8, 128), F32)
    low, high = lax.fori_loop(0, B // (2 * group), body, (zero, zero))
    parts[0, 0:8, :] = low
    parts[0, 8:16, :] = high


def sum_all(parts, out, held, send, recv):
    copies = []
    for at, (n, me, target) in enumerate(lines()):
        mine = []
        for d in range(1, n):
            c = pltpu.make_async_remote_copy(
                src_ref=parts.at[at],
                dst_ref=held.at[at, me],
                send_sem=send.at[at, d],
                recv_sem=recv.at[at, d],
                device_id=target(lax.rem(me + d, n)),
                device_id_type=MESH,
            )
            c.start()
            mine.append(c)
        held[at, me] = parts[at]
        for c in mine:
            c.wait_recv()
        total = held[at, 0]
        for i in range(1, n):
            total = total + held[at, i]
        if at < 2:
            parts[at + 1] = total
        else:
            out[...] = total
        copies += mine
    for c in copies:
        c.wait_send()


def scatter_kernel(copies, rows_s, plane_s, cells_v, weights, table, out, obs, values0, values1, *accs):
    B, K = rows_s.shape
    group = values0.shape[0] // K
    size = out.shape[0]
    accs3 = [by_row(acc) for acc in accs]

    @pl.loop(0, size // 64)
    def _(i):
        for acc in accs:
            acc[pl.ds(pl.multiple_of(i * 64, 64), 64), :] = jnp.zeros((64, 128), F32)

    sub, _ = ids((128, K))
    _, lane = ids((32, 128))
    packed = table[...]
    low = packed[0:8]
    po = jnp.concatenate(
        [low, pltpu.roll(low, 128 - PLANES, 1), pltpu.roll(low, 128 - 2 * PLANES, 1), packed[8:16]],
        axis=0,
    )
    po = jnp.where(lane < PLANES, po, 0.0)
    obs[...] = po[:, :PLANES]

    def spread(g, values):
        for j in range(group):
            b = g * group + j
            inner = by_row(cells_v)[b] & 127
            mine = jnp.sum(jnp.where(lane == plane_s[b], po, 0.0), axis=1, keepdims=True)
            back = jnp.sum(weights[b].astype(F32) * mine, axis=0, keepdims=True)
            values[j * K : (j + 1) * K, :] = jnp.where(sub == inner, back, 0.0).T

    def add(g, values):
        held = by_row(values)
        for j in range(group):
            for k in range(0, K, copies):
                at = [rows_s[g * group + j, k + i] for i in range(copies)]
                new = [accs3[i][at[i]] + held[j * K + k + i] for i in range(copies)]
                for i in range(copies):
                    accs3[i][at[i]] = new[i]

    spread(0, values0)

    @pl.loop(0, B // (2 * group))
    def _(i):
        spread(2 * i + 1, values1)
        add(2 * i, values0)
        spread(jnp.minimum(2 * i + 2, B // group - 1), values0)
        add(2 * i + 1, values1)

    @pl.loop(0, size // 64)
    def _(i):
        here = pl.ds(pl.multiple_of(i * 64, 64), 64)
        value = accs[0][here, :]
        for acc in accs[1:]:
            value = value + acc[here, :]
        out[here, :] = value


def shards(velocity, yield_stress, stress_step, block_weights, block_cells, block_plane):
    CZ, CY, NX = velocity.shape
    B, S, K = block_weights.shape
    core, padded = (CZ, CY, 8, 128), (CZ + 2, CY + 2, 8, 128)
    tiles = (CZ * CY // 8, 64, 128)

    def tiled(field):
        return field.reshape(CZ, CY // 8, 8, 8, 128).transpose(0, 1, 3, 2, 4).reshape(tiles)

    def sds(shape):
        return jax.ShapeDtypeStruct(shape, F32)

    def vm(shape):
        return pltpu.VMEM(shape, F32)

    def params(limit, n=None):
        if n is None:
            return pltpu.CompilerParams(vmem_limit_bytes=limit * MIB)
        return pltpu.CompilerParams(
            vmem_limit_bytes=limit * MIB, collective_id=n, has_side_effects=True
        )

    DMA = pltpu.SemaphoreType.DMA
    numbers = jax.ShapeDtypeStruct((B, K), jnp.int32)
    held, spare = [vm((divisor(B // 2, 4) * K, 128))] * 2, [vm((divisor(B // 2, 2) * K, 128))] * 2
    mu, vel, rows, table = pl.pallas_call(
        functools.partial(tangent_kernel, CZ, CY),
        out_shape=(sds(padded), sds(padded), numbers, sds((16, 128))),
        in_specs=[HBM] * 6,
        out_specs=(ANY, ANY, ANY, VMEM),
        scratch_shapes=[pltpu.SMEM((B, K), jnp.int32), pltpu.SMEM((B,), jnp.int32)]
        + [pltpu.VMEM((B, K), jnp.int32)] * 2 + [vm(tiles)] * 3 + [pltpu.VMEM((B, S, K), BF16)]
        + [vm(padded)] * 3 + [vm((6,) + core), vm(core)] + [vm(padded)] * 3
        + [vm((CZ * CY * 8, 128))] + held
        + [vm((3, 8, 16, 128)), vm((3, 16, 128))]
        + [DMA((6,)), DMA((4,)), DMA((6, 4)), DMA((6, 4)), DMA((3, 8)), DMA((3, 8))],
        compiler_params=params(56, 0),
        name="tangent",
    )(
        block_cells, block_plane,
        tiled(velocity), tiled(yield_stress), tiled(stress_step), block_weights,
    )

    copies = 8
    adj, obs = pl.pallas_call(
        functools.partial(scatter_kernel, copies),
        out_shape=(sds((CZ * CY * 8, 128)), sds((S, PLANES))),
        in_specs=[SMEM, SMEM, VMEM, VMEM, VMEM],
        out_specs=(VMEM, VMEM),
        scratch_shapes=spare + [vm((CZ * CY * 8, 128))] * copies,
        compiler_params=params(24),
        name="scatter",
    )(rows, block_plane, block_cells, block_weights, table)

    product = pl.pallas_call(
        functools.partial(adjoint_kernel, CZ, CY),
        out_shape=sds(core),
        in_specs=[ANY] * 3,
        out_specs=ANY,
        scratch_shapes=[vm(core), vm(padded), vm(padded), vm((6,) + core), vm(core)]
        + [vm(padded)] * 4 + [vm(core), DMA((3,)), DMA, DMA((4, 4)), DMA((4, 4))],
        compiler_params=params(48, 1),
        name="adjoint",
    )(adj.reshape(core), mu, vel)
    return product.reshape(CZ, CY, NX), obs.T


def solution(mesh):
    placed = (
        P("gz", "xy", None),
        P("gz", "xy", None),
        P("gz", "xy", None),
        P(("gz", "xy"), None, None),
        P(("gz", "xy"), None),
        P(("gz", "xy")),
    )
    return jax.shard_map(
        shards, mesh=mesh, in_specs=placed, out_specs=(P("gz", "xy", None), P()), check_vma=False
    )
```

```python
import functools
import jax
import jax.numpy as jnp
from jax import lax
from jax.experimental import pallas as pl
from jax.experimental.pallas import tpu as pltpu
from jax.sharding import PartitionSpec as P

PLANES = 40
KEEP = 0.2
DAMP = 0.8
MESH = pl.DeviceIdType.MESH
F32 = jnp.float32
BF16 = jnp.bfloat16
VMEM = pl.BlockSpec(memory_space=pltpu.VMEM)
SMEM = pl.BlockSpec(memory_space=pltpu.SMEM)
ANY = pl.BlockSpec(memory_space=pl.ANY)
HBM = pl.BlockSpec(memory_space=pltpu.HBM)
MIB = 1024 * 1024
BATCH = 16


def ids(shape):
    rank = len(shape)
    return (
        lax.broadcasted_iota(jnp.int32, shape, rank - 2),
        lax.broadcasted_iota(jnp.int32, shape, rank - 1),
    )


def x_next(a, wrap=True):
    sub, lane = ids(a.shape)
    r = pltpu.roll(a, 127, a.ndim - 1)
    r = jnp.where(lane == 127, pltpu.roll(r, 7, a.ndim - 2), r)
    return r if wrap else jnp.where((lane == 127) & (sub == 7), 0.0, r)


def x_prev(a, wrap=True):
    sub, lane = ids(a.shape)
    r = pltpu.roll(a, 1, a.ndim - 1)
    r = jnp.where(lane == 0, pltpu.roll(r, 1, a.ndim - 2), r)
    return r if wrap else jnp.where((lane == 0) & (sub == 0), 0.0, r)


def divisor(n, most):
    return max(d for d in range(1, most + 1) if n % d == 0)


class Faces:
    def __init__(self, CZ, CY, send, recv):
        self.CZ, self.CY, self.send, self.recv = CZ, CY, send, recv
        G, X = lax.axis_size("gz"), lax.axis_size("xy")
        g, x = lax.axis_index("gz"), lax.axis_index("xy")
        self.has = (g > 0, g < G - 1, x > 0, x < X - 1)
        lower, upper = jnp.maximum(g - 1, 0), jnp.minimum(g + 1, G - 1)
        left, right = jnp.maximum(x - 1, 0), jnp.minimum(x + 1, X - 1)
        self.to = ((lower, x), (upper, x), (g, left), (g, right))

    def copy(self, buf, e, d):
        CZ, CY = self.CZ, self.CY
        zs, ys = pl.ds(1, CZ), pl.ds(1, CY)
        src = (buf.at[1, ys], buf.at[CZ, ys], buf.at[zs, 1], buf.at[zs, CY])[d]
        dst = (buf.at[CZ + 1, ys], buf.at[0, ys], buf.at[zs, CY + 1], buf.at[zs, 0])[d]
        return pltpu.make_async_remote_copy(
            src_ref=src,
            dst_ref=dst,
            send_sem=self.send.at[e, d],
            recv_sem=self.recv.at[e, d],
            device_id=self.to[d],
            device_id_type=MESH,
        )

    def leave(self, buf, e, d):
        @pl.when(self.has[d])
        def _():
            self.copy(buf, e, d).start()

    def start(self, buf, e):
        for d in range(4):
            self.leave(buf, e, d)

    def arrive(self, buf, e):
        for d in range(4):

            @pl.when(self.has[d ^ 1])
            def _():
                self.copy(buf, e, d).wait_recv()

    def finish(self, buf, e):
        for d in range(4):

            @pl.when(self.has[d])
            def _():
                self.copy(buf, e, d).wait_send()


def lines():
    G, X = lax.axis_size("gz"), lax.axis_size("xy")
    g, x = lax.axis_index("gz"), lax.axis_index("xy")
    across = min(X, 4)
    return (
        (G, g, lambda t: (t, x)),
        (across, x % across, lambda t: (g, (x // across) * across + t)),
        (X // across, x // across, lambda t: (g, t * across + x % across)),
    )


def greet(all_lines):
    G, X = lax.axis_size("gz"), lax.axis_size("xy")
    g, x = lax.axis_index("gz"), lax.axis_index("xy")
    sem = pltpu.get_barrier_semaphore()
    count = jnp.int32(0)
    for has, to in (
        (g > 0, (jnp.maximum(g - 1, 0), x)),
        (g < G - 1, (jnp.minimum(g + 1, G - 1), x)),
        (x > 0, (g, jnp.maximum(x - 1, 0))),
        (x < X - 1, (g, jnp.minimum(x + 1, X - 1))),
    ):
        count = count + has.astype(jnp.int32)

        @pl.when(has)
        def _():
            pl.semaphore_signal(sem, inc=1, device_id=to, device_id_type=MESH)

    if all_lines:
        for n, me, target in lines():
            for d in range(1, n):
                to = target(lax.rem(me + d, n))
                pl.semaphore_signal(sem, inc=1, device_id=to, device_id_type=MESH)
            count = count + (n - 1)
    pl.semaphore_wait(sem, count)


def clear_faces(bufs, CZ, CY):
    plane = jnp.zeros((CY + 2, 8, 128), F32)
    row = jnp.zeros((CZ, 8, 128), F32)
    for buf in bufs:
        buf[0] = plane
        buf[CZ + 1] = plane
        buf[pl.ds(1, CZ), 0] = row
        buf[pl.ds(1, CZ), CY + 1] = row


def interior(CZ, CY, f, planes):
    yn = divisor(CY - 2, 6)
    planes = divisor(CZ - 2, planes)

    @pl.loop(0, (CZ - 2) // planes)
    def _(i):
        for p in range(planes):
            for y in range(1, CY - 1, yn):
                f(1 + i * planes + p, y, 1, yn)


def boundary(CZ, CY, f, leave=None):
    yn, zn = divisor(CY, 8), divisor(CZ - 2, 8)
    for d, z in enumerate((0, CZ - 1)):
        for y in range(0, CY, yn):
            f(z, y, 1, yn)
        if leave:
            leave(d)
    for d, y in enumerate((0, CY - 1)):
        for z in range(1, CZ - 1, zn):
            f(z, y, zn, 1)
        if leave:
            leave(2 + d)


def around(ref, z, y, zn, yn):
    zs, ys = pl.ds(z + 1, zn), pl.ds(y + 1, yn)
    if zn == 1:
        wide = ref[zs, pl.ds(y, yn + 2)]
        return (
            wide[:, 1 : yn + 1],
            wide[:, :yn],
            wide[:, 2:],
            ref[pl.ds(z, 1), ys],
            ref[pl.ds(z + 2, 1), ys],
        )
    wide = ref[pl.ds(z, zn + 2), ys]
    return (
        wide[1 : zn + 1],
        ref[zs, pl.ds(y, yn)],
        ref[zs, pl.ds(y + 2, yn)],
        wide[:zn],
        wide[2:],
    )


def regularized(dz, dy, dx):
    return lax.rsqrt((dz * dz + dy * dy + dx * dx) + 0.01)


def coefficients(MU, z, y, zn, yn):
    m, ym, yp, zm, zp = around(MU, z, y, zn, yn)
    xm, xp = x_prev(m, False), x_next(m, False)
    total = ((xm + xp) + (ym + yp)) + (zm + zp)
    dinv = DAMP / (1.0 + (3.0 * m + 0.5 * total))
    half = 0.5 * dinv
    sub, lane = ids(m.shape)
    first, last = (sub == 0) & (lane == 0), (sub == 7) & (lane == 127)
    faces = (
        jnp.where(first, 0.0, half * (m + xm)),
        jnp.where(last, 0.0, half * (m + xp)),
        half * (m + ym),
        half * (m + yp),
        half * (m + zm),
        half * (m + zp),
    )
    return faces, dinv


def sweep(A, R, src, put, z, y, zn, yn):
    w, ym, yp, zm, zp = around(src, z, y, zn, yn)
    zs, ys = pl.ds(z, zn), pl.ds(y, yn)
    total = KEEP * w + R[zs, ys]
    for at, value in enumerate((x_prev(w), x_next(w), ym, yp, zm, zp)):
        total = total + A[at, zs, ys] * value
    put(total, z, y, zn, yn)


def put_padded(dst):
    def put(value, z, y, zn, yn):
        dst[pl.ds(z + 1, zn), pl.ds(y + 1, yn)] = value

    return put


def put_rows(dst, CY):
    def put(value, z, y, zn, yn):
        for i in range(zn):
            at = pl.multiple_of(((z + i) * CY + y) * 8, 8)
            dst[pl.ds(at, 8 * yn), :] = value[i].reshape(8 * yn, 128)

    return put


def by_row(ref):
    return ref.reshape(ref.shape[0], 1, 128)


def tangent_kernel(
    CZ, CY, c_in, p_in, v_in, y_in, s_in, w_in, mu_out, v_out, table,
    rows_s, plane_s, cells_v, rows_v, vin, yin, sin, weights, V, MU, DMU, A, R, W1, W2, W3, T, rows0, rows1, held, parts,
    load, store, send, recv, sum_send, sum_recv,
):
    tiles = CY // 8
    loads = [
        pltpu.make_async_copy(src, dst, load.at[i])
        for i, (src, dst) in enumerate(
            (
                (v_in, vin), (y_in, yin), (s_in, sin), (w_in, weights),
                (c_in, cells_v), (p_in, plane_s),
            )
        )
    ]
    for c in loads:
        c.start()
    faces = Faces(CZ, CY, send, recv)
    clear_faces((V, MU, DMU, W1, W2, W3), CZ, CY)
    greet(True)
    loads[0].wait()

    @pl.loop(0, CZ * tiles // 2)
    def _(j):
        for i in (2 * j, 2 * j + 1):
            z, y = i // tiles, (i % tiles) * 8
            for s in range(8):
                V[z + 1, y + 1 + s] = vin[i, pl.ds(s, 8, stride=8), :]

    faces.start(V, 0)
    loads[1].wait()
    loads[2].wait()

    def viscosity(z, t):
        i, y = z * tiles + t, t * 8
        here = pl.ds(y + 1, 8)
        c = V[z + 1, here]
        dz = V[z + 2, here] - c
        dy = V[z + 1, pl.ds(y + 2, 8)] - c
        dx = x_next(c, False) - c
        reg = regularized(dz, dy, dx)
        for s in range(8):
            MU[z + 1, y + 1 + s] = 1.0 + yin[i, pl.ds(s, 8, stride=8), :] * reg[s]
            DMU[z + 1, y + 1 + s] = sin[i, pl.ds(s, 8, stride=8), :] * reg[s]

    some = divisor(CZ - 1, 3)

    @pl.loop(0, (CZ - 1) // some)
    def _(i):
        for j in range(some):
            for t in range(tiles - 1):
                viscosity(i * some + j, t)

    faces.arrive(V, 0)
    for t in range(tiles):
        viscosity(CZ - 1, t)

    @pl.loop(0, (CZ - 1) // some)
    def _(i):
        for j in range(some):
            viscosity(i * some + j, tiles - 1)

    faces.start(MU, 1)
    faces.start(DMU, 2)
    loads[4].wait()
    rows_v[...] = cells_v[...] >> 7
    numbers = pltpu.make_async_copy(rows_v, rows_s, store.at[2])
    numbers.start()

    def source(z, y, zn, yn):
        zs, ys = pl.ds(z, zn), pl.ds(y, yn)
        face, dinv = coefficients(MU, z, y, zn, yn)
        for at in range(6):
            A[at, zs, ys] = face[at]
        d, *ds = around(DMU, z, y, zn, yn)
        v, *vs = around(V, z, y, zn, yn)
        ds += [x_prev(d, False), x_next(d, False)]
        vs += [x_prev(v, False), x_next(v, False)]
        total = (d + ds[0]) * (vs[0] - v)
        for dn, vn in zip(ds[1:], vs[1:]):
            total = total + (d + dn) * (vn - v)
        first = (0.5 * dinv) * total
        R[zs, ys] = first
        W1[pl.ds(z + 1, zn), pl.ds(y + 1, yn)] = first

    interior(CZ, CY, source, 2)
    faces.arrive(MU, 1)
    faces.arrive(DMU, 2)
    stores = [
        pltpu.make_async_copy(src, dst, store.at[i])
        for i, (src, dst) in enumerate(((MU, mu_out), (V, v_out)))
    ]
    for c in stores:
        c.start()
    boundary(CZ, CY, source, functools.partial(faces.leave, W1, 3))
    for step, (src, dst) in enumerate(((W1, W2), (W2, W3), (W3, None))):
        put = put_rows(T, CY) if dst is None else put_padded(dst)
        go = functools.partial(sweep, A, R, src, put)
        interior(CZ, CY, go, 2)
        faces.arrive(src, 3 + step)
        boundary(CZ, CY, go, dst is not None and functools.partial(faces.leave, dst, 4 + step))

    loads[3].wait()
    loads[5].wait()
    numbers.wait()
    observe(rows_s, plane_s, cells_v, weights, T, parts, (rows0, rows1))
    sum_all(parts, table, held, sum_send, sum_recv)
    for e, buf in enumerate((V, MU, DMU, W1, W2, W3)):
        faces.finish(buf, e)
    for c in stores:
        c.wait()


def adjoint_kernel(
    CZ, CY, q_in, mu_in, v_in, out,
    Q, MU, V, A, R, W1, W2, W3, W4, T, load, store, send, recv,
):
    loads = [
        pltpu.make_async_copy(src, dst, load.at[i])
        for i, (src, dst) in enumerate(((mu_in, MU), (q_in, Q), (v_in, V)))
    ]
    for c in loads:
        c.start()
    faces = Faces(CZ, CY, send, recv)
    clear_faces((W1, W2, W3, W4), CZ, CY)
    greet(False)
    loads[0].wait()
    loads[1].wait()

    def begin(z, y, zn, yn):
        zs, ys = pl.ds(z, zn), pl.ds(y, yn)
        face, dinv = coefficients(MU, z, y, zn, yn)
        for at in range(6):
            A[at, zs, ys] = face[at]
        first = dinv * Q[zs, ys]
        R[zs, ys] = first
        W1[pl.ds(z + 1, zn), pl.ds(y + 1, yn)] = first

    def product(z, y, zn, yn):
        zs, ys = pl.ds(z, zn), pl.ds(y, yn)
        v, *vs = around(V, z, y, zn, yn)
        a, *many = around(W4, z, y, zn, yn)
        vs += [x_prev(v, False), x_next(v, False)]
        many += [x_prev(a, False), x_next(a, False)]
        total = (v - vs[0]) * (a - many[0])
        for vn, an in zip(vs[1:], many[1:]):
            total = total + (v - vn) * (a - an)
        dy, dz, dx = vs[1] - v, vs[3] - v, vs[5] - v
        T[zs, ys] = (-0.5 * regularized(dz, dy, dx)) * total

    boundary(CZ, CY, begin, functools.partial(faces.leave, W1, 0))
    interior(CZ, CY, begin, 2)
    for step, (src, dst) in enumerate(((W1, W2), (W2, W3), (W3, W4))):
        go = functools.partial(sweep, A, R, src, put_padded(dst))
        interior(CZ, CY, go, 2)
        faces.arrive(src, step)
        boundary(CZ, CY, go, functools.partial(faces.leave, dst, step + 1))
    loads[2].wait()
    interior(CZ, CY, product, 2)
    faces.arrive(W4, 3)
    boundary(CZ, CY, product)
    last = pltpu.make_async_copy(T, out, store)
    last.start()
    for e, buf in enumerate((W1, W2, W3, W4)):
        faces.finish(buf, e)
    last.wait()


def observe(rows_s, plane_s, cells_v, weights, field, parts, rows):
    B, K = rows_s.shape
    group = rows[0].shape[0] // K
    sub, _ = ids((128, K))
    _, lane = ids((8, 128))
    source = by_row(field)

    def fetch(g, held):
        target = by_row(held)
        for j in range(group):
            for k in range(0, K, BATCH):
                got = [source[rows_s[g * group + j, k + i]] for i in range(BATCH)]
                for i in range(BATCH):
                    target[j * K + k + i] = got[i]

    def share(g, held, acc):
        low, high = acc
        for j in range(group):
            b = g * group + j
            inner = by_row(cells_v)[b] & 127
            across = held[j * K : (j + 1) * K, :].T
            cells = jnp.sum(jnp.where(sub == inner, across, 0.0), axis=0, keepdims=True)
            total = jnp.sum(weights[b].astype(F32) * cells, axis=1, keepdims=True)
            p = plane_s[b]
            p = jnp.where(p < PLANES, p, -1000)
            for n in range(3):
                low = low + jnp.where(lane == p + PLANES * n, total[8 * n : 8 * n + 8], 0.0)
            high = high + jnp.where(lane == p, total[24:32], 0.0)
        return low, high

    fetch(0, rows[0])

    def body(i, acc):
        acc = share(2 * i, rows[0], acc)
        fetch(2 * i + 1, rows[1])
        acc = share(2 * i + 1, rows[1], acc)
        fetch(jnp.minimum(2 * i + 2, B // group - 1), rows[0])
        return acc

    zero = jnp.zeros((8, 128), F32)
    low, high = lax.fori_loop(0, B // (2 * group), body, (zero, zero))
    parts[0, 0:8, :] = low
    parts[0, 8:16, :] = high


def sum_all(parts, out, held, send, recv):
    copies = []
    for at, (n, me, target) in enumerate(lines()):
        mine = []
        for d in range(1, n):
            c = pltpu.make_async_remote_copy(
                src_ref=parts.at[at],
                dst_ref=held.at[at, me],
                send_sem=send.at[at, d],
                recv_sem=recv.at[at, d],
                device_id=target(lax.rem(me + d, n)),
                device_id_type=MESH,
            )
            c.start()
            mine.append(c)
        held[at, me] = parts[at]
        for c in mine:
            c.wait_recv()
        total = held[at, 0]
        for i in range(1, n):
            total = total + held[at, i]
        if at < 2:
            parts[at + 1] = total
        else:
            out[...] = total
        copies += mine
    for c in copies:
        c.wait_send()


def scatter_kernel(
    copies, plane_s, cells_v, weights, table, out, obs,
    rows_s, rows_v, values0, values1, sem, *accs,
):
    B, K = rows_s.shape
    rows_v[...] = cells_v[...] >> 7
    numbers = pltpu.make_async_copy(rows_v, rows_s, sem)
    numbers.start()
    group = values0.shape[0] // K
    size = out.shape[0]
    accs3 = [by_row(acc) for acc in accs]

    @pl.loop(0, size // 64)
    def _(i):
        for acc in accs:
            acc[pl.ds(pl.multiple_of(i * 64, 64), 64), :] = jnp.zeros((64, 128), F32)

    sub, _ = ids((128, K))
    _, lane = ids((32, 128))
    packed = table[...]
    low = packed[0:8]
    po = jnp.concatenate(
        [low, pltpu.roll(low, 128 - PLANES, 1), pltpu.roll(low, 128 - 2 * PLANES, 1), packed[8:16]],
        axis=0,
    )
    po = jnp.where(lane < PLANES, po, 0.0)
    obs[...] = po[:, :PLANES]

    def spread(g, values):
        for j in range(group):
            b = g * group + j
            inner = by_row(cells_v)[b] & 127
            mine = jnp.sum(jnp.where(lane == plane_s[b], po, 0.0), axis=1, keepdims=True)
            back = jnp.sum(weights[b].astype(F32) * mine, axis=0, keepdims=True)
            values[j * K : (j + 1) * K, :] = jnp.where(sub == inner, back, 0.0).T

    def add(g, values):
        held = by_row(values)
        for j in range(group):
            for k in range(0, K, copies):
                at = [rows_s[g * group + j, k + i] for i in range(copies)]
                new = [accs3[i][at[i]] + held[j * K + k + i] for i in range(copies)]
                for i in range(copies):
                    accs3[i][at[i]] = new[i]

    spread(0, values0)
    numbers.wait()

    @pl.loop(0, B // (2 * group))
    def _(i):
        spread(2 * i + 1, values1)
        add(2 * i, values0)
        spread(jnp.minimum(2 * i + 2, B // group - 1), values0)
        add(2 * i + 1, values1)

    @pl.loop(0, size // 64)
    def _(i):
        here = pl.ds(pl.multiple_of(i * 64, 64), 64)
        value = accs[0][here, :]
        for acc in accs[1:]:
            value = value + acc[here, :]
        out[here, :] = value


def shards(velocity, yield_stress, stress_step, block_weights, block_cells, block_plane):
    CZ, CY, NX = velocity.shape
    B, S, K = block_weights.shape
    core, padded = (CZ, CY, 8, 128), (CZ + 2, CY + 2, 8, 128)
    tiles = (CZ * CY // 8, 64, 128)

    def tiled(field):
        return field.reshape(CZ, CY // 8, 8, 8, 128).transpose(0, 1, 3, 2, 4).reshape(tiles)

    def sds(shape):
        return jax.ShapeDtypeStruct(shape, F32)

    def vm(shape):
        return pltpu.VMEM(shape, F32)

    def params(limit, n=None):
        if n is None:
            return pltpu.CompilerParams(vmem_limit_bytes=limit * MIB)
        return pltpu.CompilerParams(
            vmem_limit_bytes=limit * MIB, collective_id=n, has_side_effects=True
        )

    DMA = pltpu.SemaphoreType.DMA
    held = [vm((divisor(B // 2, 4) * K, 128))] * 2
    mu, vel, table = pl.pallas_call(
        functools.partial(tangent_kernel, CZ, CY),
        out_shape=(sds(padded), sds(padded), sds((16, 128))),
        in_specs=[HBM] * 6,
        out_specs=(ANY, ANY, VMEM),
        scratch_shapes=[pltpu.SMEM((B, K), jnp.int32), pltpu.SMEM((B,), jnp.int32)]
        + [pltpu.VMEM((B, K), jnp.int32)] * 2 + [vm(tiles)] * 3 + [pltpu.VMEM((B, S, K), BF16)]
        + [vm(padded)] * 3 + [vm((6,) + core), vm(core)] + [vm(padded)] * 3
        + [vm((CZ * CY * 8, 128))] + held
        + [vm((3, 8, 16, 128)), vm((3, 16, 128))]
        + [DMA((6,)), DMA((3,)), DMA((6, 4)), DMA((6, 4)), DMA((3, 8)), DMA((3, 8))],
        compiler_params=params(56, 0),
        name="tangent",
    )(
        block_cells, block_plane,
        tiled(velocity), tiled(yield_stress), tiled(stress_step), block_weights,
    )

    copies = 8
    adj, obs = pl.pallas_call(
        functools.partial(scatter_kernel, copies),
        out_shape=(sds((CZ * CY * 8, 128)), sds((S, PLANES))),
        in_specs=[SMEM, VMEM, VMEM, VMEM],
        out_specs=(VMEM, VMEM),
        scratch_shapes=[pltpu.SMEM((B, K), jnp.int32), pltpu.VMEM((B, K), jnp.int32)]
        + [vm((K, 128))] * 2 + [DMA] + [vm((CZ * CY * 8, 128))] * copies,
        compiler_params=params(24),
        name="scatter",
    )(block_plane, block_cells, block_weights, table)

    product = pl.pallas_call(
        functools.partial(adjoint_kernel, CZ, CY),
        out_shape=sds(core),
        in_specs=[ANY] * 3,
        out_specs=ANY,
        scratch_shapes=[vm(core), vm(padded), vm(padded), vm((6,) + core), vm(core)]
        + [vm(padded)] * 4 + [vm(core), DMA((3,)), DMA, DMA((4, 4)), DMA((4, 4))],
        compiler_params=params(48, 1),
        name="adjoint",
    )(adj.reshape(core), mu, vel)
    return product.reshape(CZ, CY, NX), obs.T


def solution(mesh):
    placed = (
        P("gz", "xy", None),
        P("gz", "xy", None),
        P("gz", "xy", None),
        P(("gz", "xy"), None, None),
        P(("gz", "xy"), None),
        P(("gz", "xy")),
    )
    return jax.shard_map(
        shards, mesh=mesh, in_specs=placed, out_specs=(P("gz", "xy", None), P()), check_vma=False
    )
```

```python
import functools
import jax
import jax.numpy as jnp
from jax import lax
from jax.experimental import pallas as pl
from jax.experimental.pallas import tpu as pltpu
from jax.sharding import PartitionSpec as P

PLANES = 40
KEEP = 0.2
DAMP = 0.8
MESH = pl.DeviceIdType.MESH
F32 = jnp.float32
BF16 = jnp.bfloat16
VMEM = pl.BlockSpec(memory_space=pltpu.VMEM)
SMEM = pl.BlockSpec(memory_space=pltpu.SMEM)
ANY = pl.BlockSpec(memory_space=pl.ANY)
HBM = pl.BlockSpec(memory_space=pltpu.HBM)
MIB = 1024 * 1024
BATCH = 16


def ids(shape):
    rank = len(shape)
    return (
        lax.broadcasted_iota(jnp.int32, shape, rank - 2),
        lax.broadcasted_iota(jnp.int32, shape, rank - 1),
    )


def x_next(a, wrap=True):
    sub, lane = ids(a.shape)
    r = pltpu.roll(a, 127, a.ndim - 1)
    r = jnp.where(lane == 127, pltpu.roll(r, 7, a.ndim - 2), r)
    return r if wrap else jnp.where((lane == 127) & (sub == 7), 0.0, r)


def x_prev(a, wrap=True):
    sub, lane = ids(a.shape)
    r = pltpu.roll(a, 1, a.ndim - 1)
    r = jnp.where(lane == 0, pltpu.roll(r, 1, a.ndim - 2), r)
    return r if wrap else jnp.where((lane == 0) & (sub == 0), 0.0, r)


def divisor(n, most):
    return max(d for d in range(1, most + 1) if n % d == 0)


class Faces:
    def __init__(self, CZ, CY, send, recv):
        self.CZ, self.CY, self.send, self.recv = CZ, CY, send, recv
        G, X = lax.axis_size("gz"), lax.axis_size("xy")
        g, x = lax.axis_index("gz"), lax.axis_index("xy")
        self.has = (g > 0, g < G - 1, x > 0, x < X - 1)
        lower, upper = jnp.maximum(g - 1, 0), jnp.minimum(g + 1, G - 1)
        left, right = jnp.maximum(x - 1, 0), jnp.minimum(x + 1, X - 1)
        self.to = ((lower, x), (upper, x), (g, left), (g, right))

    def copy(self, buf, e, d):
        CZ, CY = self.CZ, self.CY
        zs, ys = pl.ds(1, CZ), pl.ds(1, CY)
        src = (buf.at[1, ys], buf.at[CZ, ys], buf.at[zs, 1], buf.at[zs, CY])[d]
        dst = (buf.at[CZ + 1, ys], buf.at[0, ys], buf.at[zs, CY + 1], buf.at[zs, 0])[d]
        return pltpu.make_async_remote_copy(
            src_ref=src,
            dst_ref=dst,
            send_sem=self.send.at[e, d],
            recv_sem=self.recv.at[e, d],
            device_id=self.to[d],
            device_id_type=MESH,
        )

    def leave(self, buf, e, d):
        @pl.when(self.has[d])
        def _():
            self.copy(buf, e, d).start()

    def start(self, buf, e):
        for d in range(4):
            self.leave(buf, e, d)

    def arrive(self, buf, e):
        for d in range(4):

            @pl.when(self.has[d ^ 1])
            def _():
                self.copy(buf, e, d).wait_recv()

    def finish(self, buf, e):
        for d in range(4):

            @pl.when(self.has[d])
            def _():
                self.copy(buf, e, d).wait_send()


def lines():
    G, X = lax.axis_size("gz"), lax.axis_size("xy")
    g, x = lax.axis_index("gz"), lax.axis_index("xy")
    across = min(X, 4)
    return (
        (G, g, lambda t: (t, x)),
        (across, x % across, lambda t: (g, (x // across) * across + t)),
        (X // across, x // across, lambda t: (g, t * across + x % across)),
    )


def greet(all_lines):
    G, X = lax.axis_size("gz"), lax.axis_size("xy")
    g, x = lax.axis_index("gz"), lax.axis_index("xy")
    sem = pltpu.get_barrier_semaphore()
    count = jnp.int32(0)
    for has, to in (
        (g > 0, (jnp.maximum(g - 1, 0), x)),
        (g < G - 1, (jnp.minimum(g + 1, G - 1), x)),
        (x > 0, (g, jnp.maximum(x - 1, 0))),
        (x < X - 1, (g, jnp.minimum(x + 1, X - 1))),
    ):
        count = count + has.astype(jnp.int32)

        @pl.when(has)
        def _():
            pl.semaphore_signal(sem, inc=1, device_id=to, device_id_type=MESH)

    if all_lines:
        for n, me, target in lines():
            for d in range(1, n):
                to = target(lax.rem(me + d, n))
                pl.semaphore_signal(sem, inc=1, device_id=to, device_id_type=MESH)
            count = count + (n - 1)
    pl.semaphore_wait(sem, count)


def clear_faces(bufs, CZ, CY):
    plane = jnp.zeros((CY + 2, 8, 128), F32)
    row = jnp.zeros((CZ, 8, 128), F32)
    for buf in bufs:
        buf[0] = plane
        buf[CZ + 1] = plane
        buf[pl.ds(1, CZ), 0] = row
        buf[pl.ds(1, CZ), CY + 1] = row


def interior(CZ, CY, f, planes):
    yn = divisor(CY - 2, 6)
    planes = divisor(CZ - 2, planes)

    @pl.loop(0, (CZ - 2) // planes)
    def _(i):
        for p in range(planes):
            for y in range(1, CY - 1, yn):
                f(1 + i * planes + p, y, 1, yn)


def boundary(CZ, CY, f, leave=None):
    yn, zn = divisor(CY, 8), divisor(CZ - 2, 8)
    for d, z in enumerate((0, CZ - 1)):
        for y in range(0, CY, yn):
            f(z, y, 1, yn)
        if leave:
            leave(d)
    for d, y in enumerate((0, CY - 1)):
        for z in range(1, CZ - 1, zn):
            f(z, y, zn, 1)
        if leave:
            leave(2 + d)


def around(ref, z, y, zn, yn):
    zs, ys = pl.ds(z + 1, zn), pl.ds(y + 1, yn)
    if zn == 1:
        wide = ref[zs, pl.ds(y, yn + 2)]
        return (
            wide[:, 1 : yn + 1],
            wide[:, :yn],
            wide[:, 2:],
            ref[pl.ds(z, 1), ys],
            ref[pl.ds(z + 2, 1), ys],
        )
    wide = ref[pl.ds(z, zn + 2), ys]
    return (
        wide[1 : zn + 1],
        ref[zs, pl.ds(y, yn)],
        ref[zs, pl.ds(y + 2, yn)],
        wide[:zn],
        wide[2:],
    )


def regularized(dz, dy, dx):
    return lax.rsqrt((dz * dz + dy * dy + dx * dx) + 0.01)


def coefficients(MU, z, y, zn, yn):
    m, ym, yp, zm, zp = around(MU, z, y, zn, yn)
    xm, xp = x_prev(m, False), x_next(m, False)
    total = ((xm + xp) + (ym + yp)) + (zm + zp)
    dinv = DAMP / (1.0 + (3.0 * m + 0.5 * total))
    half = 0.5 * dinv
    sub, lane = ids(m.shape)
    first, last = (sub == 0) & (lane == 0), (sub == 7) & (lane == 127)
    faces = (
        jnp.where(first, 0.0, half * (m + xm)),
        jnp.where(last, 0.0, half * (m + xp)),
        half * (m + ym),
        half * (m + yp),
        half * (m + zm),
        half * (m + zp),
    )
    return faces, dinv


def sweep(A, R, src, put, z, y, zn, yn):
    w, ym, yp, zm, zp = around(src, z, y, zn, yn)
    zs, ys = pl.ds(z, zn), pl.ds(y, yn)
    total = KEEP * w + R[zs, ys]
    for at, value in enumerate((x_prev(w), x_next(w), ym, yp, zm, zp)):
        total = total + A[at, zs, ys] * value
    put(total, z, y, zn, yn)


def put_padded(dst):
    def put(value, z, y, zn, yn):
        dst[pl.ds(z + 1, zn), pl.ds(y + 1, yn)] = value

    return put


def put_rows(dst, CY):
    def put(value, z, y, zn, yn):
        for i in range(zn):
            at = pl.multiple_of(((z + i) * CY + y) * 8, 8)
            dst[pl.ds(at, 8 * yn), :] = value[i].reshape(8 * yn, 128)

    return put


def by_row(ref):
    return ref.reshape(ref.shape[0], 1, 128)


def tangent_kernel(
    CZ, CY, c_in, p_in, v_in, y_in, s_in, w_in, mu_out, v_out, table,
    rows_s, plane_s, cells_v, rows_v, vin, yin, sin, weights, V, MU, DMU, A, R, W1, W2, W3, T, rows0, rows1, held, parts,
    load, store, send, recv, sum_send, sum_recv,
):
    tiles = CY // 8
    loads = [
        pltpu.make_async_copy(src, dst, load.at[i])
        for i, (src, dst) in enumerate(
            (
                (v_in, vin), (y_in, yin), (s_in, sin), (w_in, weights),
                (c_in, cells_v), (p_in, plane_s),
            )
        )
    ]
    for c in loads:
        c.start()
    faces = Faces(CZ, CY, send, recv)
    clear_faces((V, MU, DMU, W1, W2, W3), CZ, CY)
    greet(True)
    loads[0].wait()

    @pl.loop(0, CZ * tiles // 2)
    def _(j):
        for i in (2 * j, 2 * j + 1):
            z, y = i // tiles, (i % tiles) * 8
            for s in range(8):
                V[z + 1, y + 1 + s] = vin[i, pl.ds(s, 8, stride=8), :]

    faces.start(V, 0)
    loads[1].wait()
    loads[2].wait()

    def viscosity(z, t):
        i, y = z * tiles + t, t * 8
        here = pl.ds(y + 1, 8)
        c = V[z + 1, here]
        dz = V[z + 2, here] - c
        dy = V[z + 1, pl.ds(y + 2, 8)] - c
        dx = x_next(c, False) - c
        reg = regularized(dz, dy, dx)
        for s in range(8):
            MU[z + 1, y + 1 + s] = 1.0 + yin[i, pl.ds(s, 8, stride=8), :] * reg[s]
            DMU[z + 1, y + 1 + s] = sin[i, pl.ds(s, 8, stride=8), :] * reg[s]

    some = divisor(CZ - 1, 3)

    @pl.loop(0, (CZ - 1) // some)
    def _(i):
        for j in range(some):
            for t in range(tiles - 1):
                viscosity(i * some + j, t)

    faces.arrive(V, 0)
    for t in range(tiles):
        viscosity(CZ - 1, t)

    @pl.loop(0, (CZ - 1) // some)
    def _(i):
        for j in range(some):
            viscosity(i * some + j, tiles - 1)

    faces.start(MU, 1)
    faces.start(DMU, 2)
    loads[4].wait()
    rows_v[...] = cells_v[...] >> 7
    numbers = pltpu.make_async_copy(rows_v, rows_s, store.at[2])
    numbers.start()

    def source(z, y, zn, yn):
        zs, ys = pl.ds(z, zn), pl.ds(y, yn)
        face, dinv = coefficients(MU, z, y, zn, yn)
        for at in range(6):
            A[at, zs, ys] = face[at]
        d, *ds = around(DMU, z, y, zn, yn)
        v, *vs = around(V, z, y, zn, yn)
        ds += [x_prev(d, False), x_next(d, False)]
        vs += [x_prev(v, False), x_next(v, False)]
        total = (d + ds[0]) * (vs[0] - v)
        for dn, vn in zip(ds[1:], vs[1:]):
            total = total + (d + dn) * (vn - v)
        first = (0.5 * dinv) * total
        R[zs, ys] = first
        W1[pl.ds(z + 1, zn), pl.ds(y + 1, yn)] = first

    interior(CZ, CY, source, 2)
    faces.arrive(MU, 1)
    faces.arrive(DMU, 2)
    stores = [
        pltpu.make_async_copy(src, dst, store.at[i])
        for i, (src, dst) in enumerate(((MU, mu_out), (V, v_out)))
    ]
    for c in stores:
        c.start()
    boundary(CZ, CY, source, functools.partial(faces.leave, W1, 3))
    for step, (src, dst) in enumerate(((W1, W2), (W2, W3), (W3, None))):
        put = put_rows(T, CY) if dst is None else put_padded(dst)
        go = functools.partial(sweep, A, R, src, put)
        interior(CZ, CY, go, 7)
        faces.arrive(src, 3 + step)
        boundary(CZ, CY, go, dst is not None and functools.partial(faces.leave, dst, 4 + step))

    loads[3].wait()
    loads[5].wait()
    numbers.wait()
    observe(rows_s, plane_s, cells_v, weights, T, parts, (rows0, rows1))
    sum_all(parts, table, held, sum_send, sum_recv)
    for e, buf in enumerate((V, MU, DMU, W1, W2, W3)):
        faces.finish(buf, e)
    for c in stores:
        c.wait()


def adjoint_kernel(
    CZ, CY, q_in, mu_in, v_in, out,
    Q, MU, V, A, R, W1, W2, W3, W4, T, load, store, send, recv,
):
    loads = [
        pltpu.make_async_copy(src, dst, load.at[i])
        for i, (src, dst) in enumerate(((mu_in, MU), (q_in, Q), (v_in, V)))
    ]
    for c in loads:
        c.start()
    faces = Faces(CZ, CY, send, recv)
    clear_faces((W1, W2, W3, W4), CZ, CY)
    greet(False)
    loads[0].wait()
    loads[1].wait()

    def begin(z, y, zn, yn):
        zs, ys = pl.ds(z, zn), pl.ds(y, yn)
        face, dinv = coefficients(MU, z, y, zn, yn)
        for at in range(6):
            A[at, zs, ys] = face[at]
        first = dinv * Q[zs, ys]
        R[zs, ys] = first
        W1[pl.ds(z + 1, zn), pl.ds(y + 1, yn)] = first

    def product(z, y, zn, yn):
        zs, ys = pl.ds(z, zn), pl.ds(y, yn)
        v, *vs = around(V, z, y, zn, yn)
        a, *many = around(W4, z, y, zn, yn)
        vs += [x_prev(v, False), x_next(v, False)]
        many += [x_prev(a, False), x_next(a, False)]
        total = (v - vs[0]) * (a - many[0])
        for vn, an in zip(vs[1:], many[1:]):
            total = total + (v - vn) * (a - an)
        dy, dz, dx = vs[1] - v, vs[3] - v, vs[5] - v
        T[zs, ys] = (-0.5 * regularized(dz, dy, dx)) * total

    boundary(CZ, CY, begin, functools.partial(faces.leave, W1, 0))
    interior(CZ, CY, begin, 2)
    for step, (src, dst) in enumerate(((W1, W2), (W2, W3), (W3, W4))):
        go = functools.partial(sweep, A, R, src, put_padded(dst))
        interior(CZ, CY, go, 7)
        faces.arrive(src, step)
        boundary(CZ, CY, go, functools.partial(faces.leave, dst, step + 1))
    loads[2].wait()
    interior(CZ, CY, product, 2)
    faces.arrive(W4, 3)
    boundary(CZ, CY, product)
    last = pltpu.make_async_copy(T, out, store)
    last.start()
    for e, buf in enumerate((W1, W2, W3, W4)):
        faces.finish(buf, e)
    last.wait()


def observe(rows_s, plane_s, cells_v, weights, field, parts, rows):
    B, K = rows_s.shape
    group = rows[0].shape[0] // K
    sub, _ = ids((128, K))
    _, lane = ids((8, 128))
    source = by_row(field)

    def fetch(g, held):
        target = by_row(held)
        for j in range(group):
            for k in range(0, K, BATCH):
                got = [source[rows_s[g * group + j, k + i]] for i in range(BATCH)]
                for i in range(BATCH):
                    target[j * K + k + i] = got[i]

    def share(g, held, acc):
        low, high = acc
        for j in range(group):
            b = g * group + j
            inner = by_row(cells_v)[b] & 127
            across = held[j * K : (j + 1) * K, :].T
            cells = jnp.sum(jnp.where(sub == inner, across, 0.0), axis=0, keepdims=True)
            total = jnp.sum(weights[b].astype(F32) * cells, axis=1, keepdims=True)
            p = plane_s[b]
            p = jnp.where(p < PLANES, p, -1000)
            for n in range(3):
                low = low + jnp.where(lane == p + PLANES * n, total[8 * n : 8 * n + 8], 0.0)
            high = high + jnp.where(lane == p, total[24:32], 0.0)
        return low, high

    fetch(0, rows[0])

    def body(i, acc):
        acc = share(2 * i, rows[0], acc)
        fetch(2 * i + 1, rows[1])
        acc = share(2 * i + 1, rows[1], acc)
        fetch(jnp.minimum(2 * i + 2, B // group - 1), rows[0])
        return acc

    zero = jnp.zeros((8, 128), F32)
    low, high = lax.fori_loop(0, B // (2 * group), body, (zero, zero))
    parts[0, 0:8, :] = low
    parts[0, 8:16, :] = high


def sum_all(parts, out, held, send, recv):
    copies = []
    for at, (n, me, target) in enumerate(lines()):
        mine = []
        for d in range(1, n):
            c = pltpu.make_async_remote_copy(
                src_ref=parts.at[at],
                dst_ref=held.at[at, me],
                send_sem=send.at[at, d],
                recv_sem=recv.at[at, d],
                device_id=target(lax.rem(me + d, n)),
                device_id_type=MESH,
            )
            c.start()
            mine.append(c)
        held[at, me] = parts[at]
        for c in mine:
            c.wait_recv()
        total = held[at, 0]
        for i in range(1, n):
            total = total + held[at, i]
        if at < 2:
            parts[at + 1] = total
        else:
            out[...] = total
        copies += mine
    for c in copies:
        c.wait_send()


def scatter_kernel(
    copies, plane_s, cells_v, weights, table, out, obs,
    rows_s, rows_v, values0, values1, sem, *accs,
):
    B, K = rows_s.shape
    rows_v[...] = cells_v[...] >> 7
    numbers = pltpu.make_async_copy(rows_v, rows_s, sem)
    numbers.start()
    group = values0.shape[0] // K
    size = out.shape[0]
    accs3 = [by_row(acc) for acc in accs]

    @pl.loop(0, size // 64)
    def _(i):
        for acc in accs:
            acc[pl.ds(pl.multiple_of(i * 64, 64), 64), :] = jnp.zeros((64, 128), F32)

    sub, _ = ids((128, K))
    _, lane = ids((32, 128))
    packed = table[...]
    low = packed[0:8]
    po = jnp.concatenate(
        [low, pltpu.roll(low, 128 - PLANES, 1), pltpu.roll(low, 128 - 2 * PLANES, 1), packed[8:16]],
        axis=0,
    )
    po = jnp.where(lane < PLANES, po, 0.0)
    obs[...] = po[:, :PLANES]

    def spread(g, values):
        for j in range(group):
            b = g * group + j
            inner = by_row(cells_v)[b] & 127
            mine = jnp.sum(jnp.where(lane == plane_s[b], po, 0.0), axis=1, keepdims=True)
            back = jnp.sum(weights[b].astype(F32) * mine, axis=0, keepdims=True)
            values[j * K : (j + 1) * K, :] = jnp.where(sub == inner, back, 0.0).T

    def add(g, values):
        held = by_row(values)
        for j in range(group):
            for k in range(0, K, copies):
                at = [rows_s[g * group + j, k + i] for i in range(copies)]
                new = [accs3[i][at[i]] + held[j * K + k + i] for i in range(copies)]
                for i in range(copies):
                    accs3[i][at[i]] = new[i]

    spread(0, values0)
    numbers.wait()

    @pl.loop(0, B // (2 * group))
    def _(i):
        spread(2 * i + 1, values1)
        add(2 * i, values0)
        spread(jnp.minimum(2 * i + 2, B // group - 1), values0)
        add(2 * i + 1, values1)

    @pl.loop(0, size // 64)
    def _(i):
        here = pl.ds(pl.multiple_of(i * 64, 64), 64)
        value = accs[0][here, :]
        for acc in accs[1:]:
            value = value + acc[here, :]
        out[here, :] = value


def shards(velocity, yield_stress, stress_step, block_weights, block_cells, block_plane):
    CZ, CY, NX = velocity.shape
    B, S, K = block_weights.shape
    core, padded = (CZ, CY, 8, 128), (CZ + 2, CY + 2, 8, 128)
    tiles = (CZ * CY // 8, 64, 128)

    def tiled(field):
        return field.reshape(CZ, CY // 8, 8, 8, 128).transpose(0, 1, 3, 2, 4).reshape(tiles)

    def sds(shape):
        return jax.ShapeDtypeStruct(shape, F32)

    def vm(shape):
        return pltpu.VMEM(shape, F32)

    def params(limit, n=None):
        if n is None:
            return pltpu.CompilerParams(vmem_limit_bytes=limit * MIB)
        return pltpu.CompilerParams(
            vmem_limit_bytes=limit * MIB, collective_id=n, has_side_effects=True
        )

    DMA = pltpu.SemaphoreType.DMA
    held = [vm((divisor(B // 2, 4) * K, 128))] * 2
    mu, vel, table = pl.pallas_call(
        functools.partial(tangent_kernel, CZ, CY),
        out_shape=(sds(padded), sds(padded), sds((16, 128))),
        in_specs=[HBM] * 6,
        out_specs=(ANY, ANY, VMEM),
        scratch_shapes=[pltpu.SMEM((B, K), jnp.int32), pltpu.SMEM((B,), jnp.int32)]
        + [pltpu.VMEM((B, K), jnp.int32)] * 2 + [vm(tiles)] * 3 + [pltpu.VMEM((B, S, K), BF16)]
        + [vm(padded)] * 3 + [vm((6,) + core), vm(core)] + [vm(padded)] * 3
        + [vm((CZ * CY * 8, 128))] + held
        + [vm((3, 8, 16, 128)), vm((3, 16, 128))]
        + [DMA((6,)), DMA((3,)), DMA((6, 4)), DMA((6, 4)), DMA((3, 8)), DMA((3, 8))],
        compiler_params=params(56, 0),
        name="tangent",
    )(
        block_cells, block_plane,
        tiled(velocity), tiled(yield_stress), tiled(stress_step), block_weights,
    )

    copies = 8
    adj, obs = pl.pallas_call(
        functools.partial(scatter_kernel, copies),
        out_shape=(sds((CZ * CY * 8, 128)), sds((S, PLANES))),
        in_specs=[SMEM, VMEM, VMEM, VMEM],
        out_specs=(VMEM, VMEM),
        scratch_shapes=[pltpu.SMEM((B, K), jnp.int32), pltpu.VMEM((B, K), jnp.int32)]
        + [vm((K, 128))] * 2 + [DMA] + [vm((CZ * CY * 8, 128))] * copies,
        compiler_params=params(24),
        name="scatter",
    )(block_plane, block_cells, block_weights, table)

    product = pl.pallas_call(
        functools.partial(adjoint_kernel, CZ, CY),
        out_shape=sds(core),
        in_specs=[ANY] * 3,
        out_specs=ANY,
        scratch_shapes=[vm(core), vm(padded), vm(padded), vm((6,) + core), vm(core)]
        + [vm(padded)] * 4 + [vm(core), DMA((3,)), DMA, DMA((4, 4)), DMA((4, 4))],
        compiler_params=params(48, 1),
        name="adjoint",
    )(adj.reshape(core), mu, vel)
    return product.reshape(CZ, CY, NX), obs.T


def solution(mesh):
    placed = (
        P("gz", "xy", None),
        P("gz", "xy", None),
        P("gz", "xy", None),
        P(("gz", "xy"), None, None),
        P(("gz", "xy"), None),
        P(("gz", "xy")),
    )
    return jax.shard_map(
        shards, mesh=mesh, in_specs=placed, out_specs=(P("gz", "xy", None), P()), check_vma=False
    )
```
